32 devices in a mesh: ulysses: 4 (over y, x), blk: 4 (over z), tensor: 2 (over core).
Axes of the slice: x: 2, y: 2, z: 4, core: 2. Of those that a mesh axis runs over, the one named last changes fastest.
Arguments:
- tokens: bfloat16 [1024, 3072], P(('ulysses', 'blk'), 'tensor'), may hold values from -12 to 12
- cond: bfloat16 [3072], replicated, may hold values from -4 to 4
- mod_weight: bfloat16 [3072, 18432], P(None, ('ulysses', 'blk', 'tensor')), may hold values from -0.109375 to 0.109375
- qkv_weight: bfloat16 [3072, 3, 3072], P('tensor', None, 'ulysses'), as said below
- q_gain: float32 [128], replicated, may hold values from 1.2 to 3.4, as said below
- k_gain: float32 [128], replicated, may hold values from 1.2 to 3.4, as said below
- out_weight: bfloat16 [3072, 3072], P('ulysses', 'tensor'), may hold values from -0.109375 to 0.109375
- up_weight: bfloat16 [3072, 12288], P('tensor', 'ulysses'), may hold values from -0.109375 to 0.109375
- down_weight: bfloat16 [12288, 3072], P('ulysses', 'tensor'), may hold values from -0.0546875 to 0.0546875
Outputs:
- block_out: float32 [1024, 3072], P(('ulysses', 'blk'), 'tensor')
The draws below stay inside these ranges and needn't reach their ends.
Inputs may be any that keep to these rules, and one draw needn't show every extreme that they name: `qkv_weight`: entries lie within four times 3072 ** -0.5 of zero. `q_gain`: positive gains. `k_gain`: positive gains.
All inputs are finite; a program needn't handle non-finite values.
Results may differ from the reference program's by a relative error of at most 0.011.
Values may be sent and summed in bfloat16 or wider, within the bound.
No kernel may reach another device: no remote copies, remote signals or barrier semaphores. Data moves between devices by JAX's collectives and lax.ppermute only.
A program may use at most 128 MiB of HBM per device.

```python
import math
import jax
import jax.numpy as jnp
from jax import lax

D = 3072
HEADS = 24
HEAD = 128
FF = 12288
TOKENS = 1024
N_ULYSSES = 4
N_TENSOR = 2


def draw_tokens(key, part):
    key = jax.random.fold_in(key, 11)
    first, second, third = jax.random.split(key, 3)
    column_pos = jnp.arange(D, dtype=jnp.float32) / D
    column_scale = jnp.power(3.0, column_pos) / math.sqrt(3.0) * jnp.power(10.0, jax.random.uniform(second, (D,), minval=-0.15, maxval=0.15))
    row_scale = jnp.power(10.0, jax.random.uniform(third, (TOKENS, 1), minval=-0.15, maxval=0.15))
    base = jax.random.truncated_normal(first, -2.8, 2.8, (TOKENS, D))
    return (base * row_scale * column_scale).astype(jnp.bfloat16)


def draw_qkv_weight(key, part):
    key = jax.random.fold_in(key, 12)
    weights = jax.random.truncated_normal(key, -4.0, 4.0, (D, 3, HEADS * HEAD)) / math.sqrt(D)
    return weights.astype(jnp.bfloat16)


def draw_q_gain(key, part):
    key = jax.random.fold_in(key, 13)
    gains = jax.random.uniform(key, (HEAD,), minval=1.2, maxval=2.2)
    return gains.astype(jnp.float32)


def draw_k_gain(key, part):
    key = jax.random.fold_in(key, 14)
    gains = jax.random.uniform(key, (HEAD,), minval=1.2, maxval=2.2)
    return gains.astype(jnp.float32)


def block_levels(own_key, dims, cuts, smallest, largest):
    def one(position, parts):
        steps = jax.random.uniform(jax.random.fold_in(jax.random.fold_in(own_key, 6), position), (parts,), jnp.float32, smallest / len(cuts), largest / len(cuts))
        return jnp.repeat(jnp.exp(steps), dims[position] // parts).reshape((-1,) + (1,) * (len(dims) - position - 1))

    level = one(*cuts[0])
    for cut in cuts[1:]:
        level = level * one(*cut)
    return level


def scatter_about(own_key, extent, deviation, most, cuts=(), kind=jnp.bfloat16):
    factor_of = block_levels(own_key, extent, cuts, -0.22, 0.18) if cuts else 1.0
    entries = jax.random.normal(own_key, extent, jnp.float32) * deviation * factor_of
    return jnp.minimum(jnp.maximum(entries, -most), most).astype(kind)


def setup_inputs(seed: int = 0) -> dict:
    key_list = jax.random.split(jax.random.key(seed), 10)
    tokens = draw_tokens(jax.random.fold_in(key_list[9], 71), 0)
    cond = scatter_about(key_list[1], (D,), 1.0, 4.0)
    mod_weight = scatter_about(key_list[2], (D, 6 * D), D ** -0.5, 0.109375, ((1, 32),))
    qkv_weight = draw_qkv_weight(jax.random.fold_in(key_list[9], 71), 0)
    q_gain = draw_q_gain(jax.random.fold_in(key_list[9], 71), 0)
    k_gain = draw_k_gain(jax.random.fold_in(key_list[9], 71), 0)
    out_weight = scatter_about(key_list[6], (HEADS * HEAD, D), (HEADS * HEAD) ** -0.5, 0.109375, ((0, 4), (1, 2)))
    up_weight = scatter_about(key_list[7], (D, FF), D ** -0.5, 0.109375, ((0, 2), (1, 4)))
    down_weight = scatter_about(key_list[8], (FF, D), FF ** -0.5, 0.0546875, ((0, 4), (1, 2)))
    return {"tokens": tokens, "cond": cond, "mod_weight": mod_weight, "qkv_weight": qkv_weight, "q_gain": q_gain, "k_gain": k_gain, "out_weight": out_weight, "up_weight": up_weight, "down_weight": down_weight}


def layer_norm(values):
    center = values - lax.optimization_barrier(jnp.mean(values, axis=-1, keepdims=True))
    variance = lax.optimization_barrier(jnp.mean(center * center, axis=-1, keepdims=True))
    return center * lax.rsqrt(variance + 1e-06)

def head_norm(values, gains):
    return values * lax.rsqrt(lax.optimization_barrier(jnp.mean(values * values, axis=-1, keepdims=True)) + 1e-06) * gains

def rounded(values):
    return lax.optimization_barrier(values.astype(jnp.bfloat16)).astype(jnp.float32)

def grouped_product(left, right, groups):
    width = left.shape[1] // groups
    result = jnp.zeros((left.shape[0], right.shape[1]), jnp.float32)
    for group in range(groups):
        partial_product = jnp.dot(left[:, group * width:(group + 1) * width], right[group * width:(group + 1) * width], preferred_element_type=jnp.float32)
        result = result + rounded(partial_product)
    return result

def reference(tokens, cond, mod_weight, qkv_weight, q_gain, k_gain, out_weight, up_weight, down_weight):
    activated = jax.nn.silu(cond.astype(jnp.float32)).astype(jnp.bfloat16)
    modulation = jnp.dot(activated[None, :], mod_weight, preferred_element_type=jnp.float32)[0].reshape(6, D)
    resid = tokens.astype(jnp.float32)
    normed = (layer_norm(resid) * (1.0 + modulation[1]) + modulation[0]).astype(jnp.bfloat16)
    inner = HEADS * HEAD
    projected = grouped_product(normed, qkv_weight.reshape(D, 3 * inner), N_TENSOR)
    projected = projected.reshape(TOKENS, 3, HEADS, HEAD)
    queries = head_norm(projected[:, 0], q_gain).astype(jnp.bfloat16)
    keys = head_norm(projected[:, 1], k_gain).astype(jnp.bfloat16)
    values = projected[:, 2].astype(jnp.bfloat16)
    score_scale = 1.0 / math.sqrt(HEAD)

    def one_head(operands):
        head_query, head_key, head_value = operands
        scores = jnp.dot(head_query, head_key.T, preferred_element_type=jnp.float32) * score_scale
        weights = jnp.exp(scores - lax.optimization_barrier(jnp.max(scores, axis=-1, keepdims=True)))
        denominator = lax.optimization_barrier(jnp.sum(weights, axis=-1, keepdims=True))
        summed = jnp.dot(weights.astype(jnp.bfloat16), head_value, preferred_element_type=jnp.float32)
        return (summed / denominator).astype(jnp.bfloat16)
    context = lax.map(one_head, (jnp.moveaxis(queries, 1, 0), jnp.moveaxis(keys, 1, 0), jnp.moveaxis(values, 1, 0)))
    context = jnp.moveaxis(context, 0, 1).reshape(TOKENS, inner)
    attended = grouped_product(context, out_weight, N_ULYSSES)
    mixed = resid + modulation[2] * attended
    normed_two = (layer_norm(mixed) * (1.0 + modulation[4]) + modulation[3]).astype(jnp.bfloat16)
    hidden = grouped_product(normed_two, up_weight, N_TENSOR)
    activ = jax.nn.gelu(hidden, approximate=True).astype(jnp.bfloat16)
    feedforward = grouped_product(activ, down_weight, N_ULYSSES)
    return mixed + modulation[5] * feedforward
```

```python
import math

import jax
import jax.numpy as jnp
from jax import lax
from jax.sharding import PartitionSpec as P


def joined(array, axis, combine):
    everything = jax.tree.map(
        lambda part, kind: lax.all_gather(part.astype(kind), axis),
        array,
        jax.tree.map(lambda a: jnp.bfloat16 if a.dtype == jnp.float32 else a.dtype, array),
    )

    def take(k):
        return jax.tree.map(lambda part, own: part[k].astype(own.dtype), everything, array)

    return lax.fori_loop(
        1, lax.axis_size(axis), lambda k, so_far: combine(so_far, take(k)), take(0)
    )


def moments_norm(values, shift_row, scale_row, features):
    sums = lax.psum((jnp.sum(values, axis=-1), jnp.sum(values * values, axis=-1)), "tensor")
    average = sums[0][:, None] / features
    variance = sums[1][:, None] / features - average * average
    normal_rows = (values - average) * lax.rsqrt(variance + 1e-06)
    return (normal_rows * (1.0 + scale_row) + shift_row).astype(jnp.bfloat16)


def spread_rows(values):
    return lax.all_gather(values, "ulysses", axis=0, tiled=True)


def head_norm(values, gains):
    return values * lax.rsqrt(jnp.mean(values * values, axis=-1, keepdims=True) + 1e-06) * gains


def make_absorb(queries, score_scale, running, kv_block):
    keys_part, values_part = kv_block
    top_score, total_weight, summed = running
    scores = (
        jnp.einsum("qhd,khd->qhk", queries, keys_part, preferred_element_type=jnp.float32)
        * score_scale
    )
    new_top = jnp.max(scores, axis=-1)
    decay = jnp.exp(top_score - new_top)
    weights = jnp.exp(scores - new_top[..., None])
    total_weight = total_weight * decay + jnp.sum(weights, axis=-1)
    summed = summed * decay[..., None] + jnp.einsum(
        "qhk,khd->qhd",
        weights.astype(jnp.bfloat16),
        values_part,
        preferred_element_type=jnp.float32,
    )
    return (new_top, total_weight, summed)


def empty_state(row_count, heads_local, head_size):
    return (
        jnp.full((row_count, heads_local), -jnp.inf, jnp.float32),
        jnp.zeros((row_count, heads_local), jnp.float32),
        jnp.zeros((row_count, heads_local, head_size), jnp.float32),
    )


def combine_parts(first_part, second_part):
    top_score = jnp.maximum(first_part[0], second_part[0])
    first_decay = jnp.exp(first_part[0] - top_score)
    second_decay = jnp.exp(second_part[0] - top_score)
    total_weight = first_part[1] * first_decay + second_part[1] * second_decay
    summed = first_part[2] * first_decay[..., None] + second_part[2] * second_decay[..., None]
    return (top_score, total_weight, summed)


def on_device(
    tokens, cond, mod_weight, qkv_weight, q_gain, k_gain, out_weight, up_weight, down_weight
):
    tensor_size = lax.axis_size("tensor")
    tensor_pos = lax.axis_index("tensor")
    width = tokens.shape[1]
    features = width * tensor_size
    activated = jax.nn.silu(cond.astype(jnp.float32)).astype(jnp.bfloat16)
    local_mod = jnp.dot(activated[None, :], mod_weight, preferred_element_type=jnp.float32)[0]
    full_mod = lax.all_gather(local_mod, ("ulysses", "blk", "tensor"), axis=0, tiled=True).reshape(
        6, features
    )
    own_mod = lax.dynamic_slice_in_dim(full_mod, tensor_pos * width, width, 1)
    resid = tokens.astype(jnp.float32)
    normed = moments_norm(resid, own_mod[0], own_mod[1], features)
    gathered = spread_rows(normed)
    group_rows = gathered.shape[0]
    attn_rows = group_rows // tensor_size
    inner_local = qkv_weight.shape[2]
    head_size = q_gain.shape[0]
    heads_local = inner_local // head_size
    flat_qkv = qkv_weight.reshape(width, 3 * inner_local)
    projected = (
        lax.psum_scatter(
            jnp.dot(gathered, flat_qkv, preferred_element_type=jnp.float32).astype(jnp.bfloat16),
            "tensor",
            scatter_dimension=0,
            tiled=True,
        )
        .astype(jnp.float32)
        .reshape(attn_rows, 3, heads_local, head_size)
    )
    queries = head_norm(projected[:, 0], q_gain).astype(jnp.bfloat16)
    keys_local = head_norm(projected[:, 1], k_gain).astype(jnp.bfloat16)
    values_local = projected[:, 2].astype(jnp.bfloat16)
    score_scale = 1.0 / math.sqrt(head_size)
    all_queries = lax.all_gather(queries, "tensor", axis=0, tiled=True)
    state = make_absorb(
        all_queries,
        score_scale,
        empty_state(group_rows, heads_local, head_size),
        (
            lax.all_gather(keys_local, "blk", axis=0, tiled=True),
            lax.all_gather(values_local, "blk", axis=0, tiled=True),
        ),
    )
    merged = joined(state, "tensor", combine_parts)
    context = (
        (merged[2] / merged[1][..., None]).astype(jnp.bfloat16).reshape(group_rows, inner_local)
    )
    attended = lax.psum_scatter(
        jnp.dot(context, out_weight, preferred_element_type=jnp.float32).astype(jnp.bfloat16),
        "ulysses",
        scatter_dimension=0,
        tiled=True,
    ).astype(jnp.float32)
    mixed = resid + own_mod[2] * attended
    normed_two = moments_norm(mixed, own_mod[3], own_mod[4], features)
    gathered_two = spread_rows(normed_two)
    hidden = lax.psum_scatter(
        jnp.dot(gathered_two, up_weight, preferred_element_type=jnp.float32).astype(jnp.bfloat16),
        "tensor",
        scatter_dimension=0,
        tiled=True,
    ).astype(jnp.float32)
    activ = jax.nn.gelu(hidden, approximate=True).astype(jnp.bfloat16)
    activ_rows = lax.all_gather(activ, "tensor", axis=0, tiled=True)
    feedforward = lax.psum_scatter(
        jnp.dot(activ_rows, down_weight, preferred_element_type=jnp.float32).astype(jnp.bfloat16),
        "ulysses",
        scatter_dimension=0,
        tiled=True,
    ).astype(jnp.float32)
    return mixed + own_mod[5] * feedforward


def partners(axis):
    size = lax.axis_size(axis)
    return [[(i, i ^ k) for i in range(size)] for k in range(1, size)]


def from_all(values, axis):
    return [values] + [lax.ppermute(values, axis, pairs) for pairs in partners(axis)]


def to_all(blocks, axis):
    return [blocks[0]] + [
        lax.ppermute(block, axis, pairs) for block, pairs in zip(blocks[1:], partners(axis))
    ]


def swapped(values):
    return lax.ppermute(values, "tensor", [(0, 1), (1, 0)])


def in_order(pieces, axis):
    position = lax.axis_index(axis)
    bit = 1
    while bit < len(pieces):
        flip = (position & bit) != 0
        pieces = [jnp.where(flip, pieces[i ^ bit], pieces[i]) for i in range(len(pieces))]
        bit *= 2
    return jnp.concatenate(pieces, axis=0)


def modulation_rows(cond, mod_weight, features, width):
    activated = jax.nn.silu(cond.astype(jnp.float32)).astype(jnp.bfloat16)
    piece = jnp.dot(activated[None, :], mod_weight, preferred_element_type=jnp.float32)[0]
    for axis in ("tensor", "blk", "ulysses"):
        piece = in_order(from_all(piece, axis), axis)
    rows = piece.reshape(6, features)
    return lax.dynamic_slice_in_dim(rows, lax.axis_index("tensor") * width, width, 1)


def row_sums(values):
    return jnp.stack([jnp.sum(values, axis=-1), jnp.sum(values * values, axis=-1)])


def apply_norm(values, sums, shift_row, scale_row, features):
    average = sums[0][:, None] / features
    variance = sums[1][:, None] / features - average * average
    normal_rows = (values - average) * lax.rsqrt(variance + 1e-06)
    return (normal_rows * (1.0 + scale_row) + shift_row).astype(jnp.bfloat16)


def product(left, right):
    return jnp.dot(left, right, preferred_element_type=jnp.float32).astype(jnp.bfloat16)


def added(blocks):
    total = blocks[0].astype(jnp.float32)
    for block in blocks[1:]:
        total = total + block.astype(jnp.float32)
    return total


def on_pair(
    tokens, cond, mod_weight, qkv_weight, q_gain, k_gain, out_weight, up_weight, down_weight
):
    tensor_pos = lax.axis_index("tensor")
    rows, width = tokens.shape
    features = width * lax.axis_size("tensor")
    head_size = q_gain.shape[0]
    inner_local = qkv_weight.shape[2]
    half = inner_local // 2
    heads = half // head_size

    chunks = [from_all(block, "ulysses") for block in from_all(tokens, "blk")]
    own_mod = modulation_rows(cond, mod_weight, features, width)

    def half_weight(position):
        part = lax.dynamic_slice_in_dim(qkv_weight, position * half, half, 2)
        return part.reshape(width, 3 * half)

    weight_own = half_weight(tensor_pos)
    weight_other = half_weight(1 - tensor_pos)

    queries, keys, values = None, [], []
    for index, blocks in enumerate(chunks):
        chunk = jnp.concatenate(blocks, axis=0).astype(jnp.float32)
        sums = row_sums(chunk)
        sums = sums + swapped(sums)
        normed = apply_norm(chunk, sums, own_mod[0], own_mod[1], features)
        first = 0 if index == 0 else half
        arrived = swapped(product(normed, weight_other[:, first:]))
        projected = added([product(normed, weight_own[:, first:]), arrived])
        projected = projected.reshape(projected.shape[0], -1, heads, head_size)
        if index == 0:
            queries = head_norm(projected[:, 0], q_gain).astype(jnp.bfloat16)
        keys.append(head_norm(projected[:, -2], k_gain).astype(jnp.bfloat16))
        values.append(projected[:, -1].astype(jnp.bfloat16))

    scores = jnp.einsum(
        "qhd,khd->hqk", queries, jnp.concatenate(keys, 0), preferred_element_type=jnp.float32
    ) * (1.0 / math.sqrt(head_size))
    weights = jnp.exp(scores - jnp.max(scores, axis=-1, keepdims=True))
    denominator = jnp.sum(weights, axis=-1)
    summed = jnp.einsum(
        "hqk,khd->qhd",
        weights.astype(jnp.bfloat16),
        jnp.concatenate(values, 0),
        preferred_element_type=jnp.float32,
    )
    context = (summed / denominator.T[..., None]).astype(jnp.bfloat16)
    context = context.reshape(context.shape[0], half)
    context = in_order_columns(context, tensor_pos)

    resid = tokens.astype(jnp.float32)
    attended = reduced_rows(product(context, out_weight), rows)
    mixed = resid + own_mod[2] * attended
    sums = row_sums(mixed)
    sums = sums + swapped(sums)
    normed_two = apply_norm(mixed, sums, own_mod[3], own_mod[4], features)
    gathered_two = jnp.concatenate(from_all(normed_two, "ulysses"), axis=0)
    partial = product(gathered_two, up_weight)
    hidden = added([partial, swapped(partial)])
    activ = jax.nn.gelu(hidden, approximate=True).astype(jnp.bfloat16)
    feedforward = reduced_rows(product(activ, down_weight), rows)
    return mixed + own_mod[5] * feedforward


def in_order_columns(values, tensor_pos):
    other = swapped(values)
    first = jnp.where(tensor_pos == 0, values, other)
    second = jnp.where(tensor_pos == 0, other, values)
    return jnp.concatenate([first, second], axis=1)


def reduced_rows(partial, rows):
    blocks = [partial[i : i + rows] for i in range(0, partial.shape[0], rows)]
    return added(to_all(blocks, "ulysses"))


def solution(mesh):
    sizes = [mesh.shape[axis] for axis in ("ulysses", "blk")]
    pairs = mesh.shape["tensor"] == 2 and all(size & (size - 1) == 0 for size in sizes)
    return jax.shard_map(
        on_pair if pairs else on_device,
        mesh=mesh,
        in_specs=(
            P(("ulysses", "blk"), "tensor"),
            P(),
            P(None, ("ulysses", "blk", "tensor")),
            P("tensor", None, "ulysses"),
            P(),
            P(),
            P("ulysses", "tensor"),
            P("tensor", "ulysses"),
            P("ulysses", "tensor"),
        ),
        out_specs=P(("ulysses", "blk"), "tensor"),
        check_vma=False,
    )
```

```python
import math

import jax
import jax.numpy as jnp
from jax import lax
from jax.experimental import pallas as pl
from jax.experimental.pallas import tpu as pltpu
from jax.sharding import PartitionSpec as P


def joined(array, axis, combine):
    everything = jax.tree.map(
        lambda part, kind: lax.all_gather(part.astype(kind), axis),
        array,
        jax.tree.map(lambda a: jnp.bfloat16 if a.dtype == jnp.float32 else a.dtype, array),
    )

    def take(k):
        return jax.tree.map(lambda part, own: part[k].astype(own.dtype), everything, array)

    return lax.fori_loop(
        1, lax.axis_size(axis), lambda k, so_far: combine(so_far, take(k)), take(0)
    )


def moments_norm(values, shift_row, scale_row, features):
    sums = lax.psum((jnp.sum(values, axis=-1), jnp.sum(values * values, axis=-1)), "tensor")
    average = sums[0][:, None] / features
    variance = sums[1][:, None] / features - average * average
    normal_rows = (values - average) * lax.rsqrt(variance + 1e-06)
    return (normal_rows * (1.0 + scale_row) + shift_row).astype(jnp.bfloat16)


def spread_rows(values):
    return lax.all_gather(values, "ulysses", axis=0, tiled=True)


def head_norm(values, gains):
    return values * lax.rsqrt(jnp.mean(values * values, axis=-1, keepdims=True) + 1e-06) * gains


def make_absorb(queries, score_scale, running, kv_block):
    keys_part, values_part = kv_block
    top_score, total_weight, summed = running
    scores = (
        jnp.einsum("qhd,khd->qhk", queries, keys_part, preferred_element_type=jnp.float32)
        * score_scale
    )
    new_top = jnp.max(scores, axis=-1)
    decay = jnp.exp(top_score - new_top)
    weights = jnp.exp(scores - new_top[..., None])
    total_weight = total_weight * decay + jnp.sum(weights, axis=-1)
    summed = summed * decay[..., None] + jnp.einsum(
        "qhk,khd->qhd",
        weights.astype(jnp.bfloat16),
        values_part,
        preferred_element_type=jnp.float32,
    )
    return (new_top, total_weight, summed)


def empty_state(row_count, heads_local, head_size):
    return (
        jnp.full((row_count, heads_local), -jnp.inf, jnp.float32),
        jnp.zeros((row_count, heads_local), jnp.float32),
        jnp.zeros((row_count, heads_local, head_size), jnp.float32),
    )


def combine_parts(first_part, second_part):
    top_score = jnp.maximum(first_part[0], second_part[0])
    first_decay = jnp.exp(first_part[0] - top_score)
    second_decay = jnp.exp(second_part[0] - top_score)
    total_weight = first_part[1] * first_decay + second_part[1] * second_decay
    summed = first_part[2] * first_decay[..., None] + second_part[2] * second_decay[..., None]
    return (top_score, total_weight, summed)


def on_device(
    tokens, cond, mod_weight, qkv_weight, q_gain, k_gain, out_weight, up_weight, down_weight
):
    tensor_size = lax.axis_size("tensor")
    tensor_pos = lax.axis_index("tensor")
    width = tokens.shape[1]
    features = width * tensor_size
    activated = jax.nn.silu(cond.astype(jnp.float32)).astype(jnp.bfloat16)
    local_mod = jnp.dot(activated[None, :], mod_weight, preferred_element_type=jnp.float32)[0]
    full_mod = lax.all_gather(local_mod, ("ulysses", "blk", "tensor"), axis=0, tiled=True).reshape(
        6, features
    )
    own_mod = lax.dynamic_slice_in_dim(full_mod, tensor_pos * width, width, 1)
    resid = tokens.astype(jnp.float32)
    normed = moments_norm(resid, own_mod[0], own_mod[1], features)
    gathered = spread_rows(normed)
    group_rows = gathered.shape[0]
    attn_rows = group_rows // tensor_size
    inner_local = qkv_weight.shape[2]
    head_size = q_gain.shape[0]
    heads_local = inner_local // head_size
    flat_qkv = qkv_weight.reshape(width, 3 * inner_local)
    projected = (
        lax.psum_scatter(
            jnp.dot(gathered, flat_qkv, preferred_element_type=jnp.float32).astype(jnp.bfloat16),
            "tensor",
            scatter_dimension=0,
            tiled=True,
        )
        .astype(jnp.float32)
        .reshape(attn_rows, 3, heads_local, head_size)
    )
    queries = head_norm(projected[:, 0], q_gain).astype(jnp.bfloat16)
    keys_local = head_norm(projected[:, 1], k_gain).astype(jnp.bfloat16)
    values_local = projected[:, 2].astype(jnp.bfloat16)
    score_scale = 1.0 / math.sqrt(head_size)
    all_queries = lax.all_gather(queries, "tensor", axis=0, tiled=True)
    state = make_absorb(
        all_queries,
        score_scale,
        empty_state(group_rows, heads_local, head_size),
        (
            lax.all_gather(keys_local, "blk", axis=0, tiled=True),
            lax.all_gather(values_local, "blk", axis=0, tiled=True),
        ),
    )
    merged = joined(state, "tensor", combine_parts)
    context = (
        (merged[2] / merged[1][..., None]).astype(jnp.bfloat16).reshape(group_rows, inner_local)
    )
    attended = lax.psum_scatter(
        jnp.dot(context, out_weight, preferred_element_type=jnp.float32).astype(jnp.bfloat16),
        "ulysses",
        scatter_dimension=0,
        tiled=True,
    ).astype(jnp.float32)
    mixed = resid + own_mod[2] * attended
    normed_two = moments_norm(mixed, own_mod[3], own_mod[4], features)
    gathered_two = spread_rows(normed_two)
    hidden = lax.psum_scatter(
        jnp.dot(gathered_two, up_weight, preferred_element_type=jnp.float32).astype(jnp.bfloat16),
        "tensor",
        scatter_dimension=0,
        tiled=True,
    ).astype(jnp.float32)
    activ = jax.nn.gelu(hidden, approximate=True).astype(jnp.bfloat16)
    activ_rows = lax.all_gather(activ, "tensor", axis=0, tiled=True)
    feedforward = lax.psum_scatter(
        jnp.dot(activ_rows, down_weight, preferred_element_type=jnp.float32).astype(jnp.bfloat16),
        "ulysses",
        scatter_dimension=0,
        tiled=True,
    ).astype(jnp.float32)
    return mixed + own_mod[5] * feedforward


VMEM_BYTES = 48 * 1024 * 1024


def permuted(values, axis, distance):
    size = lax.axis_size(axis)
    return lax.ppermute(values, axis, [(i, i ^ distance) for i in range(size)])


def from_all(values, axis):
    return [values] + [permuted(values, axis, k) for k in range(1, lax.axis_size(axis))]


def to_all(blocks, axis):
    return [blocks[0]] + [permuted(blocks[k], axis, k) for k in range(1, len(blocks))]


def doubled(piece, axis):
    position = lax.axis_index(axis)
    distance = 1
    while distance < lax.axis_size(axis):
        other = permuted(piece, axis, distance)
        upper = (position & distance) != 0
        piece = jnp.concatenate(
            [jnp.where(upper, other, piece), jnp.where(upper, piece, other)], axis=0
        )
        distance *= 2
    return piece


def modulation_rows(cond, mod_weight, features, width):
    activated = jax.nn.silu(cond.astype(jnp.float32)).astype(jnp.bfloat16)
    piece = jnp.dot(activated[None, :], mod_weight, preferred_element_type=jnp.float32)[0]
    for axis in ("tensor", "blk", "ulysses"):
        piece = doubled(piece, axis)
    rows = piece.reshape(6, features)
    return lax.dynamic_slice_in_dim(rows, lax.axis_index("tensor") * width, width, 1)


def standardized(values, features):
    sums = jnp.stack([jnp.sum(values, axis=-1), jnp.sum(values * values, axis=-1)])
    sums = sums + permuted(sums, "tensor", 1)
    average = sums[0][:, None] / features
    variance = sums[1][:, None] / features - average * average
    return (values - average) * lax.rsqrt(variance + 1e-06)


def product(left, right):
    return jnp.dot(left, right, preferred_element_type=jnp.float32).astype(jnp.bfloat16)


def added(blocks):
    total = blocks[0].astype(jnp.float32)
    for block in blocks[1:]:
        total = total + block.astype(jnp.float32)
    return total


def project_kernel(pick, *refs):
    *block_refs, shift_ref, scale_ref, weight_ref, out_ref, normed_ref = refs

    @pl.when(pl.program_id(0) == 0)
    def _():
        rows = block_refs[0].shape[0]
        for k, block_ref in enumerate(block_refs):
            values = block_ref[...].astype(jnp.float32)
            values = values * (1.0 + scale_ref[...]) + shift_ref[...]
            normed_ref[k * rows : (k + 1) * rows, :] = values.astype(jnp.bfloat16)

    out_ref[...] = jnp.dot(
        normed_ref[...], weight_ref[0], preferred_element_type=jnp.float32
    ).astype(jnp.bfloat16)


def projected(blocks, shift_row, scale_row, weights, first, half, pick):
    rows, width = blocks[0].shape
    all_rows = rows * len(blocks)
    count = weights.shape[0] - first
    whole = lambda shape: pl.BlockSpec(shape, lambda j, pick: (0, 0))
    return pl.pallas_call(
        project_kernel,
        grid_spec=pltpu.PrefetchScalarGridSpec(
            num_scalar_prefetch=1,
            grid=(count,),
            in_specs=[whole((rows, width)) for _ in blocks]
            + [whole((1, width)), whole((1, width))]
            + [pl.BlockSpec((1, width, half), lambda j, pick: (j + first, 0, pick[0]))],
            out_specs=pl.BlockSpec((all_rows, half), lambda j, pick: (0, j)),
            scratch_shapes=[pltpu.VMEM((all_rows, width), jnp.bfloat16)],
        ),
        out_shape=jax.ShapeDtypeStruct((all_rows, count * half), jnp.bfloat16),
        compiler_params=pltpu.CompilerParams(vmem_limit_bytes=VMEM_BYTES // 2),
        cost_estimate=pl.CostEstimate(
            flops=2 * all_rows * width * count * half,
            bytes_accessed=2 * width * count * half,
            transcendentals=0,
        ),
        name="projected",
    )(pick, *blocks, shift_row, scale_row, weights)


def heads_kernel(count, head_size, own_ref, arrived_ref, q_gain_ref, k_gain_ref, *out_refs):
    half = own_ref.shape[1] // count
    total = lambda lo: (
        own_ref[:, lo : lo + head_size].astype(jnp.float32)
        + arrived_ref[:, lo : lo + head_size].astype(jnp.float32)
    )

    def normal(lo, gain_ref):
        values = total(lo)
        spread = jnp.mean(values * values, axis=-1, keepdims=True) + 1e-06
        return (values * lax.rsqrt(spread) * gain_ref[...]).astype(jnp.bfloat16)

    for lo in range(0, half, head_size):
        if count == 3:
            out_refs[1][:, lo : lo + head_size] = normal(lo, q_gain_ref)
        key_lo = (count - 2) * half + lo
        out_refs[0][:, lo : lo + head_size] = normal(key_lo, k_gain_ref)
        out_refs[0][:, half + lo : half + lo + head_size] = total(key_lo + half).astype(
            jnp.bfloat16
        )


def split_heads(own, arrived, q_gain, k_gain, count):
    rows, columns = own.shape
    half = columns // count
    head_size = q_gain.shape[0]
    shapes = [jax.ShapeDtypeStruct((rows, 2 * half), jnp.bfloat16)]
    if count == 3:
        shapes.append(jax.ShapeDtypeStruct((rows, half), jnp.bfloat16))
    return pl.pallas_call(
        lambda *refs: heads_kernel(count, head_size, *refs),
        out_shape=shapes,
        compiler_params=pltpu.CompilerParams(vmem_limit_bytes=VMEM_BYTES // 4),
        cost_estimate=pl.CostEstimate(
            flops=8 * rows * columns, bytes_accessed=6 * rows * columns, transcendentals=rows * 6
        ),
        name="split_heads",
    )(own, arrived, q_gain[None, :], k_gain[None, :])


def attention_kernel(head_size, query_ref, *refs):
    *kv_refs, out_ref = refs
    half = query_ref.shape[1]
    score_scale = 1.0 / math.sqrt(head_size)
    for lo in range(0, half, head_size):
        query = query_ref[:, lo : lo + head_size]
        scores = [
            lax.dot_general(
                query,
                kv_ref[:, lo : lo + head_size],
                (((1,), (1,)), ((), ())),
                preferred_element_type=jnp.float32,
            )
            * score_scale
            for kv_ref in kv_refs
        ]
        top = jnp.max(scores[0], axis=-1, keepdims=True)
        for part in scores[1:]:
            top = jnp.maximum(top, jnp.max(part, axis=-1, keepdims=True))
        denominator, summed = 0.0, 0.0
        for part, kv_ref in zip(scores, kv_refs):
            weights = jnp.exp(part - top)
            denominator = denominator + jnp.sum(weights, axis=-1, keepdims=True)
            summed = summed + jnp.dot(
                weights.astype(jnp.bfloat16),
                kv_ref[:, half + lo : half + lo + head_size],
                preferred_element_type=jnp.float32,
            )
        out_ref[:, lo : lo + head_size] = (summed / denominator).astype(jnp.bfloat16)


def attention(queries, kv_parts, head_size):
    rows, half = queries.shape
    keys = sum(part.shape[0] for part in kv_parts)
    return pl.pallas_call(
        lambda *refs: attention_kernel(head_size, *refs),
        out_shape=jax.ShapeDtypeStruct((rows, half), jnp.bfloat16),
        compiler_params=pltpu.CompilerParams(vmem_limit_bytes=VMEM_BYTES),
        cost_estimate=pl.CostEstimate(
            flops=4 * rows * keys * half,
            bytes_accessed=4 * keys * half,
            transcendentals=rows * keys * half // head_size,
        ),
        name="attention",
    )(queries, *kv_parts)


def on_pair(
    tokens, cond, mod_weight, qkv_weight, q_gain, k_gain, out_weight, up_weight, down_weight
):
    tensor_pos = lax.axis_index("tensor")
    rows, width = tokens.shape
    features = width * lax.axis_size("tensor")
    head_size = q_gain.shape[0]
    half = qkv_weight.shape[2] // 2
    blocks_z = lax.axis_size("blk")

    resid = tokens.astype(jnp.float32)
    normal = standardized(resid, features).astype(jnp.bfloat16)
    remote = {0: normal}
    for k in range(2, blocks_z):
        remote[k] = permuted(remote[k - 1] if k % 2 else normal, "blk", 1 if k % 2 else k)
    chunks = [from_all(remote[k], "ulysses") for k in sorted(remote)]

    own_mod = modulation_rows(cond, mod_weight, features, width)
    weights = jnp.moveaxis(qkv_weight, 1, 0)
    pick_own = tensor_pos.reshape(1).astype(jnp.int32)
    shift_row, scale_row = own_mod[0:1], own_mod[1:2]

    queries, kv_parts = None, []
    for index, blocks in enumerate(chunks):
        first = 0 if index == 0 else 1
        arrived = permuted(
            projected(blocks, shift_row, scale_row, weights, first, half, 1 - pick_own),
            "tensor",
            1,
        )
        own = projected(blocks, shift_row, scale_row, weights, first, half, pick_own)
        outs = split_heads(own, arrived, q_gain, k_gain, 3 - first)
        kv_parts.append(outs[0])
        if index == 0:
            queries = outs[1]
            if blocks_z > 1:
                kv_parts.append(permuted(outs[0], "blk", 1))

    context = attention(queries, kv_parts, head_size)
    other = permuted(context, "tensor", 1)
    context = jnp.concatenate(
        [
            jnp.where(tensor_pos == 0, context, other),
            jnp.where(tensor_pos == 0, other, context),
        ],
        axis=1,
    )

    attended = reduced_rows(product(context, out_weight), rows)
    mixed = resid + own_mod[2] * attended
    normed_two = standardized(mixed, features) * (1.0 + own_mod[4]) + own_mod[3]
    gathered_two = jnp.concatenate(from_all(normed_two.astype(jnp.bfloat16), "ulysses"), axis=0)
    partial = product(gathered_two, up_weight)
    hidden = added([partial, permuted(partial, "tensor", 1)])
    activ = jax.nn.gelu(hidden, approximate=True).astype(jnp.bfloat16)
    feedforward = reduced_rows(product(activ, down_weight), rows)
    return mixed + own_mod[5] * feedforward


def reduced_rows(partial, rows):
    blocks = [partial[i : i + rows] for i in range(0, partial.shape[0], rows)]
    return added(to_all(blocks, "ulysses"))


def solution(mesh):
    sizes = [mesh.shape[axis] for axis in ("ulysses", "blk")]
    pairs = mesh.shape["tensor"] == 2 and all(size & (size - 1) == 0 for size in sizes)
    return jax.shard_map(
        on_pair if pairs else on_device,
        mesh=mesh,
        in_specs=(
            P(("ulysses", "blk"), "tensor"),
            P(),
            P(None, ("ulysses", "blk", "tensor")),
            P("tensor", None, "ulysses"),
            P(),
            P(),
            P("ulysses", "tensor"),
            P("tensor", "ulysses"),
            P("ulysses", "tensor"),
        ),
        out_specs=P(("ulysses", "blk"), "tensor"),
        check_vma=False,
    )
```

```python
import math

import jax
import jax.numpy as jnp
from jax import lax
from jax.experimental import pallas as pl
from jax.experimental.pallas import tpu as pltpu
from jax.sharding import PartitionSpec as P


def joined(array, axis, combine):
    everything = jax.tree.map(
        lambda part, kind: lax.all_gather(part.astype(kind), axis),
        array,
        jax.tree.map(lambda a: jnp.bfloat16 if a.dtype == jnp.float32 else a.dtype, array),
    )

    def take(k):
        return jax.tree.map(lambda part, own: part[k].astype(own.dtype), everything, array)

    return lax.fori_loop(
        1, lax.axis_size(axis), lambda k, so_far: combine(so_far, take(k)), take(0)
    )


def moments_norm(values, shift_row, scale_row, features):
    sums = lax.psum((jnp.sum(values, axis=-1), jnp.sum(values * values, axis=-1)), "tensor")
    average = sums[0][:, None] / features
    variance = sums[1][:, None] / features - average * average
    normal_rows = (values - average) * lax.rsqrt(variance + 1e-06)
    return (normal_rows * (1.0 + scale_row) + shift_row).astype(jnp.bfloat16)


def spread_rows(values):
    return lax.all_gather(values, "ulysses", axis=0, tiled=True)


def head_norm(values, gains):
    return values * lax.rsqrt(jnp.mean(values * values, axis=-1, keepdims=True) + 1e-06) * gains


def make_absorb(queries, score_scale, running, kv_block):
    keys_part, values_part = kv_block
    top_score, total_weight, summed = running
    scores = (
        jnp.einsum("qhd,khd->qhk", queries, keys_part, preferred_element_type=jnp.float32)
        * score_scale
    )
    new_top = jnp.max(scores, axis=-1)
    decay = jnp.exp(top_score - new_top)
    weights = jnp.exp(scores - new_top[..., None])
    total_weight = total_weight * decay + jnp.sum(weights, axis=-1)
    summed = summed * decay[..., None] + jnp.einsum(
        "qhk,khd->qhd",
        weights.astype(jnp.bfloat16),
        values_part,
        preferred_element_type=jnp.float32,
    )
    return (new_top, total_weight, summed)


def empty_state(row_count, heads_local, head_size):
    return (
        jnp.full((row_count, heads_local), -jnp.inf, jnp.float32),
        jnp.zeros((row_count, heads_local), jnp.float32),
        jnp.zeros((row_count, heads_local, head_size), jnp.float32),
    )


def combine_parts(first_part, second_part):
    top_score = jnp.maximum(first_part[0], second_part[0])
    first_decay = jnp.exp(first_part[0] - top_score)
    second_decay = jnp.exp(second_part[0] - top_score)
    total_weight = first_part[1] * first_decay + second_part[1] * second_decay
    summed = first_part[2] * first_decay[..., None] + second_part[2] * second_decay[..., None]
    return (top_score, total_weight, summed)


def on_device(
    tokens, cond, mod_weight, qkv_weight, q_gain, k_gain, out_weight, up_weight, down_weight
):
    tensor_size = lax.axis_size("tensor")
    tensor_pos = lax.axis_index("tensor")
    width = tokens.shape[1]
    features = width * tensor_size
    activated = jax.nn.silu(cond.astype(jnp.float32)).astype(jnp.bfloat16)
    local_mod = jnp.dot(activated[None, :], mod_weight, preferred_element_type=jnp.float32)[0]
    full_mod = lax.all_gather(local_mod, ("ulysses", "blk", "tensor"), axis=0, tiled=True).reshape(
        6, features
    )
    own_mod = lax.dynamic_slice_in_dim(full_mod, tensor_pos * width, width, 1)
    resid = tokens.astype(jnp.float32)
    normed = moments_norm(resid, own_mod[0], own_mod[1], features)
    gathered = spread_rows(normed)
    group_rows = gathered.shape[0]
    attn_rows = group_rows // tensor_size
    inner_local = qkv_weight.shape[2]
    head_size = q_gain.shape[0]
    heads_local = inner_local // head_size
    flat_qkv = qkv_weight.reshape(width, 3 * inner_local)
    projected = (
        lax.psum_scatter(
            jnp.dot(gathered, flat_qkv, preferred_element_type=jnp.float32).astype(jnp.bfloat16),
            "tensor",
            scatter_dimension=0,
            tiled=True,
        )
        .astype(jnp.float32)
        .reshape(attn_rows, 3, heads_local, head_size)
    )
    queries = head_norm(projected[:, 0], q_gain).astype(jnp.bfloat16)
    keys_local = head_norm(projected[:, 1], k_gain).astype(jnp.bfloat16)
    values_local = projected[:, 2].astype(jnp.bfloat16)
    score_scale = 1.0 / math.sqrt(head_size)
    all_queries = lax.all_gather(queries, "tensor", axis=0, tiled=True)
    state = make_absorb(
        all_queries,
        score_scale,
        empty_state(group_rows, heads_local, head_size),
        (
            lax.all_gather(keys_local, "blk", axis=0, tiled=True),
            lax.all_gather(values_local, "blk", axis=0, tiled=True),
        ),
    )
    merged = joined(state, "tensor", combine_parts)
    context = (
        (merged[2] / merged[1][..., None]).astype(jnp.bfloat16).reshape(group_rows, inner_local)
    )
    attended = lax.psum_scatter(
        jnp.dot(context, out_weight, preferred_element_type=jnp.float32).astype(jnp.bfloat16),
        "ulysses",
        scatter_dimension=0,
        tiled=True,
    ).astype(jnp.float32)
    mixed = resid + own_mod[2] * attended
    normed_two = moments_norm(mixed, own_mod[3], own_mod[4], features)
    gathered_two = spread_rows(normed_two)
    hidden = lax.psum_scatter(
        jnp.dot(gathered_two, up_weight, preferred_element_type=jnp.float32).astype(jnp.bfloat16),
        "tensor",
        scatter_dimension=0,
        tiled=True,
    ).astype(jnp.float32)
    activ = jax.nn.gelu(hidden, approximate=True).astype(jnp.bfloat16)
    activ_rows = lax.all_gather(activ, "tensor", axis=0, tiled=True)
    feedforward = lax.psum_scatter(
        jnp.dot(activ_rows, down_weight, preferred_element_type=jnp.float32).astype(jnp.bfloat16),
        "ulysses",
        scatter_dimension=0,
        tiled=True,
    ).astype(jnp.float32)
    return mixed + own_mod[5] * feedforward


VMEM_BYTES = 1024 * 1024
NO_COST = pl.CostEstimate(flops=0, bytes_accessed=0, transcendentals=0)


def permuted(values, axis, distance):
    size = lax.axis_size(axis)
    return lax.ppermute(values, axis, [(i, i ^ distance) for i in range(size)])


def from_all(values, axis):
    return [values] + [permuted(values, axis, k) for k in range(1, lax.axis_size(axis))]


def to_all(blocks, axis):
    return [blocks[0]] + [permuted(blocks[k], axis, k) for k in range(1, len(blocks))]


def after_specs(after):
    return [pl.BlockSpec((16, 128), lambda j: (0, 0)) for _ in after]


def merge_kernel(axis, distance, own_ref, other_ref, *refs):
    out_ref = refs[-1]
    rows = own_ref.shape[0]
    upper = (lax.axis_index(axis) & distance) != 0
    out_ref[:rows, :] = jnp.where(upper, other_ref[...], own_ref[...])
    out_ref[rows:, :] = jnp.where(upper, own_ref[...], other_ref[...])


def doubled_once(piece, axis, distance, after):
    other = permuted(piece, axis, distance)
    rows, length = piece.shape
    block = pl.BlockSpec((rows, length), lambda j: (0, 0))
    return pl.pallas_call(
        lambda *refs: merge_kernel(axis, distance, *refs),
        grid=(1,),
        in_specs=[block, block] + after_specs(after),
        out_specs=pl.BlockSpec((2 * rows, length), lambda j: (0, 0)),
        out_shape=jax.ShapeDtypeStruct((2 * rows, length), piece.dtype),
        compiler_params=pltpu.CompilerParams(vmem_limit_bytes=VMEM_BYTES),
        cost_estimate=NO_COST,
        name="merged",
    )(piece, other, *after)


def assemble_kernel(pieces_ref, out_ref):
    length = pieces_ref.shape[1]
    width = out_ref.shape[1]
    vectors = out_ref.shape[0]
    halves = pieces_ref.shape[0] * length // (vectors * width)
    for half in range(halves):

        @pl.when(lax.axis_index("tensor") == half)
        def _(half=half):
            for vector in range(vectors):
                at = (vector * halves + half) * width
                end = at + width
                parts = []
                while at < end:
                    row, low = divmod(at, length)
                    high = min(length, low + end - at)
                    parts.append(pieces_ref[row : row + 1, low:high])
                    at += high - low
                out_ref[vector : vector + 1, :] = jnp.concatenate(parts, axis=1)


def assembled(pieces, width):
    return pl.pallas_call(
        assemble_kernel,
        out_shape=jax.ShapeDtypeStruct((6, width), jnp.float32),
        compiler_params=pltpu.CompilerParams(vmem_limit_bytes=VMEM_BYTES),
        cost_estimate=NO_COST,
        name="assembled",
    )(pieces)


def row_sums_kernel(values_ref, out_ref, copy_ref):
    values = values_ref[...].astype(jnp.float32)
    lane = lax.broadcasted_iota(jnp.int32, out_ref.shape, 1)
    out_ref[...] = jnp.where(
        lane < out_ref.shape[1] // 2,
        jnp.sum(values, axis=-1, keepdims=True),
        jnp.sum(values * values, axis=-1, keepdims=True),
    )
    copy_ref[...] = values_ref[...]


def row_sums(values):
    rows = values.shape[0]
    return pl.pallas_call(
        row_sums_kernel,
        out_shape=[
            jax.ShapeDtypeStruct((rows, 128), jnp.float32),
            jax.ShapeDtypeStruct(values.shape, values.dtype),
        ],
        compiler_params=pltpu.CompilerParams(vmem_limit_bytes=VMEM_BYTES * 2),
        cost_estimate=NO_COST,
        name="row_sums",
    )(values)


def centered(values, own, arrived, features):
    total = own + arrived
    average = total[:, :1] / features
    variance = total[:, total.shape[1] // 2 :][:, :1] / features - average * average
    return (values - average) * lax.rsqrt(variance + 1e-06)


def standardize_kernel(features, values_ref, own_ref, arrived_ref, out_ref):
    values = values_ref[...].astype(jnp.float32)
    out_ref[...] = centered(values, own_ref[...], arrived_ref[...], features).astype(jnp.bfloat16)


def standardized(values, features):
    own, values = row_sums(values)
    return pl.pallas_call(
        lambda *refs: standardize_kernel(features, *refs),
        out_shape=jax.ShapeDtypeStruct(values.shape, jnp.bfloat16),
        compiler_params=pltpu.CompilerParams(vmem_limit_bytes=VMEM_BYTES * 2),
        cost_estimate=NO_COST,
        name="standardized",
    )(values, own, permuted(own, "tensor", 1))


def normalized(values, features):
    sums = jnp.stack([jnp.sum(values, axis=-1), jnp.sum(values * values, axis=-1)])
    sums = sums + permuted(sums, "tensor", 1)
    average = sums[0][:, None] / features
    variance = sums[1][:, None] / features - average * average
    return (values - average) * lax.rsqrt(variance + 1e-06)


def product(left, right):
    return jnp.dot(left, right, preferred_element_type=jnp.float32).astype(jnp.bfloat16)


def added(blocks):
    total = blocks[0].astype(jnp.float32)
    for block in blocks[1:]:
        total = total + block.astype(jnp.float32)
    return total


def project_kernel(count, *refs):
    block_refs, (shift_ref, scale_ref, weight_ref) = refs[:count], refs[count : count + 3]
    out_ref, normed_ref = refs[-2:]

    @pl.when(pl.program_id(0) == 0)
    def _():
        rows = block_refs[0].shape[0]
        for k, block_ref in enumerate(block_refs):
            values = block_ref[...].astype(jnp.float32)
            values = values * (1.0 + scale_ref[...]) + shift_ref[...]
            normed_ref[k * rows : (k + 1) * rows, :] = values.astype(jnp.bfloat16)

    out_ref[...] = jnp.dot(
        normed_ref[...], weight_ref[0], preferred_element_type=jnp.float32
    ).astype(jnp.bfloat16)


def projected(blocks, shift_row, scale_row, weights, first, half, other, after=()):
    rows, width = blocks[0].shape
    all_rows = rows * len(blocks)
    count = weights.shape[0] - first

    def columns(j):
        position = lax.axis_index("tensor")
        return (j + first, 0, 1 - position if other else position)

    whole = lambda shape: pl.BlockSpec(shape, lambda j: (0, 0))
    return pl.pallas_call(
        lambda *refs: project_kernel(len(blocks), *refs),
        grid=(count,),
        in_specs=[whole((rows, width)) for _ in blocks]
        + [whole((1, width)), whole((1, width)), pl.BlockSpec((1, width, half), columns)]
        + after_specs(after),
        out_specs=pl.BlockSpec((all_rows, half), lambda j: (0, j)),
        out_shape=jax.ShapeDtypeStruct((all_rows, count * half), jnp.bfloat16),
        scratch_shapes=[pltpu.VMEM((all_rows, width), jnp.bfloat16)],
        compiler_params=pltpu.CompilerParams(vmem_limit_bytes=VMEM_BYTES * 8),
        cost_estimate=NO_COST,
        name="projected",
    )(*blocks, shift_row, scale_row, weights, *after)


def heads_kernel(count, head_size, own_ref, arrived_ref, q_gain_ref, k_gain_ref, *out_refs):
    half = own_ref.shape[1] // count
    total = lambda lo: (
        own_ref[:, lo : lo + head_size].astype(jnp.float32)
        + arrived_ref[:, lo : lo + head_size].astype(jnp.float32)
    )

    def normal(lo, gain_ref):
        values = total(lo)
        spread = jnp.mean(values * values, axis=-1, keepdims=True) + 1e-06
        return (values * lax.rsqrt(spread) * gain_ref[...]).astype(jnp.bfloat16)

    for lo in range(0, half, head_size):
        if count == 3:
            out_refs[1][:, lo : lo + head_size] = normal(lo, q_gain_ref)
        key_lo = (count - 2) * half + lo
        out_refs[0][:, lo : lo + head_size] = normal(key_lo, k_gain_ref)
        out_refs[0][:, half + lo : half + lo + head_size] = total(key_lo + half).astype(
            jnp.bfloat16
        )


def split_heads(own, arrived, q_gain, k_gain, count):
    rows, columns = own.shape
    half = columns // count
    head_size = q_gain.shape[0]
    shapes = [jax.ShapeDtypeStruct((rows, 2 * half), jnp.bfloat16)]
    if count == 3:
        shapes.append(jax.ShapeDtypeStruct((rows, half), jnp.bfloat16))
    return pl.pallas_call(
        lambda *refs: heads_kernel(count, head_size, *refs),
        out_shape=shapes,
        compiler_params=pltpu.CompilerParams(vmem_limit_bytes=VMEM_BYTES * 8),
        cost_estimate=pl.CostEstimate(
            flops=8 * rows * columns, bytes_accessed=6 * rows * columns, transcendentals=rows * 6
        ),
        name="split_heads",
    )(own, arrived, q_gain[None, :], k_gain[None, :])


def attention_kernel(head_size, query_ref, *refs):
    *kv_refs, out_ref = refs
    half = query_ref.shape[1]
    score_scale = 1.0 / math.sqrt(head_size)
    for lo in range(0, half, head_size):
        query = query_ref[:, lo : lo + head_size]
        scores = [
            lax.dot_general(
                query,
                kv_ref[:, lo : lo + head_size],
                (((1,), (1,)), ((), ())),
                preferred_element_type=jnp.float32,
            )
            * score_scale
            for kv_ref in kv_refs
        ]
        top = jnp.max(scores[0], axis=-1, keepdims=True)
        for part in scores[1:]:
            top = jnp.maximum(top, jnp.max(part, axis=-1, keepdims=True))
        denominator, summed = 0.0, 0.0
        for part, kv_ref in zip(scores, kv_refs):
            weights = jnp.exp(part - top)
            denominator = denominator + jnp.sum(weights, axis=-1, keepdims=True)
            summed = summed + jnp.dot(
                weights.astype(jnp.bfloat16),
                kv_ref[:, half + lo : half + lo + head_size],
                preferred_element_type=jnp.float32,
            )
        out_ref[:, lo : lo + head_size] = (summed / denominator).astype(jnp.bfloat16)


def attention(queries, kv_parts, head_size):
    rows, half = queries.shape
    keys = sum(part.shape[0] for part in kv_parts)
    return pl.pallas_call(
        lambda *refs: attention_kernel(head_size, *refs),
        out_shape=jax.ShapeDtypeStruct((rows, half), jnp.bfloat16),
        compiler_params=pltpu.CompilerParams(vmem_limit_bytes=VMEM_BYTES * 12),
        cost_estimate=pl.CostEstimate(
            flops=4 * rows * keys * half,
            bytes_accessed=4 * keys * half,
            transcendentals=rows * keys * half // head_size,
        ),
        name="attention",
    )(queries, *kv_parts)


def row_blocks(values, out_refs):
    rows = out_refs[0].shape[0]
    for k, out_ref in enumerate(out_refs):
        out_ref[...] = values[k * rows : (k + 1) * rows].astype(jnp.bfloat16)


def out_kernel(own_ref, arrived_ref, own_weight_ref, other_weight_ref, *out_refs):
    total = jnp.dot(own_ref[...], own_weight_ref[...], preferred_element_type=jnp.float32)
    total = total + jnp.dot(
        arrived_ref[...], other_weight_ref[...], preferred_element_type=jnp.float32
    )
    row_blocks(total, out_refs)


def out_projected(own, arrived, weight, rows):
    all_rows, half = own.shape
    width = weight.shape[1]
    tile = width // 3 if width % 384 == 0 else width
    whole = pl.BlockSpec((all_rows, half), lambda j: (0, 0))
    return pl.pallas_call(
        out_kernel,
        grid=(width // tile,),
        in_specs=[
            whole,
            whole,
            pl.BlockSpec((half, tile), lambda j: (lax.axis_index("tensor"), j)),
            pl.BlockSpec((half, tile), lambda j: (1 - lax.axis_index("tensor"), j)),
        ],
        out_specs=[pl.BlockSpec((rows, tile), lambda j: (0, j))] * (all_rows // rows),
        out_shape=[jax.ShapeDtypeStruct((rows, width), jnp.bfloat16)] * (all_rows // rows),
        compiler_params=pltpu.CompilerParams(vmem_limit_bytes=VMEM_BYTES * 8),
        cost_estimate=NO_COST,
        name="out_projected",
    )(own, arrived, weight, weight)


def up_kernel(*refs):
    *block_refs, weight_ref, out_ref, joined_ref = refs

    @pl.when(pl.program_id(0) == 0)
    def _():
        rows = block_refs[0].shape[0]
        for k, block_ref in enumerate(block_refs):
            joined_ref[k * rows : (k + 1) * rows, :] = block_ref[...]

    out_ref[...] = jnp.dot(
        joined_ref[...], weight_ref[...], preferred_element_type=jnp.float32
    ).astype(jnp.bfloat16)


def up_projected(blocks, weight, part, parts):
    rows, width = blocks[0].shape
    all_rows = rows * len(blocks)
    columns = weight.shape[1] // parts
    tile = columns // 3 if columns % 384 == 0 else columns
    first = part * columns // tile
    return pl.pallas_call(
        up_kernel,
        grid=(columns // tile,),
        in_specs=[pl.BlockSpec((rows, width), lambda j: (0, 0)) for _ in blocks]
        + [pl.BlockSpec((width, tile), lambda j: (0, j + first))],
        out_specs=pl.BlockSpec((all_rows, tile), lambda j: (0, j)),
        out_shape=jax.ShapeDtypeStruct((all_rows, columns), jnp.bfloat16),
        scratch_shapes=[pltpu.VMEM((all_rows, width), jnp.bfloat16)],
        compiler_params=pltpu.CompilerParams(vmem_limit_bytes=VMEM_BYTES * 8),
        cost_estimate=pl.CostEstimate(
            flops=2 * all_rows * width * columns,
            bytes_accessed=2 * width * columns,
            transcendentals=0,
        ),
        name="up_projected",
    )(*blocks, weight)


def down_kernel(last, own_ref, arrived_ref, weight_ref, *refs):
    step = pl.program_id(0)
    out_refs, total_ref = refs[:-1], refs[-1]
    hidden = own_ref[...].astype(jnp.float32) + arrived_ref[...].astype(jnp.float32)
    activ = jax.nn.gelu(hidden, approximate=True).astype(jnp.bfloat16)
    partial = jnp.dot(activ, weight_ref[...], preferred_element_type=jnp.float32)
    if last:
        before_ref, *out_refs = out_refs
    else:
        total_ref = out_refs[0]

    @pl.when(step == 0)
    def _():
        total_ref[...] = partial + before_ref[...] if last else partial

    @pl.when(step > 0)
    def _():
        total_ref[...] += partial

    if last:

        @pl.when(step == pl.num_programs(0) - 1)
        def _():
            row_blocks(total_ref[...], out_refs)


def down_projected(own, arrived, weight, part, parts, before, rows):
    all_rows, columns = own.shape
    width = weight.shape[1]
    tile = columns // 3 if columns % 384 == 0 else columns
    first = part * columns // tile
    last = before is not None
    whole = pl.BlockSpec((all_rows, width), lambda j: (0, 0))
    if last:
        shapes = [jax.ShapeDtypeStruct((rows, width), jnp.bfloat16)] * (all_rows // rows)
        out_specs = [pl.BlockSpec((rows, width), lambda j: (0, 0))] * (all_rows // rows)
    else:
        shapes = [jax.ShapeDtypeStruct((all_rows, width), jnp.float32)]
        out_specs = [whole]
    scratch = pltpu.VMEM((all_rows, width) if last else (8, 128), jnp.float32)
    return pl.pallas_call(
        lambda *refs: down_kernel(last, *refs),
        grid=(columns // tile,),
        in_specs=[
            pl.BlockSpec((all_rows, tile), lambda j: (0, j)),
            pl.BlockSpec((all_rows, tile), lambda j: (0, j)),
            pl.BlockSpec((tile, width), lambda j: (j + first, 0)),
        ]
        + [whole] * last,
        out_specs=out_specs,
        out_shape=shapes,
        scratch_shapes=[scratch],
        compiler_params=pltpu.CompilerParams(vmem_limit_bytes=VMEM_BYTES * 12),
        cost_estimate=pl.CostEstimate(
            flops=2 * all_rows * width * columns,
            bytes_accessed=2 * width * columns,
            transcendentals=all_rows * columns,
        ),
        name="down_projected",
    )(own, arrived, weight, *([before] * last))


def on_pair(
    tokens, cond, mod_weight, qkv_weight, q_gain, k_gain, out_weight, up_weight, down_weight
):
    stages = [
        (axis, 1 << bit)
        for axis in ("tensor", "blk", "ulysses")
        for bit in range(lax.axis_size(axis).bit_length() - 1)
    ]
    rows, width = tokens.shape
    features = width * lax.axis_size("tensor")
    head_size = q_gain.shape[0]
    half = qkv_weight.shape[2] // 2
    blocks_z = lax.axis_size("blk")

    normal = standardized(tokens, features)
    remote = {0: normal}
    for k in range(2, blocks_z):
        remote[k] = permuted(remote[k - 1] if k % 2 else normal, "blk", 1 if k % 2 else k)
    chunks = [from_all(remote[k], "ulysses") for k in sorted(remote)]

    activated = jax.nn.silu(cond.astype(jnp.float32)).astype(jnp.bfloat16)
    pieces = jnp.dot(activated[None, :], mod_weight, preferred_element_type=jnp.float32)
    after = {("blk", 1): [normal], ("blk", 2): chunks[0][1:3], ("ulysses", 1): chunks[0][3:]}
    after[("ulysses", 2)] = [remote[k] for k in remote if k > 0 and k % 2 == 0]
    for stage in stages:
        pieces = doubled_once(pieces, *stage, after.get(stage, []))
    own_mod = assembled(pieces, width)
    weights = jnp.moveaxis(qkv_weight, 1, 0)
    shift_row, scale_row = own_mod[0:1], own_mod[1:2]

    queries, kv_parts = None, []
    for index, blocks in enumerate(chunks):
        first = 0 if index == 0 else 1
        after = [kv_parts[-1]] if index == 2 else []
        if index == len(chunks) - 1 and index > 0:
            after = after + [kv_parts[1]]
        common = (shift_row, scale_row, weights, first, half)
        arrived = permuted(projected(blocks, *common, True, after), "tensor", 1)
        own = projected(blocks, *common, False)
        outs = split_heads(own, arrived, q_gain, k_gain, 3 - first)
        kv_parts.append(outs[0])
        if index == 0:
            queries = outs[1]
            if blocks_z > 1:
                kv_parts.append(permuted(outs[0], "blk", 1))

    context = attention(queries, kv_parts, head_size)
    partial = out_projected(context, permuted(context, "tensor", 1), out_weight, rows)
    attended = added(to_all(partial, "ulysses"))
    mixed = tokens.astype(jnp.float32) + own_mod[2] * attended
    normed_two = normalized(mixed, features) * (1.0 + own_mod[4]) + own_mod[3]
    blocks = from_all(normed_two.astype(jnp.bfloat16), "ulysses")
    first = up_projected(blocks, up_weight, 0, 2)
    first_arrived = permuted(first, "tensor", 1)
    second = up_projected(blocks, up_weight, 1, 2)
    second_arrived = permuted(second, "tensor", 1)
    before = down_projected(first, first_arrived, down_weight, 0, 2, None, rows)[0]
    partial = down_projected(second, second_arrived, down_weight, 1, 2, before, rows)
    feedforward = added(to_all(partial, "ulysses"))
    return mixed + own_mod[5] * feedforward


def solution(mesh):
    sizes = [mesh.shape[axis] for axis in ("ulysses", "blk")]
    pairs = mesh.shape["tensor"] == 2 and all(size & (size - 1) == 0 for size in sizes)
    return jax.shard_map(
        on_pair if pairs else on_device,
        mesh=mesh,
        in_specs=(
            P(("ulysses", "blk"), "tensor"),
            P(),
            P(None, ("ulysses", "blk", "tensor")),
            P("tensor", None, "ulysses"),
            P(),
            P(),
            P("ulysses", "tensor"),
            P("tensor", "ulysses"),
            P("ulysses", "tensor"),
        ),
        out_specs=P(("ulysses", "blk"), "tensor"),
        check_vma=False,
    )
```

```python
import math

import jax
import jax.numpy as jnp
from jax import lax
from jax.experimental import pallas as pl
from jax.experimental.pallas import tpu as pltpu
from jax.sharding import PartitionSpec as P


def joined(array, axis, combine):
    everything = jax.tree.map(
        lambda part, kind: lax.all_gather(part.astype(kind), axis),
        array,
        jax.tree.map(lambda a: jnp.bfloat16 if a.dtype == jnp.float32 else a.dtype, array),
    )

    def take(k):
        return jax.tree.map(lambda part, own: part[k].astype(own.dtype), everything, array)

    return lax.fori_loop(
        1, lax.axis_size(axis), lambda k, so_far: combine(so_far, take(k)), take(0)
    )


def moments_norm(values, shift_row, scale_row, features):
    sums = lax.psum((jnp.sum(values, axis=-1), jnp.sum(values * values, axis=-1)), "tensor")
    average = sums[0][:, None] / features
    variance = sums[1][:, None] / features - average * average
    normal_rows = (values - average) * lax.rsqrt(variance + 1e-06)
    return (normal_rows * (1.0 + scale_row) + shift_row).astype(jnp.bfloat16)


def spread_rows(values):
    return lax.all_gather(values, "ulysses", axis=0, tiled=True)


def head_norm(values, gains):
    return values * lax.rsqrt(jnp.mean(values * values, axis=-1, keepdims=True) + 1e-06) * gains


def make_absorb(queries, score_scale, running, kv_block):
    keys_part, values_part = kv_block
    top_score, total_weight, summed = running
    scores = (
        jnp.einsum("qhd,khd->qhk", queries, keys_part, preferred_element_type=jnp.float32)
        * score_scale
    )
    new_top = jnp.max(scores, axis=-1)
    decay = jnp.exp(top_score - new_top)
    weights = jnp.exp(scores - new_top[..., None])
    total_weight = total_weight * decay + jnp.sum(weights, axis=-1)
    summed = summed * decay[..., None] + jnp.einsum(
        "qhk,khd->qhd",
        weights.astype(jnp.bfloat16),
        values_part,
        preferred_element_type=jnp.float32,
    )
    return (new_top, total_weight, summed)


def empty_state(row_count, heads_local, head_size):
    return (
        jnp.full((row_count, heads_local), -jnp.inf, jnp.float32),
        jnp.zeros((row_count, heads_local), jnp.float32),
        jnp.zeros((row_count, heads_local, head_size), jnp.float32),
    )


def combine_parts(first_part, second_part):
    top_score = jnp.maximum(first_part[0], second_part[0])
    first_decay = jnp.exp(first_part[0] - top_score)
    second_decay = jnp.exp(second_part[0] - top_score)
    total_weight = first_part[1] * first_decay + second_part[1] * second_decay
    summed = first_part[2] * first_decay[..., None] + second_part[2] * second_decay[..., None]
    return (top_score, total_weight, summed)


def on_device(
    tokens, cond, mod_weight, qkv_weight, q_gain, k_gain, out_weight, up_weight, down_weight
):
    tensor_size = lax.axis_size("tensor")
    tensor_pos = lax.axis_index("tensor")
    width = tokens.shape[1]
    features = width * tensor_size
    activated = jax.nn.silu(cond.astype(jnp.float32)).astype(jnp.bfloat16)
    local_mod = jnp.dot(activated[None, :], mod_weight, preferred_element_type=jnp.float32)[0]
    full_mod = lax.all_gather(local_mod, ("ulysses", "blk", "tensor"), axis=0, tiled=True).reshape(
        6, features
    )
    own_mod = lax.dynamic_slice_in_dim(full_mod, tensor_pos * width, width, 1)
    resid = tokens.astype(jnp.float32)
    normed = moments_norm(resid, own_mod[0], own_mod[1], features)
    gathered = spread_rows(normed)
    group_rows = gathered.shape[0]
    attn_rows = group_rows // tensor_size
    inner_local = qkv_weight.shape[2]
    head_size = q_gain.shape[0]
    heads_local = inner_local // head_size
    flat_qkv = qkv_weight.reshape(width, 3 * inner_local)
    projected = (
        lax.psum_scatter(
            jnp.dot(gathered, flat_qkv, preferred_element_type=jnp.float32).astype(jnp.bfloat16),
            "tensor",
            scatter_dimension=0,
            tiled=True,
        )
        .astype(jnp.float32)
        .reshape(attn_rows, 3, heads_local, head_size)
    )
    queries = head_norm(projected[:, 0], q_gain).astype(jnp.bfloat16)
    keys_local = head_norm(projected[:, 1], k_gain).astype(jnp.bfloat16)
    values_local = projected[:, 2].astype(jnp.bfloat16)
    score_scale = 1.0 / math.sqrt(head_size)
    all_queries = lax.all_gather(queries, "tensor", axis=0, tiled=True)
    state = make_absorb(
        all_queries,
        score_scale,
        empty_state(group_rows, heads_local, head_size),
        (
            lax.all_gather(keys_local, "blk", axis=0, tiled=True),
            lax.all_gather(values_local, "blk", axis=0, tiled=True),
        ),
    )
    merged = joined(state, "tensor", combine_parts)
    context = (
        (merged[2] / merged[1][..., None]).astype(jnp.bfloat16).reshape(group_rows, inner_local)
    )
    attended = lax.psum_scatter(
        jnp.dot(context, out_weight, preferred_element_type=jnp.float32).astype(jnp.bfloat16),
        "ulysses",
        scatter_dimension=0,
        tiled=True,
    ).astype(jnp.float32)
    mixed = resid + own_mod[2] * attended
    normed_two = moments_norm(mixed, own_mod[3], own_mod[4], features)
    gathered_two = spread_rows(normed_two)
    hidden = lax.psum_scatter(
        jnp.dot(gathered_two, up_weight, preferred_element_type=jnp.float32).astype(jnp.bfloat16),
        "tensor",
        scatter_dimension=0,
        tiled=True,
    ).astype(jnp.float32)
    activ = jax.nn.gelu(hidden, approximate=True).astype(jnp.bfloat16)
    activ_rows = lax.all_gather(activ, "tensor", axis=0, tiled=True)
    feedforward = lax.psum_scatter(
        jnp.dot(activ_rows, down_weight, preferred_element_type=jnp.float32).astype(jnp.bfloat16),
        "ulysses",
        scatter_dimension=0,
        tiled=True,
    ).astype(jnp.float32)
    return mixed + own_mod[5] * feedforward


VMEM_BYTES = 1024 * 1024
COPY_AT = 1
LONG = pl.CostEstimate(flops=10**10, bytes_accessed=0, transcendentals=0)
NO_COST = pl.CostEstimate(flops=0, bytes_accessed=0, transcendentals=0)


def permuted(values, axis, distance):
    size = lax.axis_size(axis)
    return lax.ppermute(values, axis, [(i, i ^ distance) for i in range(size)])


def from_all(values, axis):
    return [values] + [permuted(values, axis, k) for k in range(1, lax.axis_size(axis))]


def to_all(blocks, axis):
    return [blocks[0]] + [permuted(blocks[k], axis, k) for k in range(1, len(blocks))]


def after_specs(after):
    shapes = [(1,) * (dep.ndim - 2) + (min(16, dep.shape[-2]), 128) for dep in after]
    return [pl.BlockSpec(shape, lambda j, n=len(shape): (0,) * n) for shape in shapes]


def merge_kernel(axis, distance, own_ref, other_ref, *refs):
    out_ref = refs[-1]
    rows = own_ref.shape[0]
    upper = (lax.axis_index(axis) & distance) != 0
    out_ref[:rows, :] = jnp.where(upper, other_ref[...], own_ref[...])
    out_ref[rows:, :] = jnp.where(upper, own_ref[...], other_ref[...])


def doubled_once(piece, axis, distance, after):
    other = permuted(piece, axis, distance)
    rows, length = piece.shape
    block = pl.BlockSpec((rows, length), lambda j: (0, 0))
    return pl.pallas_call(
        lambda *refs: merge_kernel(axis, distance, *refs),
        grid=(1,),
        in_specs=[block, block] + after_specs(after),
        out_specs=pl.BlockSpec((2 * rows, length), lambda j: (0, 0)),
        out_shape=jax.ShapeDtypeStruct((2 * rows, length), piece.dtype),
        compiler_params=pltpu.CompilerParams(vmem_limit_bytes=VMEM_BYTES),
        cost_estimate=NO_COST,
        name="merged",
    )(piece, other, *after)


def lane_tiles(rows, count, length):
    return -(-(-(-length // 128)) // (rows // count))


def pack_kernel(values_ref, pieces_ref, out_ref):
    rows, width = values_ref.shape
    count, length = pieces_ref.shape
    per = rows // count
    out_ref[:, :width] = values_ref[...]
    for tile in range((out_ref.shape[1] - width) // 128):
        lines = []
        for row in range(count):
            for low in range(tile * per * 128, (tile + 1) * per * 128, 128):
                size = max(0, min(128, length - low))
                line = jnp.zeros((1, 128 - size), jnp.float32)
                if size:
                    part = pieces_ref[row : row + 1, low : low + size]
                    line = jnp.concatenate([part, line], axis=1) if size < 128 else part
                lines.append(line)
        columns = slice(width + tile * 128, width + (tile + 1) * 128)
        out_ref[:, columns] = jnp.concatenate(lines, axis=0).astype(jnp.bfloat16)


def packed(values, pieces):
    rows, width = values.shape
    columns = width + 128 * lane_tiles(rows, *pieces.shape)
    return pl.pallas_call(
        pack_kernel,
        out_shape=jax.ShapeDtypeStruct((rows, columns), jnp.bfloat16),
        compiler_params=pltpu.CompilerParams(vmem_limit_bytes=VMEM_BYTES * 2),
        cost_estimate=NO_COST,
        name="packed",
    )(values, pieces)


def assemble_kernel(axis, count, length, *refs):
    *tile_refs, out_ref, pieces_ref = refs
    position = lax.axis_index(axis)
    tiles = [ref[...].astype(jnp.float32) for ref in tile_refs]
    bit = 1
    while bit < len(tiles):
        flip = (position & bit) != 0
        tiles = [jnp.where(flip, tiles[i ^ bit], tiles[i]) for i in range(len(tiles))]
        bit *= 2
    per = tiles[0].shape[0] // count
    for block, tile in enumerate(tiles):
        for row in range(count):
            for low in range(0, length, 128):
                line = row * per + low // 128 % per
                columns = low // 128 // per * 128
                size = min(128, length - low)
                pieces_ref[block * count + row : block * count + row + 1, low : low + size] = tile[
                    line : line + 1, columns : columns + size
                ]
    width = out_ref.shape[1]
    vectors = out_ref.shape[0]
    halves = len(tiles) * count * length // (vectors * width)
    for half in range(halves):

        @pl.when(lax.axis_index("tensor") == half)
        def _(half=half):
            for vector in range(vectors):
                at = (vector * halves + half) * width
                end = at + width
                parts = []
                while at < end:
                    row, low = divmod(at, length)
                    high = min(length, low + end - at)
                    parts.append(pieces_ref[row : row + 1, low:high])
                    at += high - low
                out_ref[vector : vector + 1, :] = jnp.concatenate(parts, axis=1)


def assembled(blocks, axis, count, length, width):
    rows, columns = blocks[0].shape
    extra = columns - width
    return pl.pallas_call(
        lambda *refs: assemble_kernel(axis, count, length, *refs),
        grid=(1,),
        in_specs=[pl.BlockSpec((rows, extra), lambda j: (0, width // extra)) for _ in blocks],
        out_specs=pl.BlockSpec((6, width), lambda j: (0, 0)),
        out_shape=jax.ShapeDtypeStruct((6, width), jnp.float32),
        scratch_shapes=[pltpu.VMEM((len(blocks) * count, -(-length // 128) * 128), jnp.float32)],
        compiler_params=pltpu.CompilerParams(vmem_limit_bytes=VMEM_BYTES),
        cost_estimate=NO_COST,
        name="assembled",
    )(*blocks)


def row_sums_kernel(count, *refs):
    block_refs, out_ref = refs[:count], refs[-1]
    rows = block_refs[0].shape[0]
    for k, block_ref in enumerate(block_refs):
        values = block_ref[...].astype(jnp.float32)
        lane = lax.broadcasted_iota(jnp.int32, (rows, out_ref.shape[1]), 1)
        out_ref[k * rows : (k + 1) * rows, :] = jnp.where(
            lane < out_ref.shape[1] // 2,
            jnp.sum(values, axis=-1, keepdims=True),
            jnp.sum(values * values, axis=-1, keepdims=True),
        )


def row_sums(blocks, width, after):
    rows = blocks[0].shape[0]
    whole = lambda *shape: pl.BlockSpec(shape, lambda j: (0, 0))
    return pl.pallas_call(
        lambda *refs: row_sums_kernel(len(blocks), *refs),
        grid=(1,),
        in_specs=[whole(rows, width)] * len(blocks) + after_specs(after),
        out_specs=whole(rows * len(blocks), 128),
        out_shape=jax.ShapeDtypeStruct((rows * len(blocks), 128), jnp.float32),
        compiler_params=pltpu.CompilerParams(vmem_limit_bytes=VMEM_BYTES * 4),
        cost_estimate=NO_COST,
        name="row_sums",
    )(*blocks, *after)


def copied_kernel(values_ref, after_ref, out_ref):
    out_ref[...] = values_ref[...]


def copied(values, after, cost):
    whole = pl.BlockSpec(values.shape, lambda j: (0, 0))
    return pl.pallas_call(
        copied_kernel,
        grid=(1,),
        in_specs=[whole] + after_specs([after]),
        out_specs=whole,
        out_shape=jax.ShapeDtypeStruct(values.shape, values.dtype),
        compiler_params=pltpu.CompilerParams(vmem_limit_bytes=VMEM_BYTES * 2),
        cost_estimate=cost,
        name="copied",
    )(values, after)


def centered(values, total, features):
    average = total[:, :1] / features
    variance = total[:, total.shape[1] // 2 :][:, :1] / features - average * average
    return (values - average) * lax.rsqrt(variance + 1e-06)


def normalized(values, features):
    sums = jnp.stack([jnp.sum(values, axis=-1), jnp.sum(values * values, axis=-1)])
    sums = sums + permuted(sums, "tensor", 1)
    average = sums[0][:, None] / features
    variance = sums[1][:, None] / features - average * average
    return (values - average) * lax.rsqrt(variance + 1e-06)


def product(left, right):
    return jnp.dot(left, right, preferred_element_type=jnp.float32).astype(jnp.bfloat16)


def added(blocks):
    total = blocks[0].astype(jnp.float32)
    for block in blocks[1:]:
        total = total + block.astype(jnp.float32)
    return total


def project_kernel(count, features, parts, *refs):
    block_refs = refs[:count]
    own_ref, arrived_ref, shift_ref, scale_ref, weight_ref = refs[count : count + 5]
    normed_ref = refs[-1]

    @pl.when(pl.program_id(0) == 0)
    def _():
        rows = block_refs[0].shape[0]
        for k, block_ref in enumerate(block_refs):
            here = slice(k * rows, (k + 1) * rows)
            total = own_ref[here, :] + arrived_ref[here, :]
            values = centered(block_ref[...].astype(jnp.float32), total, features)
            values = values * (1.0 + scale_ref[...]) + shift_ref[...]
            normed_ref[here, :] = values.astype(jnp.bfloat16)

    project_part(normed_ref, weight_ref, refs[-1 - parts : -1])


def project_part(normed_ref, weight_ref, out_refs):
    product = jnp.dot(normed_ref[...], weight_ref[0], preferred_element_type=jnp.float32)
    for k, out_ref in enumerate(out_refs):

        @pl.when(pl.program_id(0) == k)
        def _(out_ref=out_ref):
            out_ref[...] = product.astype(jnp.bfloat16)


def project_again_kernel(parts, normed_ref, weight_ref, *refs):
    project_part(normed_ref, weight_ref, refs[-parts:])


def projected(blocks, small, weights, first, half, other, after=()):
    rows, width = blocks[0].shape[0], weights.shape[1]
    all_rows = rows * len(blocks)
    count = weights.shape[0] - first

    def columns(j):
        position = lax.axis_index("tensor")
        return (j + first, 0, 1 - position if other else position)

    whole = lambda shape: pl.BlockSpec(shape, lambda j: (0, 0))
    shapes = [(all_rows, half)] * count + [(all_rows, width)] * bool(small)
    return pl.pallas_call(
        (lambda *refs: project_kernel(len(blocks), 2 * width, count, *refs))
        if small
        else (lambda *refs: project_again_kernel(count, *refs)),
        grid=(count,),
        in_specs=[whole((rows, width)) for _ in blocks]
        + [whole(array.shape) for array in small]
        + [pl.BlockSpec((1, width, half), columns)]
        + after_specs(after),
        out_specs=[whole(shape) for shape in shapes],
        out_shape=[jax.ShapeDtypeStruct(shape, jnp.bfloat16) for shape in shapes],
        compiler_params=pltpu.CompilerParams(vmem_limit_bytes=VMEM_BYTES * 9),
        cost_estimate=NO_COST,
        name="projected",
    )(*blocks, *small, weights, *after)


def staged(weights, after):
    block = pl.BlockSpec(memory_space=pl.ANY)
    count, width, columns = weights.shape

    def kernel(weight_ref, after_ref, out_ref, sem):
        copy = pltpu.make_async_copy(weight_ref, out_ref, sem)
        copy.start()
        copy.wait()

    return pl.pallas_call(
        kernel,
        in_specs=[block, pl.BlockSpec(memory_space=pltpu.VMEM)],
        out_specs=pl.BlockSpec(memory_space=pltpu.VMEM),
        out_shape=pltpu.VMEM(weights.shape, weights.dtype),
        scratch_shapes=[pltpu.SemaphoreType.DMA],
        compiler_params=pltpu.CompilerParams(vmem_limit_bytes=VMEM_BYTES * 9),
        cost_estimate=pl.CostEstimate(
            flops=0, bytes_accessed=2 * weights.size, transcendentals=0
        ),
        name="staged",
    )(weights, after)


def heads_kernel(count, head_size, *refs):
    own_refs, arrived_refs = refs[:count], refs[count : 2 * count]
    q_gain_ref, k_gain_ref = refs[2 * count : 2 * count + 2]
    out_refs = refs[-1:] if count == 2 else refs[-2:]
    half = own_refs[0].shape[1]

    def total(part, here):
        return own_refs[part][:, here].astype(jnp.float32) + arrived_refs[part][:, here].astype(
            jnp.float32
        )

    def normal(values, gain_ref):
        spread = jnp.mean(values * values, axis=-1, keepdims=True) + 1e-06
        return (values * lax.rsqrt(spread) * gain_ref[...]).astype(jnp.bfloat16)

    for low in range(0, half, head_size):
        here = slice(low, low + head_size)
        if count == 3:
            out_refs[1][:, here] = normal(total(0, here), q_gain_ref)
        out_refs[0][:, here] = normal(total(count - 2, here), k_gain_ref)
        out_refs[0][:, half + low : half + low + head_size] = total(count - 1, here).astype(
            jnp.bfloat16
        )


def split_heads(own, arrived, q_gain, k_gain, after=()):
    count = len(own)
    rows, half = own[0].shape
    head_size = q_gain.shape[0]
    widths = [2 * half] if count == 2 else [2 * half, half]
    whole = lambda *shape: pl.BlockSpec(shape, lambda j: (0, 0))
    return pl.pallas_call(
        lambda *refs: heads_kernel(count, head_size, *refs),
        grid=(1,),
        in_specs=[whole(rows, half)] * (2 * count)
        + [whole(1, head_size)] * 2
        + after_specs(after),
        out_specs=[whole(rows, width) for width in widths],
        out_shape=[jax.ShapeDtypeStruct((rows, width), jnp.bfloat16) for width in widths],
        compiler_params=pltpu.CompilerParams(vmem_limit_bytes=VMEM_BYTES * 5),
        cost_estimate=NO_COST,
        name="split_heads",
    )(*own, *arrived, q_gain[None, :], k_gain[None, :], *after)


def attention_kernel(head_size, query_ref, *refs):
    *kv_refs, out_ref = refs
    half = query_ref.shape[1]
    score_scale = 1.0 / math.sqrt(head_size)
    for lo in range(0, half, head_size):
        query = query_ref[:, lo : lo + head_size]
        scores = [
            lax.dot_general(
                query,
                kv_ref[:, lo : lo + head_size],
                (((1,), (1,)), ((), ())),
                preferred_element_type=jnp.float32,
            )
            * score_scale
            for kv_ref in kv_refs
        ]
        top = jnp.max(scores[0], axis=-1, keepdims=True)
        for part in scores[1:]:
            top = jnp.maximum(top, jnp.max(part, axis=-1, keepdims=True))
        denominator, summed = 0.0, 0.0
        for part, kv_ref in zip(scores, kv_refs):
            weights = jnp.exp(part - top)
            denominator = denominator + jnp.sum(weights, axis=-1, keepdims=True)
            summed = summed + jnp.dot(
                weights.astype(jnp.bfloat16),
                kv_ref[:, half + lo : half + lo + head_size],
                preferred_element_type=jnp.float32,
            )
        out_ref[:, lo : lo + head_size] = (summed / denominator).astype(jnp.bfloat16)


def attention(queries, kv_parts, head_size):
    rows, half = queries.shape
    keys = sum(part.shape[0] for part in kv_parts)
    return pl.pallas_call(
        lambda *refs: attention_kernel(head_size, *refs),
        out_shape=jax.ShapeDtypeStruct((rows, half), jnp.bfloat16),
        compiler_params=pltpu.CompilerParams(vmem_limit_bytes=VMEM_BYTES * 12),
        cost_estimate=pl.CostEstimate(
            flops=4 * rows * keys * half,
            bytes_accessed=4 * keys * half,
            transcendentals=rows * keys * half // head_size,
        ),
        name="attention",
    )(queries, *kv_parts)


def row_blocks(values, out_refs):
    rows = out_refs[0].shape[0]
    for k, out_ref in enumerate(out_refs):
        out_ref[...] = values[k * rows : (k + 1) * rows].astype(jnp.bfloat16)


def out_kernel(own_ref, arrived_ref, own_weight_ref, other_weight_ref, *out_refs):
    total = jnp.dot(own_ref[...], own_weight_ref[...], preferred_element_type=jnp.float32)
    total = total + jnp.dot(
        arrived_ref[...], other_weight_ref[...], preferred_element_type=jnp.float32
    )
    row_blocks(total, out_refs)


def out_projected(own, arrived, weight, rows):
    all_rows, half = own.shape
    width = weight.shape[1]
    tile = width // 3 if width % 384 == 0 else width
    whole = pl.BlockSpec((all_rows, half), lambda j: (0, 0))
    return pl.pallas_call(
        out_kernel,
        grid=(width // tile,),
        in_specs=[
            whole,
            whole,
            pl.BlockSpec((half, tile), lambda j: (lax.axis_index("tensor"), j)),
            pl.BlockSpec((half, tile), lambda j: (1 - lax.axis_index("tensor"), j)),
        ],
        out_specs=[pl.BlockSpec((rows, tile), lambda j: (0, j))] * (all_rows // rows),
        out_shape=[jax.ShapeDtypeStruct((rows, width), jnp.bfloat16)] * (all_rows // rows),
        compiler_params=pltpu.CompilerParams(vmem_limit_bytes=VMEM_BYTES * 8),
        cost_estimate=NO_COST,
        name="out_projected",
    )(own, arrived, weight, weight)


def up_kernel(*refs):
    *block_refs, weight_ref, out_ref, joined_ref = refs

    @pl.when(pl.program_id(0) == 0)
    def _():
        rows = block_refs[0].shape[0]
        for k, block_ref in enumerate(block_refs):
            joined_ref[k * rows : (k + 1) * rows, :] = block_ref[...]

    out_ref[...] = jnp.dot(
        joined_ref[...], weight_ref[...], preferred_element_type=jnp.float32
    ).astype(jnp.bfloat16)


def up_projected(blocks, weight, part, parts):
    rows, width = blocks[0].shape
    all_rows = rows * len(blocks)
    columns = weight.shape[1] // parts
    tile = columns // 3 if columns % 384 == 0 else columns
    first = part * columns // tile
    return pl.pallas_call(
        up_kernel,
        grid=(columns // tile,),
        in_specs=[pl.BlockSpec((rows, width), lambda j: (0, 0)) for _ in blocks]
        + [pl.BlockSpec((width, tile), lambda j: (0, j + first))],
        out_specs=pl.BlockSpec((all_rows, tile), lambda j: (0, j)),
        out_shape=jax.ShapeDtypeStruct((all_rows, columns), jnp.bfloat16),
        scratch_shapes=[pltpu.VMEM((all_rows, width), jnp.bfloat16)],
        compiler_params=pltpu.CompilerParams(vmem_limit_bytes=VMEM_BYTES * 8),
        cost_estimate=pl.CostEstimate(
            flops=2 * all_rows * width * columns,
            bytes_accessed=2 * width * columns,
            transcendentals=0,
        ),
        name="up_projected",
    )(*blocks, weight)


def down_kernel(last, own_ref, arrived_ref, weight_ref, *refs):
    step = pl.program_id(0)
    out_refs, total_ref = refs[:-1], refs[-1]
    hidden = own_ref[...].astype(jnp.float32) + arrived_ref[...].astype(jnp.float32)
    activ = jax.nn.gelu(hidden, approximate=True).astype(jnp.bfloat16)
    partial = jnp.dot(activ, weight_ref[...], preferred_element_type=jnp.float32)
    if last:
        before_ref, *out_refs = out_refs
    else:
        total_ref = out_refs[0]

    @pl.when(step == 0)
    def _():
        total_ref[...] = partial + before_ref[...] if last else partial

    @pl.when(step > 0)
    def _():
        total_ref[...] += partial

    if last:

        @pl.when(step == pl.num_programs(0) - 1)
        def _():
            row_blocks(total_ref[...], out_refs)


def down_projected(own, arrived, weight, part, parts, before, rows):
    all_rows, columns = own.shape
    width = weight.shape[1]
    tile = columns // 3 if columns % 384 == 0 else columns
    first = part * columns // tile
    last = before is not None
    whole = pl.BlockSpec((all_rows, width), lambda j: (0, 0))
    if last:
        shapes = [jax.ShapeDtypeStruct((rows, width), jnp.bfloat16)] * (all_rows // rows)
        out_specs = [pl.BlockSpec((rows, width), lambda j: (0, 0))] * (all_rows // rows)
    else:
        shapes = [jax.ShapeDtypeStruct((all_rows, width), jnp.float32)]
        out_specs = [whole]
    scratch = pltpu.VMEM((all_rows, width) if last else (8, 128), jnp.float32)
    return pl.pallas_call(
        lambda *refs: down_kernel(last, *refs),
        grid=(columns // tile,),
        in_specs=[
            pl.BlockSpec((all_rows, tile), lambda j: (0, j)),
            pl.BlockSpec((all_rows, tile), lambda j: (0, j)),
            pl.BlockSpec((tile, width), lambda j: (j + first, 0)),
        ]
        + [whole] * last,
        out_specs=out_specs,
        out_shape=shapes,
        scratch_shapes=[scratch],
        compiler_params=pltpu.CompilerParams(vmem_limit_bytes=VMEM_BYTES * 12),
        cost_estimate=pl.CostEstimate(
            flops=2 * all_rows * width * columns,
            bytes_accessed=2 * width * columns,
            transcendentals=all_rows * columns,
        ),
        name="down_projected",
    )(own, arrived, weight, *([before] * last))


def on_pair(
    tokens, cond, mod_weight, qkv_weight, q_gain, k_gain, out_weight, up_weight, down_weight
):
    stages = [
        (axis, 1 << bit)
        for axis in ("tensor", "blk")
        for bit in range(lax.axis_size(axis).bit_length() - 1)
    ]
    rows, width = tokens.shape
    features = width * lax.axis_size("tensor")
    head_size = q_gain.shape[0]
    half = qkv_weight.shape[2] // 2
    blocks_z = lax.axis_size("blk")

    activated = jax.nn.silu(cond.astype(jnp.float32)).astype(jnp.bfloat16)
    pieces = jnp.dot(activated[None, :], mod_weight, preferred_element_type=jnp.float32)
    weights = jnp.moveaxis(qkv_weight, 1, 0)
    start = copied(tokens, pieces, NO_COST)
    remote = [permuted(start, "blk", k) for k in range(2, blocks_z, 2)]
    for stage in stages:
        after = remote if stage == ("blk", 2) else []
        pieces = doubled_once(pieces, *stage, after)
    own = packed(tokens, pieces)
    weights = staged(pltpu.with_memory_space_constraint(weights, pltpu.HBM), own)
    chunks = [from_all(own, "ulysses")]
    chunks += [from_all(block, "ulysses") for block in remote]
    own_mod = assembled(chunks[0], "ulysses", *pieces.shape, width)
    mod_rows = [own_mod[0:1], own_mod[1:2]]

    far = [block for blocks in chunks[1:] for block in blocks[1:]]
    kv_parts = []
    for index, blocks in enumerate(chunks):
        first = min(index, 1)
        after = [[], [], far]
        if index:
            after = [[own[0]], [kv_parts[0]], []]
        sums = row_sums(blocks, width, after[0])
        small = [sums, permuted(sums, "tensor", 1), *mod_rows]
        *partial, normed = projected(blocks, small, weights, first, half, True, after[1])
        arrived = [permuted(part, "tensor", 1) for part in partial]
        own = projected([normed], [], weights, first, half, False)
        outs = split_heads(own, arrived, q_gain, k_gain, after[2])
        kv_parts.append(outs[0])
        if index == 0:
            queries = outs[1]
        if blocks_z > 1:
            arrived = permuted(outs[0], "blk", 1)
            kv_parts.append(arrived if index else copied(arrived, arrived, LONG))

    context = attention(queries, kv_parts, head_size)
    partial = out_projected(context, permuted(context, "tensor", 1), out_weight, rows)
    attended = added(to_all(partial, "ulysses"))
    mixed = tokens.astype(jnp.float32) + own_mod[2] * attended
    normed_two = normalized(mixed, features) * (1.0 + own_mod[4]) + own_mod[3]
    blocks = from_all(normed_two.astype(jnp.bfloat16), "ulysses")
    first = up_projected(blocks, up_weight, 0, 2)
    first_arrived = permuted(first, "tensor", 1)
    second = up_projected(blocks, up_weight, 1, 2)
    second_arrived = permuted(second, "tensor", 1)
    before = down_projected(first, first_arrived, down_weight, 0, 2, None, rows)[0]
    partial = down_projected(second, second_arrived, down_weight, 1, 2, before, rows)
    feedforward = added(to_all(partial, "ulysses"))
    return mixed + own_mod[5] * feedforward


def solution(mesh):
    sizes = [mesh.shape[axis] for axis in ("ulysses", "blk")]
    pairs = mesh.shape["tensor"] == 2 and all(size & (size - 1) == 0 for size in sizes)
    return jax.shard_map(
        on_pair if pairs else on_device,
        mesh=mesh,
        in_specs=(
            P(("ulysses", "blk"), "tensor"),
            P(),
            P(None, ("ulysses", "blk", "tensor")),
            P("tensor", None, "ulysses"),
            P(),
            P(),
            P("ulysses", "tensor"),
            P("tensor", "ulysses"),
            P("ulysses", "tensor"),
        ),
        out_specs=P(("ulysses", "blk"), "tensor"),
        check_vma=False,
    )
```

```python
import math

import jax
import jax.numpy as jnp
from jax import lax
from jax.experimental import pallas as pl
from jax.experimental.pallas import tpu as pltpu
from jax.sharding import PartitionSpec as P


def joined(array, axis, combine):
    everything = jax.tree.map(
        lambda part, kind: lax.all_gather(part.astype(kind), axis),
        array,
        jax.tree.map(lambda a: jnp.bfloat16 if a.dtype == jnp.float32 else a.dtype, array),
    )

    def take(k):
        return jax.tree.map(lambda part, own: part[k].astype(own.dtype), everything, array)

    return lax.fori_loop(
        1, lax.axis_size(axis), lambda k, so_far: combine(so_far, take(k)), take(0)
    )


def moments_norm(values, shift_row, scale_row, features):
    sums = lax.psum((jnp.sum(values, axis=-1), jnp.sum(values * values, axis=-1)), "tensor")
    average = sums[0][:, None] / features
    variance = sums[1][:, None] / features - average * average
    normal_rows = (values - average) * lax.rsqrt(variance + 1e-06)
    return (normal_rows * (1.0 + scale_row) + shift_row).astype(jnp.bfloat16)


def spread_rows(values):
    return lax.all_gather(values, "ulysses", axis=0, tiled=True)


def head_norm(values, gains):
    return values * lax.rsqrt(jnp.mean(values * values, axis=-1, keepdims=True) + 1e-06) * gains


def make_absorb(queries, score_scale, running, kv_block):
    keys_part, values_part = kv_block
    top_score, total_weight, summed = running
    scores = (
        jnp.einsum("qhd,khd->qhk", queries, keys_part, preferred_element_type=jnp.float32)
        * score_scale
    )
    new_top = jnp.max(scores, axis=-1)
    decay = jnp.exp(top_score - new_top)
    weights = jnp.exp(scores - new_top[..., None])
    total_weight = total_weight * decay + jnp.sum(weights, axis=-1)
    summed = summed * decay[..., None] + jnp.einsum(
        "qhk,khd->qhd",
        weights.astype(jnp.bfloat16),
        values_part,
        preferred_element_type=jnp.float32,
    )
    return (new_top, total_weight, summed)


def empty_state(row_count, heads_local, head_size):
    return (
        jnp.full((row_count, heads_local), -jnp.inf, jnp.float32),
        jnp.zeros((row_count, heads_local), jnp.float32),
        jnp.zeros((row_count, heads_local, head_size), jnp.float32),
    )


def combine_parts(first_part, second_part):
    top_score = jnp.maximum(first_part[0], second_part[0])
    first_decay = jnp.exp(first_part[0] - top_score)
    second_decay = jnp.exp(second_part[0] - top_score)
    total_weight = first_part[1] * first_decay + second_part[1] * second_decay
    summed = first_part[2] * first_decay[..., None] + second_part[2] * second_decay[..., None]
    return (top_score, total_weight, summed)


def on_device(
    tokens, cond, mod_weight, qkv_weight, q_gain, k_gain, out_weight, up_weight, down_weight
):
    tensor_size = lax.axis_size("tensor")
    tensor_pos = lax.axis_index("tensor")
    width = tokens.shape[1]
    features = width * tensor_size
    activated = jax.nn.silu(cond.astype(jnp.float32)).astype(jnp.bfloat16)
    local_mod = jnp.dot(activated[None, :], mod_weight, preferred_element_type=jnp.float32)[0]
    full_mod = lax.all_gather(local_mod, ("ulysses", "blk", "tensor"), axis=0, tiled=True).reshape(
        6, features
    )
    own_mod = lax.dynamic_slice_in_dim(full_mod, tensor_pos * width, width, 1)
    resid = tokens.astype(jnp.float32)
    normed = moments_norm(resid, own_mod[0], own_mod[1], features)
    gathered = spread_rows(normed)
    group_rows = gathered.shape[0]
    attn_rows = group_rows // tensor_size
    inner_local = qkv_weight.shape[2]
    head_size = q_gain.shape[0]
    heads_local = inner_local // head_size
    flat_qkv = qkv_weight.reshape(width, 3 * inner_local)
    projected = (
        lax.psum_scatter(
            jnp.dot(gathered, flat_qkv, preferred_element_type=jnp.float32).astype(jnp.bfloat16),
            "tensor",
            scatter_dimension=0,
            tiled=True,
        )
        .astype(jnp.float32)
        .reshape(attn_rows, 3, heads_local, head_size)
    )
    queries = head_norm(projected[:, 0], q_gain).astype(jnp.bfloat16)
    keys_local = head_norm(projected[:, 1], k_gain).astype(jnp.bfloat16)
    values_local = projected[:, 2].astype(jnp.bfloat16)
    score_scale = 1.0 / math.sqrt(head_size)
    all_queries = lax.all_gather(queries, "tensor", axis=0, tiled=True)
    state = make_absorb(
        all_queries,
        score_scale,
        empty_state(group_rows, heads_local, head_size),
        (
            lax.all_gather(keys_local, "blk", axis=0, tiled=True),
            lax.all_gather(values_local, "blk", axis=0, tiled=True),
        ),
    )
    merged = joined(state, "tensor", combine_parts)
    context = (
        (merged[2] / merged[1][..., None]).astype(jnp.bfloat16).reshape(group_rows, inner_local)
    )
    attended = lax.psum_scatter(
        jnp.dot(context, out_weight, preferred_element_type=jnp.float32).astype(jnp.bfloat16),
        "ulysses",
        scatter_dimension=0,
        tiled=True,
    ).astype(jnp.float32)
    mixed = resid + own_mod[2] * attended
    normed_two = moments_norm(mixed, own_mod[3], own_mod[4], features)
    gathered_two = spread_rows(normed_two)
    hidden = lax.psum_scatter(
        jnp.dot(gathered_two, up_weight, preferred_element_type=jnp.float32).astype(jnp.bfloat16),
        "tensor",
        scatter_dimension=0,
        tiled=True,
    ).astype(jnp.float32)
    activ = jax.nn.gelu(hidden, approximate=True).astype(jnp.bfloat16)
    activ_rows = lax.all_gather(activ, "tensor", axis=0, tiled=True)
    feedforward = lax.psum_scatter(
        jnp.dot(activ_rows, down_weight, preferred_element_type=jnp.float32).astype(jnp.bfloat16),
        "ulysses",
        scatter_dimension=0,
        tiled=True,
    ).astype(jnp.float32)
    return mixed + own_mod[5] * feedforward


VMEM_BYTES = 1024 * 1024
COPY_AT = 1
SHORT = pl.CostEstimate(flops=10000000000, bytes_accessed=0, transcendentals=0)
LONG = pl.CostEstimate(flops=10**10, bytes_accessed=0, transcendentals=0)
NO_COST = pl.CostEstimate(flops=0, bytes_accessed=0, transcendentals=0)


def permuted(values, axis, distance):
    size = lax.axis_size(axis)
    return lax.ppermute(values, axis, [(i, i ^ distance) for i in range(size)])


def from_all(values, axis):
    return [values] + [permuted(values, axis, k) for k in range(1, lax.axis_size(axis))]


def to_all(blocks, axis):
    return [blocks[0]] + [permuted(blocks[k], axis, k) for k in range(1, len(blocks))]


def after_specs(after):
    shapes = [(1,) * (dep.ndim - 2) + (min(16, dep.shape[-2]), 128) for dep in after]
    return [pl.BlockSpec(shape, lambda j, n=len(shape): (0,) * n) for shape in shapes]


def merge_kernel(axis, distance, own_ref, other_ref, *refs):
    out_ref = refs[-1]
    rows = own_ref.shape[0]
    upper = (lax.axis_index(axis) & distance) != 0
    out_ref[:rows, :] = jnp.where(upper, other_ref[...], own_ref[...])
    out_ref[rows:, :] = jnp.where(upper, own_ref[...], other_ref[...])


def doubled_once(piece, axis, distance, after):
    other = permuted(piece, axis, distance)
    rows, length = piece.shape
    block = pl.BlockSpec((rows, length), lambda j: (0, 0))
    return pl.pallas_call(
        lambda *refs: merge_kernel(axis, distance, *refs),
        grid=(1,),
        in_specs=[block, block] + after_specs(after),
        out_specs=pl.BlockSpec((2 * rows, length), lambda j: (0, 0)),
        out_shape=jax.ShapeDtypeStruct((2 * rows, length), piece.dtype),
        compiler_params=pltpu.CompilerParams(vmem_limit_bytes=VMEM_BYTES),
        cost_estimate=NO_COST,
        name="merged",
    )(piece, other, *after)


def lane_tiles(rows, count, length):
    return -(-(-(-length // 128)) // (rows // count))


def pack_kernel(values_ref, pieces_ref, out_ref):
    rows, width = values_ref.shape
    count, length = pieces_ref.shape
    per = rows // count
    out_ref[:, :width] = values_ref[...]
    for tile in range((out_ref.shape[1] - width) // 128):
        lines = []
        for row in range(count):
            for low in range(tile * per * 128, (tile + 1) * per * 128, 128):
                size = max(0, min(128, length - low))
                line = jnp.zeros((1, 128 - size), jnp.float32)
                if size:
                    part = pieces_ref[row : row + 1, low : low + size]
                    line = jnp.concatenate([part, line], axis=1) if size < 128 else part
                lines.append(line)
        columns = slice(width + tile * 128, width + (tile + 1) * 128)
        out_ref[:, columns] = jnp.concatenate(lines, axis=0).astype(jnp.bfloat16)


def packed(values, pieces):
    rows, width = values.shape
    columns = width + 128 * lane_tiles(rows, *pieces.shape)
    return pl.pallas_call(
        pack_kernel,
        out_shape=jax.ShapeDtypeStruct((rows, columns), jnp.bfloat16),
        compiler_params=pltpu.CompilerParams(vmem_limit_bytes=VMEM_BYTES * 2),
        cost_estimate=NO_COST,
        name="packed",
    )(values, pieces)


def assemble_kernel(axis, count, length, *refs):
    *tile_refs, out_ref, pieces_ref = refs
    position = lax.axis_index(axis)
    tiles = [ref[...].astype(jnp.float32) for ref in tile_refs]
    bit = 1
    while bit < len(tiles):
        flip = (position & bit) != 0
        tiles = [jnp.where(flip, tiles[i ^ bit], tiles[i]) for i in range(len(tiles))]
        bit *= 2
    per = tiles[0].shape[0] // count
    for block, tile in enumerate(tiles):
        for row in range(count):
            for low in range(0, length, 128):
                line = row * per + low // 128 % per
                columns = low // 128 // per * 128
                size = min(128, length - low)
                pieces_ref[block * count + row : block * count + row + 1, low : low + size] = tile[
                    line : line + 1, columns : columns + size
                ]
    width = out_ref.shape[1]
    vectors = out_ref.shape[0]
    halves = len(tiles) * count * length // (vectors * width)
    for half in range(halves):

        @pl.when(lax.axis_index("tensor") == half)
        def _(half=half):
            for vector in range(vectors):
                at = (vector * halves + half) * width
                end = at + width
                parts = []
                while at < end:
                    row, low = divmod(at, length)
                    high = min(length, low + end - at)
                    parts.append(pieces_ref[row : row + 1, low:high])
                    at += high - low
                out_ref[vector : vector + 1, :] = jnp.concatenate(parts, axis=1)


def assembled(blocks, axis, count, length, width):
    rows, columns = blocks[0].shape
    extra = columns - width
    return pl.pallas_call(
        lambda *refs: assemble_kernel(axis, count, length, *refs),
        grid=(1,),
        in_specs=[pl.BlockSpec((rows, extra), lambda j: (0, width // extra)) for _ in blocks],
        out_specs=pl.BlockSpec((6, width), lambda j: (0, 0)),
        out_shape=jax.ShapeDtypeStruct((6, width), jnp.float32),
        scratch_shapes=[pltpu.VMEM((len(blocks) * count, -(-length // 128) * 128), jnp.float32)],
        compiler_params=pltpu.CompilerParams(vmem_limit_bytes=VMEM_BYTES),
        cost_estimate=NO_COST,
        name="assembled",
    )(*blocks)


def row_sums_kernel(values_ref, out_ref, copy_ref):
    values = values_ref[...].astype(jnp.float32)
    lane = lax.broadcasted_iota(jnp.int32, out_ref.shape, 1)
    out_ref[...] = jnp.where(
        lane < out_ref.shape[1] // 2,
        jnp.sum(values, axis=-1, keepdims=True),
        jnp.sum(values * values, axis=-1, keepdims=True),
    )
    copy_ref[...] = values_ref[...]


def row_sums(values):
    return pl.pallas_call(
        row_sums_kernel,
        out_shape=[
            jax.ShapeDtypeStruct((values.shape[0], 128), jnp.float32),
            jax.ShapeDtypeStruct(values.shape, values.dtype),
        ],
        compiler_params=pltpu.CompilerParams(vmem_limit_bytes=VMEM_BYTES * 2),
        cost_estimate=NO_COST,
        name="row_sums",
    )(values)


def standardize_kernel(features, values_ref, own_ref, arrived_ref, *refs):
    total = own_ref[...] + arrived_ref[...]
    average = total[:, :1] / features
    variance = total[:, total.shape[1] // 2 :][:, :1] / features - average * average
    values = values_ref[...].astype(jnp.float32)
    refs[-1][...] = ((values - average) * lax.rsqrt(variance + 1e-06)).astype(jnp.bfloat16)


def standardized(values, features, after):
    own, values = row_sums(values)
    whole = lambda array: pl.BlockSpec(array.shape, lambda j: (0, 0))
    return pl.pallas_call(
        lambda *refs: standardize_kernel(features, *refs),
        grid=(1,),
        in_specs=[whole(values), whole(own), whole(own)] + after_specs(after),
        out_specs=whole(values),
        out_shape=jax.ShapeDtypeStruct(values.shape, jnp.bfloat16),
        compiler_params=pltpu.CompilerParams(vmem_limit_bytes=VMEM_BYTES * 2),
        cost_estimate=NO_COST,
        name="standardized",
    )(values, own, permuted(own, "tensor", 1), *after)


def stack_kernel(*refs):
    *block_refs, out_ref = refs
    rows = block_refs[0].shape[0]
    for k, block_ref in enumerate(block_refs):
        out_ref[k * rows : (k + 1) * rows, :] = block_ref[...]


def stacked(blocks):
    rows, width = blocks[0].shape
    return pl.pallas_call(
        stack_kernel,
        out_shape=jax.ShapeDtypeStruct((rows * len(blocks), width), blocks[0].dtype),
        compiler_params=pltpu.CompilerParams(vmem_limit_bytes=VMEM_BYTES * 2),
        cost_estimate=NO_COST,
        name="stacked",
    )(*blocks)


def copied_kernel(values_ref, after_ref, out_ref):
    out_ref[...] = values_ref[...]


def copied(values, after, cost):
    whole = pl.BlockSpec(values.shape, lambda j: (0, 0))
    return pl.pallas_call(
        copied_kernel,
        grid=(1,),
        in_specs=[whole] + after_specs([after]),
        out_specs=whole,
        out_shape=jax.ShapeDtypeStruct(values.shape, values.dtype),
        compiler_params=pltpu.CompilerParams(vmem_limit_bytes=VMEM_BYTES * 2),
        cost_estimate=cost,
        name="copied",
    )(values, after)


def normalized(values, features):
    sums = jnp.stack([jnp.sum(values, axis=-1), jnp.sum(values * values, axis=-1)])
    sums = sums + permuted(sums, "tensor", 1)
    average = sums[0][:, None] / features
    variance = sums[1][:, None] / features - average * average
    return (values - average) * lax.rsqrt(variance + 1e-06)


def product(left, right):
    return jnp.dot(left, right, preferred_element_type=jnp.float32).astype(jnp.bfloat16)


def added(blocks):
    total = blocks[0].astype(jnp.float32)
    for block in blocks[1:]:
        total = total + block.astype(jnp.float32)
    return total


def project_kernel(count, parts, other, *refs):
    block_refs = refs[:count]
    shift_ref, scale_ref = refs[count : count + 2]
    weight_refs = refs[count + 2 : count + 2 + parts]
    normed_ref = refs[-1]
    rows = block_refs[0].shape[0]
    for k, block_ref in enumerate(block_refs):
        values = block_ref[...].astype(jnp.float32)
        values = values * (1.0 + scale_ref[...]) + shift_ref[...]
        normed_ref[k * rows : (k + 1) * rows, :] = values.astype(jnp.bfloat16)
    project_parts(normed_ref, weight_refs, refs[-1 - parts : -1], other)


def project_parts(normed_ref, weight_refs, out_refs, other):
    half = out_refs[0].shape[1]
    position = lax.axis_index("tensor")
    low = pl.multiple_of((1 - position if other else position) * half, 128)
    for weight_ref, out_ref in zip(weight_refs, out_refs):
        out_ref[...] = jnp.dot(
            normed_ref[...], weight_ref[:, pl.ds(low, half)], preferred_element_type=jnp.float32
        ).astype(jnp.bfloat16)


def project_again_kernel(parts, other, normed_ref, *refs):
    project_parts(normed_ref, refs[:parts], refs[-parts:], other)


def projected(blocks, small, weights, half, other, after=()):
    rows, width = blocks[0].shape[0], weights[0].shape[0]
    all_rows = rows * len(blocks)
    count = len(weights)
    whole = lambda shape: pl.BlockSpec(shape, lambda j: (0, 0))
    shapes = [(all_rows, half)] * count + [(all_rows, width)] * bool(small)
    return pl.pallas_call(
        (lambda *refs: project_kernel(len(blocks), count, other, *refs))
        if small
        else (lambda *refs: project_again_kernel(count, other, *refs)),
        grid=(1,),
        in_specs=[whole((rows, width)) for _ in blocks]
        + [whole(array.shape) for array in small]
        + [pl.BlockSpec(memory_space=pltpu.VMEM) for _ in weights]
        + after_specs(after),
        out_specs=[whole(shape) for shape in shapes],
        out_shape=[jax.ShapeDtypeStruct(shape, jnp.bfloat16) for shape in shapes],
        compiler_params=pltpu.CompilerParams(vmem_limit_bytes=VMEM_BYTES * 20),
        cost_estimate=NO_COST,
        name="projected",
    )(*blocks, *small, *weights, *after)


def staged(weights, after, part=None):
    width, columns = weights.shape[-2:]
    pieces = 4 if width % 64 == 0 else 1
    rows = width // pieces
    anywhere = pl.BlockSpec(memory_space=pl.ANY)

    def kernel(weight_ref, after_ref, out_ref, sems):
        source_ref = weight_ref if part is None else weight_ref.at[part]
        copies = [
            pltpu.make_async_copy(
                source_ref.at[pl.ds(k * rows, rows)], out_ref.at[pl.ds(k * rows, rows)], sems.at[k]
            )
            for k in range(pieces)
        ]
        for copy in copies:
            copy.start()
        for copy in copies:
            copy.wait()

    return pl.pallas_call(
        kernel,
        grid=(1,),
        in_specs=[anywhere] + after_specs([after]),
        out_specs=pl.BlockSpec(memory_space=pltpu.VMEM),
        out_shape=pltpu.VMEM((width, columns), weights.dtype),
        scratch_shapes=[pltpu.SemaphoreType.DMA((pieces,))],
        compiler_params=pltpu.CompilerParams(vmem_limit_bytes=VMEM_BYTES),
        cost_estimate=pl.CostEstimate(
            flops=0, bytes_accessed=2 * width * columns, transcendentals=0
        ),
        name="staged",
    )(weights, after)


def mark_kernel(*refs):
    refs[-1][...] = jnp.zeros(refs[-1].shape, jnp.float32)


def mark(after, cost):
    return pl.pallas_call(
        mark_kernel,
        grid=(1,),
        in_specs=after_specs(after),
        out_specs=pl.BlockSpec((8, 128), lambda j: (0, 0)),
        out_shape=jax.ShapeDtypeStruct((8, 128), jnp.float32),
        compiler_params=pltpu.CompilerParams(vmem_limit_bytes=VMEM_BYTES),
        cost_estimate=cost,
        name="mark",
    )(*after)


def heads_kernel(count, head_size, *refs):
    own_refs, arrived_refs = refs[:count], refs[count : 2 * count]
    q_gain_ref, k_gain_ref = refs[2 * count : 2 * count + 2]
    out_refs = refs[-1:] if count == 2 else refs[-2:]
    half = own_refs[0].shape[1]

    def total(part, here):
        return own_refs[part][:, here].astype(jnp.float32) + arrived_refs[part][:, here].astype(
            jnp.float32
        )

    def normal(values, gain_ref):
        spread = jnp.mean(values * values, axis=-1, keepdims=True) + 1e-06
        return (values * lax.rsqrt(spread) * gain_ref[...]).astype(jnp.bfloat16)

    for low in range(0, half, head_size):
        here = slice(low, low + head_size)
        if count == 3:
            out_refs[1][:, here] = normal(total(0, here), q_gain_ref)
        out_refs[0][:, here] = normal(total(count - 2, here), k_gain_ref)
        out_refs[0][:, half + low : half + low + head_size] = total(count - 1, here).astype(
            jnp.bfloat16
        )


def split_heads(own, arrived, q_gain, k_gain, after=()):
    count = len(own)
    rows, half = own[0].shape
    head_size = q_gain.shape[0]
    widths = [2 * half] if count == 2 else [2 * half, half]
    whole = lambda *shape: pl.BlockSpec(shape, lambda j: (0, 0))
    return pl.pallas_call(
        lambda *refs: heads_kernel(count, head_size, *refs),
        grid=(1,),
        in_specs=[whole(rows, half)] * (2 * count)
        + [whole(1, head_size)] * 2
        + after_specs(after),
        out_specs=[whole(rows, width) for width in widths],
        out_shape=[jax.ShapeDtypeStruct((rows, width), jnp.bfloat16) for width in widths],
        compiler_params=pltpu.CompilerParams(vmem_limit_bytes=VMEM_BYTES * 5),
        cost_estimate=NO_COST,
        name="split_heads",
    )(*own, *arrived, q_gain[None, :], k_gain[None, :], *after)


def attention_kernel(head_size, count, query_ref, *refs):
    kv_refs, out_ref = refs[:count], refs[-1]
    half = query_ref.shape[1]
    score_scale = 1.0 / math.sqrt(head_size)
    for lo in range(0, half, head_size):
        query = query_ref[:, lo : lo + head_size]
        scores = [
            lax.dot_general(
                query,
                kv_ref[:, lo : lo + head_size],
                (((1,), (1,)), ((), ())),
                preferred_element_type=jnp.float32,
            )
            * score_scale
            for kv_ref in kv_refs
        ]
        top = jnp.max(scores[0], axis=-1, keepdims=True)
        for part in scores[1:]:
            top = jnp.maximum(top, jnp.max(part, axis=-1, keepdims=True))
        denominator, summed = 0.0, 0.0
        for part, kv_ref in zip(scores, kv_refs):
            weights = jnp.exp(part - top)
            denominator = denominator + jnp.sum(weights, axis=-1, keepdims=True)
            summed = summed + jnp.dot(
                weights.astype(jnp.bfloat16),
                kv_ref[:, half + lo : half + lo + head_size],
                preferred_element_type=jnp.float32,
            )
        out_ref[:, lo : lo + head_size] = (summed / denominator).astype(jnp.bfloat16)


def attention(queries, kv_parts, head_size, after):
    rows, half = queries.shape
    keys = sum(part.shape[0] for part in kv_parts)
    return pl.pallas_call(
        lambda *refs: attention_kernel(head_size, len(kv_parts), *refs),
        grid=(1,),
        in_specs=[pl.BlockSpec(array.shape, lambda j: (0, 0)) for array in [queries, *kv_parts]]
        + after_specs(after),
        out_specs=pl.BlockSpec((rows, half), lambda j: (0, 0)),
        out_shape=jax.ShapeDtypeStruct((rows, half), jnp.bfloat16),
        compiler_params=pltpu.CompilerParams(vmem_limit_bytes=VMEM_BYTES * 12),
        cost_estimate=pl.CostEstimate(
            flops=4 * rows * keys * half,
            bytes_accessed=4 * keys * half,
            transcendentals=rows * keys * half // head_size,
        ),
        name="attention",
    )(queries, *kv_parts, *after)


def column_tiles(columns):
    size = columns // 3 if columns % 384 == 0 else columns
    return [slice(low, low + size) for low in range(0, columns, size)]


def out_kernel(own_ref, arrived_ref, weight_ref, *out_refs):
    half = own_ref.shape[1]
    position = lax.axis_index("tensor")
    rows = [pl.ds(pl.multiple_of(at * half, 16), half) for at in (position, 1 - position)]
    for here in column_tiles(weight_ref.shape[1]):
        total = jnp.dot(
            own_ref[...], weight_ref[rows[0], here], preferred_element_type=jnp.float32
        ) + jnp.dot(arrived_ref[...], weight_ref[rows[1], here], preferred_element_type=jnp.float32)
        row_blocks(total, here, out_refs)


def row_blocks(values, columns, out_refs):
    rows = out_refs[0].shape[0]
    for k, out_ref in enumerate(out_refs):
        out_ref[:, columns] = values[k * rows : (k + 1) * rows].astype(jnp.bfloat16)


def out_projected(own, arrived, weight, rows):
    all_rows, half = own.shape
    width = weight.shape[1]
    whole = pl.BlockSpec((all_rows, half), lambda j: (0, 0))
    return pl.pallas_call(
        out_kernel,
        grid=(1,),
        in_specs=[whole, whole, pl.BlockSpec(memory_space=pltpu.VMEM)],
        out_specs=[pl.BlockSpec((rows, width), lambda j: (0, 0))] * (all_rows // rows),
        out_shape=[jax.ShapeDtypeStruct((rows, width), jnp.bfloat16)] * (all_rows // rows),
        compiler_params=pltpu.CompilerParams(vmem_limit_bytes=VMEM_BYTES * 8),
        cost_estimate=NO_COST,
        name="out_projected",
    )(own, arrived, weight)


def up_kernel(first, count, *refs):
    block_refs, weight_ref, (out_ref, joined_ref) = refs[:count], refs[count], refs[-2:]
    rows = block_refs[0].shape[0]
    for k, block_ref in enumerate(block_refs):
        joined_ref[k * rows : (k + 1) * rows, :] = block_ref[...]
    for here in column_tiles(out_ref.shape[1]):
        out_ref[:, here] = jnp.dot(
            joined_ref[...],
            weight_ref[:, first + here.start : first + here.stop],
            preferred_element_type=jnp.float32,
        ).astype(jnp.bfloat16)


def up_projected(blocks, weight, part, parts, after=()):
    rows, width = blocks[0].shape
    all_rows = rows * len(blocks)
    columns = weight.shape[1] // parts
    return pl.pallas_call(
        lambda *refs: up_kernel(part * columns, len(blocks), *refs),
        grid=(1,),
        in_specs=[pl.BlockSpec((rows, width), lambda j: (0, 0)) for _ in blocks]
        + [pl.BlockSpec(memory_space=pltpu.VMEM)]
        + after_specs(after),
        out_specs=pl.BlockSpec((all_rows, columns), lambda j: (0, 0)),
        out_shape=jax.ShapeDtypeStruct((all_rows, columns), jnp.bfloat16),
        scratch_shapes=[pltpu.VMEM((all_rows, width), jnp.bfloat16)],
        compiler_params=pltpu.CompilerParams(vmem_limit_bytes=VMEM_BYTES * 8),
        cost_estimate=pl.CostEstimate(
            flops=2 * all_rows * width * columns, bytes_accessed=0, transcendentals=0
        ),
        name="up_projected",
    )(*blocks, weight, *after)


def down_kernel(first, last, own_ref, arrived_ref, weight_ref, *refs):
    *out_refs, activ_ref = refs
    depth = own_ref.shape[1]
    for here in column_tiles(depth):
        hidden = own_ref[:, here].astype(jnp.float32) + arrived_ref[:, here].astype(jnp.float32)
        activ_ref[:, here] = jax.nn.gelu(hidden, approximate=True).astype(jnp.bfloat16)
    for here in column_tiles(weight_ref.shape[1]):
        total = jnp.dot(
            activ_ref[...],
            weight_ref[first : first + depth, here],
            preferred_element_type=jnp.float32,
        )
        if last:
            row_blocks(total + out_refs[0][:, here], here, out_refs[1:])
        else:
            out_refs[0][:, here] = total


def down_projected(own, arrived, weight, part, before, rows):
    all_rows, depth = own.shape
    width = weight.shape[1]
    last = before is not None
    whole = pl.BlockSpec((all_rows, width), lambda j: (0, 0))
    if last:
        shapes = [jax.ShapeDtypeStruct((rows, width), jnp.bfloat16)] * (all_rows // rows)
        out_specs = [pl.BlockSpec((rows, width), lambda j: (0, 0))] * (all_rows // rows)
    else:
        shapes = [jax.ShapeDtypeStruct((all_rows, width), jnp.float32)]
        out_specs = [whole]
    return pl.pallas_call(
        lambda *refs: down_kernel(part * depth, last, *refs),
        grid=(1,),
        in_specs=[pl.BlockSpec((all_rows, depth), lambda j: (0, 0))] * 2
        + [pl.BlockSpec(memory_space=pltpu.VMEM)]
        + [whole] * last,
        out_specs=out_specs,
        out_shape=shapes,
        scratch_shapes=[pltpu.VMEM((all_rows, depth), jnp.bfloat16)],
        compiler_params=pltpu.CompilerParams(vmem_limit_bytes=VMEM_BYTES * 12),
        cost_estimate=pl.CostEstimate(
            flops=2 * all_rows * width * depth,
            bytes_accessed=0,
            transcendentals=all_rows * depth,
        ),
        name="down_projected",
    )(own, arrived, weight, *([before] * last))


def on_pair(
    tokens, cond, mod_weight, qkv_weight, q_gain, k_gain, out_weight, up_weight, down_weight
):
    stages = [
        (axis, 1 << bit)
        for axis in ("tensor", "blk")
        for bit in range(lax.axis_size(axis).bit_length() - 1)
    ]
    rows, width = tokens.shape
    features = width * lax.axis_size("tensor")
    head_size = q_gain.shape[0]
    half = qkv_weight.shape[2] // 2
    blocks_z = lax.axis_size("blk")

    activated = jax.nn.silu(cond.astype(jnp.float32)).astype(jnp.bfloat16)
    pieces = jnp.dot(activated[None, :], mod_weight, preferred_element_type=jnp.float32)
    weights, out_weight, up_weight, down_weight = [
        pltpu.with_memory_space_constraint(weight, pltpu.HBM)
        for weight in (jnp.moveaxis(qkv_weight, 1, 0), out_weight, up_weight, down_weight)
    ]
    start = copied(tokens, pieces, NO_COST)
    remote = [permuted(start, "blk", k) for k in range(2, blocks_z, 2)]
    normal = standardized(tokens, features, [])
    parts = []
    for stage in stages:
        after = []
        if stage[0] == "blk":
            take = [0] if stage[1] == 1 else range(len(parts), weights.shape[0])
            parts += [staged(weights, pieces, part) for part in take]
            after = parts + (remote if stage[1] == 2 else [normal])
        pieces = doubled_once(pieces, *stage, after)
    own = packed(normal, pieces)
    chunks = [from_all(own, "ulysses")]
    if remote:
        far = stacked(remote + [permuted(block, "blk", 1) for block in remote])
        far = standardized(far, features, [])
        chunks.append(from_all(far, "ulysses"))
    own_mod = assembled(chunks[0], "ulysses", *pieces.shape, width)
    mod_rows = [own_mod[0:1], own_mod[1:2]]

    kv_parts = []
    for index, blocks in enumerate(chunks):
        use = parts[min(index, 1) :]
        after = [kv_parts[0], mark(blocks[1:], SHORT)] if index else [far] * bool(remote)
        *partial, normed = projected(blocks, mod_rows, use, half, True, after)
        arrived = [permuted(part, "tensor", 1) for part in partial]
        own = projected([normed], [], use, half, False)
        outs = split_heads(own, arrived, q_gain, k_gain)
        kv_parts.append(outs[0])
        if index == 0:
            queries = outs[1]
            if blocks_z > 1:
                arrived = permuted(outs[0], "blk", 1)
                kv_parts.append(copied(arrived, arrived, LONG))

    out_weight = staged(out_weight, kv_parts[0])
    up_weight = staged(up_weight, out_weight)
    down_weight = staged(down_weight, up_weight)
    context = attention(queries, kv_parts, head_size, [out_weight, up_weight])
    partial = out_projected(context, permuted(context, "tensor", 1), out_weight, rows)
    attended = added(to_all(partial, "ulysses"))
    mixed = tokens.astype(jnp.float32) + own_mod[2] * attended
    normed_two = normalized(mixed, features) * (1.0 + own_mod[4]) + own_mod[3]
    blocks = from_all(normed_two.astype(jnp.bfloat16), "ulysses")
    first = up_projected(blocks, up_weight, 0, 2, [down_weight])
    first_arrived = permuted(first, "tensor", 1)
    second = up_projected(blocks, up_weight, 1, 2)
    second_arrived = permuted(second, "tensor", 1)
    before = down_projected(first, first_arrived, down_weight, 0, None, rows)[0]
    partial = down_projected(second, second_arrived, down_weight, 1, before, rows)
    feedforward = added(to_all(partial, "ulysses"))
    return mixed + own_mod[5] * feedforward


def solution(mesh):
    sizes = [mesh.shape[axis] for axis in ("ulysses", "blk")]
    pairs = mesh.shape["tensor"] == 2 and all(size & (size - 1) == 0 for size in sizes)
    return jax.shard_map(
        on_pair if pairs else on_device,
        mesh=mesh,
        in_specs=(
            P(("ulysses", "blk"), "tensor"),
            P(),
            P(None, ("ulysses", "blk", "tensor")),
            P("tensor", None, "ulysses"),
            P(),
            P(),
            P("ulysses", "tensor"),
            P("tensor", "ulysses"),
            P("ulysses", "tensor"),
        ),
        out_specs=P(("ulysses", "blk"), "tensor"),
        check_vma=False,
    )
```

```python
import math

import jax
import jax.numpy as jnp
from jax import lax
from jax.experimental import pallas as pl
from jax.experimental.pallas import tpu as pltpu
from jax.sharding import PartitionSpec as P


def joined(array, axis, combine):
    everything = jax.tree.map(
        lambda part, kind: lax.all_gather(part.astype(kind), axis),
        array,
        jax.tree.map(lambda a: jnp.bfloat16 if a.dtype == jnp.float32 else a.dtype, array),
    )

    def take(k):
        return jax.tree.map(lambda part, own: part[k].astype(own.dtype), everything, array)

    return lax.fori_loop(
        1, lax.axis_size(axis), lambda k, so_far: combine(so_far, take(k)), take(0)
    )


def moments_norm(values, shift_row, scale_row, features):
    sums = lax.psum((jnp.sum(values, axis=-1), jnp.sum(values * values, axis=-1)), "tensor")
    average = sums[0][:, None] / features
    variance = sums[1][:, None] / features - average * average
    normal_rows = (values - average) * lax.rsqrt(variance + 1e-06)
    return (normal_rows * (1.0 + scale_row) + shift_row).astype(jnp.bfloat16)


def spread_rows(values):
    return lax.all_gather(values, "ulysses", axis=0, tiled=True)


def head_norm(values, gains):
    return values * lax.rsqrt(jnp.mean(values * values, axis=-1, keepdims=True) + 1e-06) * gains


def make_absorb(queries, score_scale, running, kv_block):
    keys_part, values_part = kv_block
    top_score, total_weight, summed = running
    scores = (
        jnp.einsum("qhd,khd->qhk", queries, keys_part, preferred_element_type=jnp.float32)
        * score_scale
    )
    new_top = jnp.max(scores, axis=-1)
    decay = jnp.exp(top_score - new_top)
    weights = jnp.exp(scores - new_top[..., None])
    total_weight = total_weight * decay + jnp.sum(weights, axis=-1)
    summed = summed * decay[..., None] + jnp.einsum(
        "qhk,khd->qhd",
        weights.astype(jnp.bfloat16),
        values_part,
        preferred_element_type=jnp.float32,
    )
    return (new_top, total_weight, summed)


def empty_state(row_count, heads_local, head_size):
    return (
        jnp.full((row_count, heads_local), -jnp.inf, jnp.float32),
        jnp.zeros((row_count, heads_local), jnp.float32),
        jnp.zeros((row_count, heads_local, head_size), jnp.float32),
    )


def combine_parts(first_part, second_part):
    top_score = jnp.maximum(first_part[0], second_part[0])
    first_decay = jnp.exp(first_part[0] - top_score)
    second_decay = jnp.exp(second_part[0] - top_score)
    total_weight = first_part[1] * first_decay + second_part[1] * second_decay
    summed = first_part[2] * first_decay[..., None] + second_part[2] * second_decay[..., None]
    return (top_score, total_weight, summed)


def on_device(
    tokens, cond, mod_weight, qkv_weight, q_gain, k_gain, out_weight, up_weight, down_weight
):
    tensor_size = lax.axis_size("tensor")
    tensor_pos = lax.axis_index("tensor")
    width = tokens.shape[1]
    features = width * tensor_size
    activated = jax.nn.silu(cond.astype(jnp.float32)).astype(jnp.bfloat16)
    local_mod = jnp.dot(activated[None, :], mod_weight, preferred_element_type=jnp.float32)[0]
    full_mod = lax.all_gather(local_mod, ("ulysses", "blk", "tensor"), axis=0, tiled=True).reshape(
        6, features
    )
    own_mod = lax.dynamic_slice_in_dim(full_mod, tensor_pos * width, width, 1)
    resid = tokens.astype(jnp.float32)
    normed = moments_norm(resid, own_mod[0], own_mod[1], features)
    gathered = spread_rows(normed)
    group_rows = gathered.shape[0]
    attn_rows = group_rows // tensor_size
    inner_local = qkv_weight.shape[2]
    head_size = q_gain.shape[0]
    heads_local = inner_local // head_size
    flat_qkv = qkv_weight.reshape(width, 3 * inner_local)
    projected = (
        lax.psum_scatter(
            jnp.dot(gathered, flat_qkv, preferred_element_type=jnp.float32).astype(jnp.bfloat16),
            "tensor",
            scatter_dimension=0,
            tiled=True,
        )
        .astype(jnp.float32)
        .reshape(attn_rows, 3, heads_local, head_size)
    )
    queries = head_norm(projected[:, 0], q_gain).astype(jnp.bfloat16)
    keys_local = head_norm(projected[:, 1], k_gain).astype(jnp.bfloat16)
    values_local = projected[:, 2].astype(jnp.bfloat16)
    score_scale = 1.0 / math.sqrt(head_size)
    all_queries = lax.all_gather(queries, "tensor", axis=0, tiled=True)
    state = make_absorb(
        all_queries,
        score_scale,
        empty_state(group_rows, heads_local, head_size),
        (
            lax.all_gather(keys_local, "blk", axis=0, tiled=True),
            lax.all_gather(values_local, "blk", axis=0, tiled=True),
        ),
    )
    merged = joined(state, "tensor", combine_parts)
    context = (
        (merged[2] / merged[1][..., None]).astype(jnp.bfloat16).reshape(group_rows, inner_local)
    )
    attended = lax.psum_scatter(
        jnp.dot(context, out_weight, preferred_element_type=jnp.float32).astype(jnp.bfloat16),
        "ulysses",
        scatter_dimension=0,
        tiled=True,
    ).astype(jnp.float32)
    mixed = resid + own_mod[2] * attended
    normed_two = moments_norm(mixed, own_mod[3], own_mod[4], features)
    gathered_two = spread_rows(normed_two)
    hidden = lax.psum_scatter(
        jnp.dot(gathered_two, up_weight, preferred_element_type=jnp.float32).astype(jnp.bfloat16),
        "tensor",
        scatter_dimension=0,
        tiled=True,
    ).astype(jnp.float32)
    activ = jax.nn.gelu(hidden, approximate=True).astype(jnp.bfloat16)
    activ_rows = lax.all_gather(activ, "tensor", axis=0, tiled=True)
    feedforward = lax.psum_scatter(
        jnp.dot(activ_rows, down_weight, preferred_element_type=jnp.float32).astype(jnp.bfloat16),
        "ulysses",
        scatter_dimension=0,
        tiled=True,
    ).astype(jnp.float32)
    return mixed + own_mod[5] * feedforward


VMEM_BYTES = 1024 * 1024
COPY_AT = 1
SHORT = pl.CostEstimate(flops=10**10, bytes_accessed=0, transcendentals=0)
LONG = pl.CostEstimate(flops=10**10, bytes_accessed=0, transcendentals=0)
NO_COST = pl.CostEstimate(flops=0, bytes_accessed=0, transcendentals=0)


def permuted(values, axis, distance):
    size = lax.axis_size(axis)
    return lax.ppermute(values, axis, [(i, i ^ distance) for i in range(size)])


def from_all(values, axis):
    return [values] + [permuted(values, axis, k) for k in range(1, lax.axis_size(axis))]


def to_all(blocks, axis):
    return [blocks[0]] + [permuted(blocks[k], axis, k) for k in range(1, len(blocks))]


def after_specs(after):
    shapes = [(1,) * (dep.ndim - 2) + (min(16, dep.shape[-2]), 128) for dep in after]
    return [pl.BlockSpec(shape, lambda j, n=len(shape): (0,) * n) for shape in shapes]


def merge_kernel(axis, distance, own_ref, other_ref, *refs):
    out_ref = refs[-1]
    rows = own_ref.shape[0]
    upper = (lax.axis_index(axis) & distance) != 0
    out_ref[:rows, :] = jnp.where(upper, other_ref[...], own_ref[...])
    out_ref[rows:, :] = jnp.where(upper, own_ref[...], other_ref[...])


def doubled_once(piece, axis, distance, after):
    other = permuted(piece, axis, distance)
    rows, length = piece.shape
    block = pl.BlockSpec((rows, length), lambda j: (0, 0))
    return pl.pallas_call(
        lambda *refs: merge_kernel(axis, distance, *refs),
        grid=(1,),
        in_specs=[block, block] + after_specs(after),
        out_specs=pl.BlockSpec((2 * rows, length), lambda j: (0, 0)),
        out_shape=jax.ShapeDtypeStruct((2 * rows, length), piece.dtype),
        compiler_params=pltpu.CompilerParams(vmem_limit_bytes=VMEM_BYTES),
        cost_estimate=NO_COST,
        name="merged",
    )(piece, other, *after)


def lane_tiles(rows, count, length):
    return -(-(-(-length // 128)) // (rows // count))


def pack_kernel(values_ref, pieces_ref, out_ref):
    rows, width = values_ref.shape
    count, length = pieces_ref.shape
    per = rows // count
    out_ref[:, :width] = values_ref[...]
    for tile in range((out_ref.shape[1] - width) // 128):
        lines = []
        for row in range(count):
            for low in range(tile * per * 128, (tile + 1) * per * 128, 128):
                size = max(0, min(128, length - low))
                line = jnp.zeros((1, 128 - size), jnp.float32)
                if size:
                    part = pieces_ref[row : row + 1, low : low + size]
                    line = jnp.concatenate([part, line], axis=1) if size < 128 else part
                lines.append(line)
        columns = slice(width + tile * 128, width + (tile + 1) * 128)
        out_ref[:, columns] = jnp.concatenate(lines, axis=0).astype(jnp.bfloat16)


def packed(values, pieces):
    rows, width = values.shape
    columns = width + 128 * lane_tiles(rows, *pieces.shape)
    return pl.pallas_call(
        pack_kernel,
        out_shape=jax.ShapeDtypeStruct((rows, columns), jnp.bfloat16),
        compiler_params=pltpu.CompilerParams(vmem_limit_bytes=VMEM_BYTES * 2),
        cost_estimate=NO_COST,
        name="packed",
    )(values, pieces)


def assemble_kernel(axis, count, length, *refs):
    *tile_refs, out_ref, pieces_ref = refs
    position = lax.axis_index(axis)
    tiles = [ref[...].astype(jnp.float32) for ref in tile_refs]
    bit = 1
    while bit < len(tiles):
        flip = (position & bit) != 0
        tiles = [jnp.where(flip, tiles[i ^ bit], tiles[i]) for i in range(len(tiles))]
        bit *= 2
    per = tiles[0].shape[0] // count
    for block, tile in enumerate(tiles):
        for row in range(count):
            for low in range(0, length, 128):
                line = row * per + low // 128 % per
                columns = low // 128 // per * 128
                size = min(128, length - low)
                pieces_ref[block * count + row : block * count + row + 1, low : low + size] = tile[
                    line : line + 1, columns : columns + size
                ]
    width = out_ref.shape[1]
    vectors = out_ref.shape[0]
    halves = len(tiles) * count * length // (vectors * width)
    for half in range(halves):

        @pl.when(lax.axis_index("tensor") == half)
        def _(half=half):
            for vector in range(vectors):
                at = (vector * halves + half) * width
                end = at + width
                parts = []
                while at < end:
                    row, low = divmod(at, length)
                    high = min(length, low + end - at)
                    parts.append(pieces_ref[row : row + 1, low:high])
                    at += high - low
                out_ref[vector : vector + 1, :] = jnp.concatenate(parts, axis=1)


def assembled(blocks, axis, count, length, width):
    rows, columns = blocks[0].shape
    extra = columns - width
    return pl.pallas_call(
        lambda *refs: assemble_kernel(axis, count, length, *refs),
        grid=(1,),
        in_specs=[pl.BlockSpec((rows, extra), lambda j: (0, width // extra)) for _ in blocks],
        out_specs=pl.BlockSpec((6, width), lambda j: (0, 0)),
        out_shape=jax.ShapeDtypeStruct((6, width), jnp.float32),
        scratch_shapes=[pltpu.VMEM((len(blocks) * count, -(-length // 128) * 128), jnp.float32)],
        compiler_params=pltpu.CompilerParams(vmem_limit_bytes=VMEM_BYTES),
        cost_estimate=NO_COST,
        name="assembled",
    )(*blocks)


def row_sums_kernel(values_ref, out_ref, copy_ref):
    values = values_ref[...].astype(jnp.float32)
    lane = lax.broadcasted_iota(jnp.int32, out_ref.shape, 1)
    out_ref[...] = jnp.where(
        lane < out_ref.shape[1] // 2,
        jnp.sum(values, axis=-1, keepdims=True),
        jnp.sum(values * values, axis=-1, keepdims=True),
    )
    copy_ref[...] = values_ref[...]


def row_sums(values):
    return pl.pallas_call(
        row_sums_kernel,
        out_shape=[
            jax.ShapeDtypeStruct((values.shape[0], 128), jnp.float32),
            jax.ShapeDtypeStruct(values.shape, values.dtype),
        ],
        compiler_params=pltpu.CompilerParams(vmem_limit_bytes=VMEM_BYTES * 2),
        cost_estimate=NO_COST,
        name="row_sums",
    )(values)


def standardize_kernel(features, values_ref, own_ref, arrived_ref, *refs):
    total = own_ref[...] + arrived_ref[...]
    average = total[:, :1] / features
    variance = total[:, total.shape[1] // 2 :][:, :1] / features - average * average
    values = values_ref[...].astype(jnp.float32)
    refs[-1][...] = ((values - average) * lax.rsqrt(variance + 1e-06)).astype(jnp.bfloat16)


def standardized(values, features, after):
    own, values = row_sums(values)
    whole = lambda array: pl.BlockSpec(array.shape, lambda j: (0, 0))
    return pl.pallas_call(
        lambda *refs: standardize_kernel(features, *refs),
        grid=(1,),
        in_specs=[whole(values), whole(own), whole(own)] + after_specs(after),
        out_specs=whole(values),
        out_shape=jax.ShapeDtypeStruct(values.shape, jnp.bfloat16),
        compiler_params=pltpu.CompilerParams(vmem_limit_bytes=VMEM_BYTES * 2),
        cost_estimate=NO_COST,
        name="standardized",
    )(values, own, permuted(own, "tensor", 1), *after)


def stack_kernel(*refs):
    *block_refs, out_ref = refs
    rows = block_refs[0].shape[0]
    for k, block_ref in enumerate(block_refs):
        out_ref[k * rows : (k + 1) * rows, :] = block_ref[...]


def stacked(blocks, cost):
    rows, width = blocks[0].shape
    return pl.pallas_call(
        stack_kernel,
        out_shape=jax.ShapeDtypeStruct((rows * len(blocks), width), blocks[0].dtype),
        compiler_params=pltpu.CompilerParams(vmem_limit_bytes=VMEM_BYTES * 2),
        cost_estimate=cost,
        name="stacked",
    )(*blocks)


def copied_kernel(values_ref, after_ref, out_ref):
    out_ref[...] = values_ref[...]


def copied(values, after, cost):
    whole = pl.BlockSpec(values.shape, lambda j: (0, 0))
    return pl.pallas_call(
        copied_kernel,
        grid=(1,),
        in_specs=[whole] + after_specs([after]),
        out_specs=whole,
        out_shape=jax.ShapeDtypeStruct(values.shape, values.dtype),
        compiler_params=pltpu.CompilerParams(vmem_limit_bytes=VMEM_BYTES * 2),
        cost_estimate=cost,
        name="copied",
    )(values, after)


def added(blocks):
    total = blocks[0].astype(jnp.float32)
    for block in blocks[1:]:
        total = total + block.astype(jnp.float32)
    return total


def project_kernel(count, parts, other, *refs):
    block_refs = refs[:count]
    shift_ref, scale_ref = refs[count : count + 2]
    weight_refs = refs[count + 2 : count + 2 + parts]
    normed_ref = refs[-1]
    rows = block_refs[0].shape[0]
    for k, block_ref in enumerate(block_refs):
        values = block_ref[...].astype(jnp.float32)
        values = values * (1.0 + scale_ref[...]) + shift_ref[...]
        normed_ref[k * rows : (k + 1) * rows, :] = values.astype(jnp.bfloat16)
    project_parts(normed_ref, weight_refs, refs[-1 - parts : -1], other)


def project_parts(normed_ref, weight_refs, out_refs, other):
    half = out_refs[0].shape[1]
    position = lax.axis_index("tensor")
    low = pl.multiple_of((1 - position if other else position) * half, 128)
    for weight_ref, out_ref in zip(weight_refs, out_refs):
        out_ref[...] = jnp.dot(
            normed_ref[...], weight_ref[:, pl.ds(low, half)], preferred_element_type=jnp.float32
        ).astype(jnp.bfloat16)


def project_again_kernel(parts, other, normed_ref, *refs):
    project_parts(normed_ref, refs[:parts], refs[-parts:], other)


def projected(blocks, small, weights, half, other, after=()):
    rows, width = blocks[0].shape[0], weights[0].shape[0]
    all_rows = rows * len(blocks)
    count = len(weights)
    whole = lambda shape: pl.BlockSpec(shape, lambda j: (0, 0))
    shapes = [(all_rows, half)] * count + [(all_rows, width)] * bool(small)
    return pl.pallas_call(
        (lambda *refs: project_kernel(len(blocks), count, other, *refs))
        if small
        else (lambda *refs: project_again_kernel(count, other, *refs)),
        grid=(1,),
        in_specs=[whole((rows, width)) for _ in blocks]
        + [whole(array.shape) for array in small]
        + [pl.BlockSpec(memory_space=pltpu.VMEM) for _ in weights]
        + after_specs(after),
        out_specs=[whole(shape) for shape in shapes],
        out_shape=[jax.ShapeDtypeStruct(shape, jnp.bfloat16) for shape in shapes],
        compiler_params=pltpu.CompilerParams(vmem_limit_bytes=VMEM_BYTES * 20),
        cost_estimate=NO_COST,
        name="projected",
    )(*blocks, *small, *weights, *after)


def staged(weights, after, part=None):
    width, columns = weights.shape[-2:]
    pieces = 4 if width % 64 == 0 else 1
    rows = width // pieces
    anywhere = pl.BlockSpec(memory_space=pl.ANY)

    def kernel(weight_ref, after_ref, out_ref, sems):
        source_ref = weight_ref if part is None else weight_ref.at[part]
        copies = [
            pltpu.make_async_copy(
                source_ref.at[pl.ds(k * rows, rows)], out_ref.at[pl.ds(k * rows, rows)], sems.at[k]
            )
            for k in range(pieces)
        ]
        for copy in copies:
            copy.start()
        for copy in copies:
            copy.wait()

    return pl.pallas_call(
        kernel,
        grid=(1,),
        in_specs=[anywhere] + after_specs([after]),
        out_specs=pl.BlockSpec(memory_space=pltpu.VMEM),
        out_shape=pltpu.VMEM((width, columns), weights.dtype),
        scratch_shapes=[pltpu.SemaphoreType.DMA((pieces,))],
        compiler_params=pltpu.CompilerParams(vmem_limit_bytes=VMEM_BYTES),
        cost_estimate=pl.CostEstimate(
            flops=0, bytes_accessed=2 * width * columns, transcendentals=0
        ),
        name="staged",
    )(weights, after)


def mark_kernel(*refs):
    refs[-1][...] = jnp.zeros(refs[-1].shape, jnp.float32)


def mark(after, cost):
    return pl.pallas_call(
        mark_kernel,
        grid=(1,),
        in_specs=after_specs(after),
        out_specs=pl.BlockSpec((8, 128), lambda j: (0, 0)),
        out_shape=jax.ShapeDtypeStruct((8, 128), jnp.float32),
        compiler_params=pltpu.CompilerParams(vmem_limit_bytes=VMEM_BYTES),
        cost_estimate=cost,
        name="mark",
    )(*after)


def head_normal(values, gain_ref):
    spread = jnp.mean(values * values, axis=-1, keepdims=True) + 1e-06
    return (values * lax.rsqrt(spread) * gain_ref[...]).astype(jnp.bfloat16)


def heads_kernel(count, head_size, *refs):
    own_refs, arrived_refs = refs[:count], refs[count : 2 * count]
    q_gain_ref, k_gain_ref = refs[2 * count : 2 * count + 2]
    out_refs = refs[-1:] if count == 2 else refs[-2:]
    half = own_refs[0].shape[1]

    def total(part, here):
        return own_refs[part][:, here].astype(jnp.float32) + arrived_refs[part][:, here].astype(
            jnp.float32
        )

    for low in range(0, half, head_size):
        here = slice(low, low + head_size)
        if count == 3:
            out_refs[1][:, here] = head_normal(total(0, here), q_gain_ref)
        out_refs[0][:, here] = head_normal(total(count - 2, here), k_gain_ref)
        out_refs[0][:, half + low : half + low + head_size] = total(count - 1, here).astype(
            jnp.bfloat16
        )


def split_heads(own, arrived, q_gain, k_gain, after=()):
    count = len(own)
    rows, half = own[0].shape
    head_size = q_gain.shape[0]
    widths = [2 * half] if count == 2 else [2 * half, half]
    whole = lambda *shape: pl.BlockSpec(shape, lambda j: (0, 0))
    return pl.pallas_call(
        lambda *refs: heads_kernel(count, head_size, *refs),
        grid=(1,),
        in_specs=[whole(rows, half)] * (2 * count)
        + [whole(1, head_size)] * 2
        + after_specs(after),
        out_specs=[whole(rows, width) for width in widths],
        out_shape=[jax.ShapeDtypeStruct((rows, width), jnp.bfloat16) for width in widths],
        compiler_params=pltpu.CompilerParams(vmem_limit_bytes=VMEM_BYTES * 5),
        cost_estimate=NO_COST,
        name="split_heads",
    )(*own, *arrived, q_gain[None, :], k_gain[None, :], *after)


def head_scores(query, key, head_size):
    product = lax.dot_general(
        query, key, (((1,), (1,)), ((), ())), preferred_element_type=jnp.float32
    )
    return product * (1.0 / math.sqrt(head_size))


def weighted(scores, values, top):
    total, summed = 0.0, 0.0
    for part, value in zip(scores, values):
        weights = jnp.exp(part - top)
        total = total + jnp.sum(weights, axis=-1, keepdims=True)
        summed = summed + jnp.dot(
            weights.astype(jnp.bfloat16), value, preferred_element_type=jnp.float32
        )
    return total, summed


def highest(scores, top=None):
    for part in scores:
        part_top = jnp.max(part, axis=-1, keepdims=True)
        top = part_top if top is None else jnp.maximum(top, part_top)
    return top


def attend_kernel(head_size, count, query_ref, *refs):
    kv_refs, (top_ref, total_ref, summed_ref) = refs[:count], refs[-3:]
    half = query_ref.shape[1]
    for low in range(0, half, head_size):
        here = slice(low, low + head_size)
        scores = [head_scores(query_ref[:, here], ref[:, here], head_size) for ref in kv_refs]
        values = [ref[:, half + low : half + low + head_size] for ref in kv_refs]
        top = highest(scores)
        total, summed = weighted(scores, values, top)
        top_ref[:, here] = jnp.broadcast_to(top, summed.shape)
        total_ref[:, here] = jnp.broadcast_to(total, summed.shape)
        summed_ref[:, here] = summed


def attend(queries, kv_parts, head_size, after):
    whole = lambda array: pl.BlockSpec(array.shape, lambda j: (0, 0))
    state = jax.ShapeDtypeStruct(queries.shape, jnp.float32)
    return pl.pallas_call(
        lambda *refs: attend_kernel(head_size, len(kv_parts), *refs),
        grid=(1,),
        in_specs=[whole(array) for array in [queries, *kv_parts]] + after_specs(after),
        out_specs=[whole(queries)] * 3,
        out_shape=[state] * 3,
        compiler_params=pltpu.CompilerParams(vmem_limit_bytes=VMEM_BYTES * 12),
        cost_estimate=NO_COST,
        name="attend",
    )(queries, *kv_parts, *after)


def finish_kernel(head_size, query_ref, top_ref, total_ref, summed_ref, *refs):
    *refs, out_ref = refs
    half = query_ref.shape[1]
    for low in range(0, half, head_size):
        here = slice(low, low + head_size)
        top, total, summed = top_ref[:, here], total_ref[:, here], summed_ref[:, here]
        if refs:
            own_key, own_value, other_key, other_value, k_gain_ref = refs
            key = head_normal(
                own_key[:, here].astype(jnp.float32) + other_key[:, here].astype(jnp.float32),
                k_gain_ref,
            )
            value = own_value[:, here].astype(jnp.float32) + other_value[:, here].astype(
                jnp.float32
            )
            scores = [head_scores(query_ref[:, here], key, head_size)]
            new_top = jnp.maximum(top, highest(scores))
            more_total, more_summed = weighted(
                scores, [value.astype(jnp.bfloat16)], new_top[:, :1]
            )
            decay = jnp.exp(top - new_top)
            total = total * decay + more_total
            summed = summed * decay + more_summed
        out_ref[:, here] = (summed / total).astype(jnp.bfloat16)


def finished(queries, state, parts, head_size):
    whole = lambda array: pl.BlockSpec(array.shape, lambda j: (0, 0))
    arrays = [queries, *state, *parts]
    return pl.pallas_call(
        lambda *refs: finish_kernel(head_size, *refs),
        grid=(1,),
        in_specs=[whole(array) for array in arrays],
        out_specs=whole(queries),
        out_shape=jax.ShapeDtypeStruct(queries.shape, jnp.bfloat16),
        compiler_params=pltpu.CompilerParams(vmem_limit_bytes=VMEM_BYTES * 12),
        cost_estimate=NO_COST,
        name="finished",
    )(*arrays)


def column_tiles(columns):
    size = columns // 3 if columns % 384 == 0 else columns
    return [slice(low, low + size) for low in range(0, columns, size)]


def out_kernel(own_ref, arrived_ref, weight_ref, *out_refs):
    half = own_ref.shape[1]
    position = lax.axis_index("tensor")
    rows = [pl.ds(pl.multiple_of(at * half, 16), half) for at in (position, 1 - position)]
    for here in column_tiles(weight_ref.shape[1]):
        total = jnp.dot(
            own_ref[...], weight_ref[rows[0], here], preferred_element_type=jnp.float32
        ) + jnp.dot(arrived_ref[...], weight_ref[rows[1], here], preferred_element_type=jnp.float32)
        row_blocks(total, here, out_refs)


def row_blocks(values, columns, out_refs):
    rows = out_refs[0].shape[0]
    for k, out_ref in enumerate(out_refs):
        out_ref[:, columns] = values[k * rows : (k + 1) * rows].astype(jnp.bfloat16)


def out_projected(own, arrived, weight, rows):
    all_rows, half = own.shape
    width = weight.shape[1]
    whole = pl.BlockSpec((all_rows, half), lambda j: (0, 0))
    return pl.pallas_call(
        out_kernel,
        grid=(1,),
        in_specs=[whole, whole, pl.BlockSpec(memory_space=pltpu.VMEM)],
        out_specs=[pl.BlockSpec((rows, width), lambda j: (0, 0))] * (all_rows // rows),
        out_shape=[jax.ShapeDtypeStruct((rows, width), jnp.bfloat16)] * (all_rows // rows),
        compiler_params=pltpu.CompilerParams(vmem_limit_bytes=VMEM_BYTES * 8),
        cost_estimate=NO_COST,
        name="out_projected",
    )(own, arrived, weight)


def up_kernel(first, count, *refs):
    block_refs, weight_ref, (out_ref, joined_ref) = refs[:count], refs[count], refs[-2:]
    rows = block_refs[0].shape[0]
    for k, block_ref in enumerate(block_refs):
        joined_ref[k * rows : (k + 1) * rows, :] = block_ref[...]
    for here in column_tiles(out_ref.shape[1]):
        out_ref[:, here] = jnp.dot(
            joined_ref[...],
            weight_ref[:, first + here.start : first + here.stop],
            preferred_element_type=jnp.float32,
        ).astype(jnp.bfloat16)


def up_projected(blocks, weight, part, parts, after=()):
    rows, width = blocks[0].shape
    all_rows = rows * len(blocks)
    columns = weight.shape[1] // parts
    return pl.pallas_call(
        lambda *refs: up_kernel(part * columns, len(blocks), *refs),
        grid=(1,),
        in_specs=[pl.BlockSpec((rows, width), lambda j: (0, 0)) for _ in blocks]
        + [pl.BlockSpec(memory_space=pltpu.VMEM)]
        + after_specs(after),
        out_specs=pl.BlockSpec((all_rows, columns), lambda j: (0, 0)),
        out_shape=jax.ShapeDtypeStruct((all_rows, columns), jnp.bfloat16),
        scratch_shapes=[pltpu.VMEM((all_rows, width), jnp.bfloat16)],
        compiler_params=pltpu.CompilerParams(vmem_limit_bytes=VMEM_BYTES * 8),
        cost_estimate=pl.CostEstimate(
            flops=2 * all_rows * width * columns, bytes_accessed=0, transcendentals=0
        ),
        name="up_projected",
    )(*blocks, weight, *after)


def down_kernel(first, count, more, own_ref, arrived_ref, weight_ref, *refs):
    *out_refs, activ_ref = refs
    depth = own_ref.shape[1]
    for here in column_tiles(depth):
        hidden = own_ref[:, here].astype(jnp.float32) + arrived_ref[:, here].astype(jnp.float32)
        activ_ref[:, here] = jax.nn.gelu(hidden, approximate=True).astype(jnp.bfloat16)
    for here in column_tiles(weight_ref.shape[1]):
        total = jnp.dot(
            activ_ref[...],
            weight_ref[first : first + depth, here],
            preferred_element_type=jnp.float32,
        )
        if more:
            total = total + out_refs[0][:, here]
        if count:
            row_blocks(total, here, out_refs[-count:])
        else:
            out_refs[0][:, here] = total


def down_projected(own, arrived, weight, first, before, count):
    all_rows, depth = own.shape
    width = weight.shape[1]
    whole = lambda *shape: pl.BlockSpec(shape, lambda j: (0, 0))
    shape, kind = (all_rows // max(count, 1), width), jnp.bfloat16 if count else jnp.float32
    return pl.pallas_call(
        lambda *refs: down_kernel(first, count, len(before), *refs),
        grid=(1,),
        in_specs=[whole(all_rows, depth)] * 2
        + [pl.BlockSpec(memory_space=pltpu.VMEM)]
        + [whole(all_rows, width)] * len(before),
        out_specs=[whole(*shape)] * max(count, 1),
        out_shape=[jax.ShapeDtypeStruct(shape, kind)] * max(count, 1),
        scratch_shapes=[pltpu.VMEM((all_rows, depth), jnp.bfloat16)],
        compiler_params=pltpu.CompilerParams(vmem_limit_bytes=VMEM_BYTES * 12),
        cost_estimate=NO_COST,
        name="down_projected",
    )(own, arrived, weight, *before)


def mix_kernel(count, *refs):
    block_refs, token_ref, gate_ref = refs[:count], refs[count], refs[count + 1]
    mixed_ref, sums_ref = refs[-2:]
    total = block_refs[0][...].astype(jnp.float32)
    for block_ref in block_refs[1:]:
        total = total + block_ref[...].astype(jnp.float32)
    mixed = token_ref[...].astype(jnp.float32) + gate_ref[...] * total
    mixed_ref[...] = mixed
    lane = lax.broadcasted_iota(jnp.int32, sums_ref.shape, 1)
    sums_ref[...] = jnp.where(
        lane < sums_ref.shape[1] // 2,
        jnp.sum(mixed, axis=-1, keepdims=True),
        jnp.sum(mixed * mixed, axis=-1, keepdims=True),
    )


def mixed_rows(blocks, tokens, gate_row, after):
    rows, width = tokens.shape
    whole = lambda *shape: pl.BlockSpec(shape, lambda j: (0, 0))
    return pl.pallas_call(
        lambda *refs: mix_kernel(len(blocks), *refs),
        grid=(1,),
        in_specs=[whole(rows, width)] * (len(blocks) + 1)
        + [whole(1, width)]
        + after_specs(after),
        out_specs=[whole(rows, width), whole(rows, 128)],
        out_shape=[
            jax.ShapeDtypeStruct((rows, width), jnp.float32),
            jax.ShapeDtypeStruct((rows, 128), jnp.float32),
        ],
        compiler_params=pltpu.CompilerParams(vmem_limit_bytes=VMEM_BYTES * 4),
        cost_estimate=NO_COST,
        name="mixed_rows",
    )(*blocks, tokens, gate_row, *after)


def norm_kernel(features, mixed_ref, own_ref, arrived_ref, shift_ref, scale_ref, out_ref):
    total = own_ref[...] + arrived_ref[...]
    average = total[:, :1] / features
    variance = total[:, total.shape[1] // 2 :][:, :1] / features - average * average
    values = (mixed_ref[...] - average) * lax.rsqrt(variance + 1e-06)
    out_ref[...] = (values * (1.0 + scale_ref[...]) + shift_ref[...]).astype(jnp.bfloat16)


def normed_rows(mixed, sums, shift_row, scale_row, features):
    return pl.pallas_call(
        lambda *refs: norm_kernel(features, *refs),
        out_shape=jax.ShapeDtypeStruct(mixed.shape, jnp.bfloat16),
        compiler_params=pltpu.CompilerParams(vmem_limit_bytes=VMEM_BYTES * 2),
        cost_estimate=NO_COST,
        name="normed_rows",
    )(mixed, sums, permuted(sums, "tensor", 1), shift_row, scale_row)


def on_pair(
    tokens, cond, mod_weight, qkv_weight, q_gain, k_gain, out_weight, up_weight, down_weight
):
    stages = [
        (axis, 1 << bit)
        for axis in ("tensor", "blk")
        for bit in range(lax.axis_size(axis).bit_length() - 1)
    ]
    rows, width = tokens.shape
    features = width * lax.axis_size("tensor")
    head_size = q_gain.shape[0]
    half = qkv_weight.shape[2] // 2
    blocks_z = lax.axis_size("blk")

    activated = jax.nn.silu(cond.astype(jnp.float32)).astype(jnp.bfloat16)
    pieces = jnp.dot(activated[None, :], mod_weight, preferred_element_type=jnp.float32)
    weights = pltpu.with_memory_space_constraint(jnp.moveaxis(qkv_weight, 1, 0), pltpu.HBM)
    start = copied(tokens, pieces, NO_COST)
    remote = [permuted(start, "blk", k) for k in range(2, blocks_z, 2)]
    normal = standardized(tokens, features, [])
    parts = []
    for stage in stages:
        after = []
        if stage[0] == "blk":
            take = [1] if stage[1] == 1 else [2]
            parts += [staged(weights, pieces, part) for part in take]
            after = parts + (remote if stage[1] == 2 else [normal])
        pieces = doubled_once(pieces, *stage, after)
    own = packed(normal, pieces)
    parts = [staged(weights, own, 0)] + parts
    chunks = [from_all(own, "ulysses")]
    if remote:
        far = stacked(remote + [permuted(block, "blk", 1) for block in remote], NO_COST)
        far = standardized(far, features, [])
        chunks.append(from_all(far, "ulysses"))
    own_mod = assembled(chunks[0], "ulysses", *pieces.shape, width)
    row = lambda k: own_mod[k : k + 1]
    out_weight, up_weight, down_weight = [
        pltpu.with_memory_space_constraint(weight, pltpu.HBM)
        for weight in (out_weight, up_weight, down_weight)
    ]

    def project(blocks, use, after):
        *partial, normed = projected(blocks, [row(0), row(1)], use, half, True, after)
        arrived = [permuted(part, "tensor", 1) for part in partial]
        return projected([normed], [], use, half, False), arrived

    own, arrived = project(chunks[0], parts, [far] * bool(remote))
    own_kv, queries = split_heads(own, arrived, q_gain, k_gain)
    kv_parts = [own_kv]
    if blocks_z > 1:
        arrived = permuted(own_kv, "blk", 1)
        kv_parts.append(copied(arrived, arrived, LONG))
    out_weight = staged(out_weight, own_kv)
    up_weight = staged(up_weight, out_weight)
    last = []
    first_blocks, last_blocks = halves(chunks[-1])
    if remote:
        own, arrived = project(first_blocks, parts[1:], [own_kv])
        kv_parts += split_heads(own, arrived, q_gain, k_gain)
    state = attend(queries, kv_parts, head_size, [out_weight, up_weight])
    if remote and last_blocks:
        tie = mark([*chunks[-1][1:], state[0]], SHORT)
        own, arrived = project(last_blocks, parts[1:], [state[0], tie])
        last = [*own, *arrived, k_gain[None, :]]
    context = finished(queries, state, last, head_size)

    partial = out_projected(context, permuted(context, "tensor", 1), out_weight, rows)
    down_weight = staged(down_weight, partial[0])
    mixed, sums = mixed_rows(to_all(partial, "ulysses"), tokens, row(2), [down_weight])
    normed_two = normed_rows(mixed, sums, row(3), row(4), features)
    blocks = from_all(normed_two, "ulysses")
    order = halves(list(range(len(blocks))))
    outs = {}
    for part, places in enumerate(order):
        if not places:
            continue
        here = [blocks[k] for k in places]
        here = [stacked(here, LONG)] if part else here
        pieces = 2
        after = [outs[order[0][0]]] if part else []
        ups = [up_projected(here, up_weight, k, pieces, after) for k in range(pieces)]
        arrived = [permuted(piece, "tensor", 1) for piece in ups]
        before = []
        for k, (own, other) in enumerate(zip(ups, arrived)):
            count = len(places) if k == pieces - 1 else 0
            before = down_projected(own, other, down_weight, k * own.shape[1], before, count)
        outs.update(zip(places, before))
    feedforward = added(to_all([outs[k] for k in range(len(blocks))], "ulysses"))
    return mixed + own_mod[5] * feedforward


def halves(items):
    order = items[:1] + items[:0:-1]
    middle = (len(order) + 1) // 2
    return order[:middle], order[middle:]


def solution(mesh):
    sizes = [mesh.shape[axis] for axis in ("ulysses", "blk")]
    pairs = mesh.shape["tensor"] == 2 and all(size & (size - 1) == 0 for size in sizes)
    return jax.shard_map(
        on_pair if pairs else on_device,
        mesh=mesh,
        in_specs=(
            P(("ulysses", "blk"), "tensor"),
            P(),
            P(None, ("ulysses", "blk", "tensor")),
            P("tensor", None, "ulysses"),
            P(),
            P(),
            P("ulysses", "tensor"),
            P("tensor", "ulysses"),
            P("ulysses", "tensor"),
        ),
        out_specs=P(("ulysses", "blk"), "tensor"),
        check_vma=False,
    )
```

```python
import math

import jax
import jax.numpy as jnp
from jax import lax
from jax.experimental import pallas as pl
from jax.experimental.pallas import tpu as pltpu
from jax.sharding import PartitionSpec as P


def joined(array, axis, combine):
    everything = jax.tree.map(
        lambda part, kind: lax.all_gather(part.astype(kind), axis),
        array,
        jax.tree.map(lambda a: jnp.bfloat16 if a.dtype == jnp.float32 else a.dtype, array),
    )

    def take(k):
        return jax.tree.map(lambda part, own: part[k].astype(own.dtype), everything, array)

    return lax.fori_loop(
        1, lax.axis_size(axis), lambda k, so_far: combine(so_far, take(k)), take(0)
    )


def moments_norm(values, shift_row, scale_row, features):
    sums = lax.psum((jnp.sum(values, axis=-1), jnp.sum(values * values, axis=-1)), "tensor")
    average = sums[0][:, None] / features
    variance = sums[1][:, None] / features - average * average
    normal_rows = (values - average) * lax.rsqrt(variance + 1e-06)
    return (normal_rows * (1.0 + scale_row) + shift_row).astype(jnp.bfloat16)


def spread_rows(values):
    return lax.all_gather(values, "ulysses", axis=0, tiled=True)


def head_norm(values, gains):
    return values * lax.rsqrt(jnp.mean(values * values, axis=-1, keepdims=True) + 1e-06) * gains


def make_absorb(queries, score_scale, running, kv_block):
    keys_part, values_part = kv_block
    top_score, total_weight, summed = running
    scores = (
        jnp.einsum("qhd,khd->qhk", queries, keys_part, preferred_element_type=jnp.float32)
        * score_scale
    )
    new_top = jnp.max(scores, axis=-1)
    decay = jnp.exp(top_score - new_top)
    weights = jnp.exp(scores - new_top[..., None])
    total_weight = total_weight * decay + jnp.sum(weights, axis=-1)
    summed = summed * decay[..., None] + jnp.einsum(
        "qhk,khd->qhd",
        weights.astype(jnp.bfloat16),
        values_part,
        preferred_element_type=jnp.float32,
    )
    return (new_top, total_weight, summed)


def empty_state(row_count, heads_local, head_size):
    return (
        jnp.full((row_count, heads_local), -jnp.inf, jnp.float32),
        jnp.zeros((row_count, heads_local), jnp.float32),
        jnp.zeros((row_count, heads_local, head_size), jnp.float32),
    )


def combine_parts(first_part, second_part):
    top_score = jnp.maximum(first_part[0], second_part[0])
    first_decay = jnp.exp(first_part[0] - top_score)
    second_decay = jnp.exp(second_part[0] - top_score)
    total_weight = first_part[1] * first_decay + second_part[1] * second_decay
    summed = first_part[2] * first_decay[..., None] + second_part[2] * second_decay[..., None]
    return (top_score, total_weight, summed)


def on_device(
    tokens, cond, mod_weight, qkv_weight, q_gain, k_gain, out_weight, up_weight, down_weight
):
    tensor_size = lax.axis_size("tensor")
    tensor_pos = lax.axis_index("tensor")
    width = tokens.shape[1]
    features = width * tensor_size
    activated = jax.nn.silu(cond.astype(jnp.float32)).astype(jnp.bfloat16)
    local_mod = jnp.dot(activated[None, :], mod_weight, preferred_element_type=jnp.float32)[0]
    full_mod = lax.all_gather(local_mod, ("ulysses", "blk", "tensor"), axis=0, tiled=True).reshape(
        6, features
    )
    own_mod = lax.dynamic_slice_in_dim(full_mod, tensor_pos * width, width, 1)
    resid = tokens.astype(jnp.float32)
    normed = moments_norm(resid, own_mod[0], own_mod[1], features)
    gathered = spread_rows(normed)
    group_rows = gathered.shape[0]
    attn_rows = group_rows // tensor_size
    inner_local = qkv_weight.shape[2]
    head_size = q_gain.shape[0]
    heads_local = inner_local // head_size
    flat_qkv = qkv_weight.reshape(width, 3 * inner_local)
    projected = (
        lax.psum_scatter(
            jnp.dot(gathered, flat_qkv, preferred_element_type=jnp.float32).astype(jnp.bfloat16),
            "tensor",
            scatter_dimension=0,
            tiled=True,
        )
        .astype(jnp.float32)
        .reshape(attn_rows, 3, heads_local, head_size)
    )
    queries = head_norm(projected[:, 0], q_gain).astype(jnp.bfloat16)
    keys_local = head_norm(projected[:, 1], k_gain).astype(jnp.bfloat16)
    values_local = projected[:, 2].astype(jnp.bfloat16)
    score_scale = 1.0 / math.sqrt(head_size)
    all_queries = lax.all_gather(queries, "tensor", axis=0, tiled=True)
    state = make_absorb(
        all_queries,
        score_scale,
        empty_state(group_rows, heads_local, head_size),
        (
            lax.all_gather(keys_local, "blk", axis=0, tiled=True),
            lax.all_gather(values_local, "blk", axis=0, tiled=True),
        ),
    )
    merged = joined(state, "tensor", combine_parts)
    context = (
        (merged[2] / merged[1][..., None]).astype(jnp.bfloat16).reshape(group_rows, inner_local)
    )
    attended = lax.psum_scatter(
        jnp.dot(context, out_weight, preferred_element_type=jnp.float32).astype(jnp.bfloat16),
        "ulysses",
        scatter_dimension=0,
        tiled=True,
    ).astype(jnp.float32)
    mixed = resid + own_mod[2] * attended
    normed_two = moments_norm(mixed, own_mod[3], own_mod[4], features)
    gathered_two = spread_rows(normed_two)
    hidden = lax.psum_scatter(
        jnp.dot(gathered_two, up_weight, preferred_element_type=jnp.float32).astype(jnp.bfloat16),
        "tensor",
        scatter_dimension=0,
        tiled=True,
    ).astype(jnp.float32)
    activ = jax.nn.gelu(hidden, approximate=True).astype(jnp.bfloat16)
    activ_rows = lax.all_gather(activ, "tensor", axis=0, tiled=True)
    feedforward = lax.psum_scatter(
        jnp.dot(activ_rows, down_weight, preferred_element_type=jnp.float32).astype(jnp.bfloat16),
        "ulysses",
        scatter_dimension=0,
        tiled=True,
    ).astype(jnp.float32)
    return mixed + own_mod[5] * feedforward


VMEM_BYTES = 1024 * 1024
COPY_AT = 1
SHORT = pl.CostEstimate(flops=10**10, bytes_accessed=0, transcendentals=0)
LONG = pl.CostEstimate(flops=10**10, bytes_accessed=0, transcendentals=0)
NO_COST = pl.CostEstimate(flops=0, bytes_accessed=0, transcendentals=0)


def permuted(values, axis, distance):
    size = lax.axis_size(axis)
    return lax.ppermute(values, axis, [(i, i ^ distance) for i in range(size)])


def from_all(values, axis):
    return [values] + [permuted(values, axis, k) for k in range(1, lax.axis_size(axis))]


def to_all(blocks, axis):
    return [blocks[0]] + [permuted(blocks[k], axis, k) for k in range(1, len(blocks))]


def after_specs(after):
    shapes = [(1,) * (dep.ndim - 2) + (min(16, dep.shape[-2]), 128) for dep in after]
    return [pl.BlockSpec(shape, lambda j, n=len(shape): (0,) * n) for shape in shapes]


def merge_kernel(axis, distance, own_ref, other_ref, *refs):
    out_ref = refs[-1]
    rows = own_ref.shape[0]
    upper = (lax.axis_index(axis) & distance) != 0
    out_ref[:rows, :] = jnp.where(upper, other_ref[...], own_ref[...])
    out_ref[rows:, :] = jnp.where(upper, own_ref[...], other_ref[...])


def doubled_once(piece, axis, distance, after):
    other = permuted(piece, axis, distance)
    rows, length = piece.shape
    block = pl.BlockSpec((rows, length), lambda j: (0, 0))
    return pl.pallas_call(
        lambda *refs: merge_kernel(axis, distance, *refs),
        grid=(1,),
        in_specs=[block, block] + after_specs(after),
        out_specs=pl.BlockSpec((2 * rows, length), lambda j: (0, 0)),
        out_shape=jax.ShapeDtypeStruct((2 * rows, length), piece.dtype),
        compiler_params=pltpu.CompilerParams(vmem_limit_bytes=VMEM_BYTES),
        cost_estimate=NO_COST,
        name="merged",
    )(piece, other, *after)


def lane_tiles(rows, count, length):
    return -(-(-(-length // 128)) // (rows // count))


def pack_kernel(values_ref, pieces_ref, out_ref):
    rows, width = values_ref.shape
    count, length = pieces_ref.shape
    per = rows // count
    out_ref[:, :width] = values_ref[...]
    for tile in range((out_ref.shape[1] - width) // 128):
        lines = []
        for row in range(count):
            for low in range(tile * per * 128, (tile + 1) * per * 128, 128):
                size = max(0, min(128, length - low))
                line = jnp.zeros((1, 128 - size), jnp.float32)
                if size:
                    part = pieces_ref[row : row + 1, low : low + size]
                    line = jnp.concatenate([part, line], axis=1) if size < 128 else part
                lines.append(line)
        columns = slice(width + tile * 128, width + (tile + 1) * 128)
        out_ref[:, columns] = jnp.concatenate(lines, axis=0).astype(jnp.bfloat16)


def packed(values, pieces):
    rows, width = values.shape
    columns = width + 128 * lane_tiles(rows, *pieces.shape)
    return pl.pallas_call(
        pack_kernel,
        out_shape=jax.ShapeDtypeStruct((rows, columns), jnp.bfloat16),
        compiler_params=pltpu.CompilerParams(vmem_limit_bytes=VMEM_BYTES * 2),
        cost_estimate=NO_COST,
        name="packed",
    )(values, pieces)


def assemble_kernel(axis, count, length, *refs):
    *tile_refs, out_ref, pieces_ref = refs
    position = lax.axis_index(axis)
    tiles = [ref[...].astype(jnp.float32) for ref in tile_refs]
    bit = 1
    while bit < len(tiles):
        flip = (position & bit) != 0
        tiles = [jnp.where(flip, tiles[i ^ bit], tiles[i]) for i in range(len(tiles))]
        bit *= 2
    per = tiles[0].shape[0] // count
    for block, tile in enumerate(tiles):
        for row in range(count):
            for low in range(0, length, 128):
                line = row * per + low // 128 % per
                columns = low // 128 // per * 128
                size = min(128, length - low)
                pieces_ref[block * count + row : block * count + row + 1, low : low + size] = tile[
                    line : line + 1, columns : columns + size
                ]
    width = out_ref.shape[1]
    vectors = out_ref.shape[0]
    halves = len(tiles) * count * length // (vectors * width)
    for half in range(halves):

        @pl.when(lax.axis_index("tensor") == half)
        def _(half=half):
            for vector in range(vectors):
                at = (vector * halves + half) * width
                end = at + width
                parts = []
                while at < end:
                    row, low = divmod(at, length)
                    high = min(length, low + end - at)
                    parts.append(pieces_ref[row : row + 1, low:high])
                    at += high - low
                out_ref[vector : vector + 1, :] = jnp.concatenate(parts, axis=1)


def assembled(blocks, axis, count, length, width):
    rows, columns = blocks[0].shape
    extra = columns - width
    return pl.pallas_call(
        lambda *refs: assemble_kernel(axis, count, length, *refs),
        grid=(1,),
        in_specs=[pl.BlockSpec((rows, extra), lambda j: (0, width // extra)) for _ in blocks],
        out_specs=pl.BlockSpec((6, width), lambda j: (0, 0)),
        out_shape=jax.ShapeDtypeStruct((6, width), jnp.float32),
        scratch_shapes=[pltpu.VMEM((len(blocks) * count, -(-length // 128) * 128), jnp.float32)],
        compiler_params=pltpu.CompilerParams(vmem_limit_bytes=VMEM_BYTES),
        cost_estimate=NO_COST,
        name="assembled",
    )(*blocks)


def row_sums_kernel(values_ref, out_ref, copy_ref):
    values = values_ref[...].astype(jnp.float32)
    lane = lax.broadcasted_iota(jnp.int32, out_ref.shape, 1)
    out_ref[...] = jnp.where(
        lane < out_ref.shape[1] // 2,
        jnp.sum(values, axis=-1, keepdims=True),
        jnp.sum(values * values, axis=-1, keepdims=True),
    )
    copy_ref[...] = values_ref[...]


def row_sums(values):
    return pl.pallas_call(
        row_sums_kernel,
        out_shape=[
            jax.ShapeDtypeStruct((values.shape[0], 128), jnp.float32),
            jax.ShapeDtypeStruct(values.shape, values.dtype),
        ],
        compiler_params=pltpu.CompilerParams(vmem_limit_bytes=VMEM_BYTES * 2),
        cost_estimate=NO_COST,
        name="row_sums",
    )(values)


def standardize_kernel(features, values_ref, own_ref, arrived_ref, *refs):
    total = own_ref[...] + arrived_ref[...]
    average = total[:, :1] / features
    variance = total[:, total.shape[1] // 2 :][:, :1] / features - average * average
    values = values_ref[...].astype(jnp.float32)
    refs[-1][...] = ((values - average) * lax.rsqrt(variance + 1e-06)).astype(jnp.bfloat16)


def standardized(values, features, after):
    own, values = row_sums(values)
    whole = lambda array: pl.BlockSpec(array.shape, lambda j: (0, 0))
    return pl.pallas_call(
        lambda *refs: standardize_kernel(features, *refs),
        grid=(1,),
        in_specs=[whole(values), whole(own), whole(own)] + after_specs(after),
        out_specs=whole(values),
        out_shape=jax.ShapeDtypeStruct(values.shape, jnp.bfloat16),
        compiler_params=pltpu.CompilerParams(vmem_limit_bytes=VMEM_BYTES * 2),
        cost_estimate=NO_COST,
        name="standardized",
    )(values, own, permuted(own, "tensor", 1), *after)


def stack_kernel(*refs):
    *block_refs, out_ref = refs
    rows = block_refs[0].shape[0]
    for k, block_ref in enumerate(block_refs):
        out_ref[k * rows : (k + 1) * rows, :] = block_ref[...]


def stacked(blocks, cost):
    rows, width = blocks[0].shape
    return pl.pallas_call(
        stack_kernel,
        out_shape=jax.ShapeDtypeStruct((rows * len(blocks), width), blocks[0].dtype),
        compiler_params=pltpu.CompilerParams(vmem_limit_bytes=VMEM_BYTES * 2),
        cost_estimate=cost,
        name="stacked",
    )(*blocks)


def copied_kernel(values_ref, after_ref, out_ref):
    out_ref[...] = values_ref[...]


def copied(values, after, cost):
    whole = pl.BlockSpec(values.shape, lambda j: (0, 0))
    return pl.pallas_call(
        copied_kernel,
        grid=(1,),
        in_specs=[whole] + after_specs([after]),
        out_specs=whole,
        out_shape=jax.ShapeDtypeStruct(values.shape, values.dtype),
        compiler_params=pltpu.CompilerParams(vmem_limit_bytes=VMEM_BYTES * 2),
        cost_estimate=cost,
        name="copied",
    )(values, after)


def added(blocks):
    total = blocks[0].astype(jnp.float32)
    for block in blocks[1:]:
        total = total + block.astype(jnp.float32)
    return total


def project_kernel(count, parts, other, *refs):
    block_refs = refs[:count]
    shift_ref, scale_ref = refs[count : count + 2]
    weight_refs = refs[count + 2 : count + 2 + parts]
    normed_ref = refs[-1]
    rows = block_refs[0].shape[0]
    for k, block_ref in enumerate(block_refs):
        values = block_ref[...].astype(jnp.float32)
        values = values * (1.0 + scale_ref[...]) + shift_ref[...]
        normed_ref[k * rows : (k + 1) * rows, :] = values.astype(jnp.bfloat16)
    project_parts(normed_ref, weight_refs, refs[-1 - parts : -1], other)


def project_parts(normed_ref, weight_refs, out_refs, other):
    half = out_refs[0].shape[1]
    position = lax.axis_index("tensor")
    low = pl.multiple_of((1 - position if other else position) * half, 128)
    for weight_ref, out_ref in zip(weight_refs, out_refs):
        out_ref[...] = jnp.dot(
            normed_ref[...], weight_ref[:, pl.ds(low, half)], preferred_element_type=jnp.float32
        ).astype(jnp.bfloat16)


def project_again_kernel(parts, other, normed_ref, *refs):
    project_parts(normed_ref, refs[:parts], refs[-parts:], other)


def projected(blocks, small, weights, half, other, after=()):
    rows, width = blocks[0].shape[0], weights[0].shape[0]
    all_rows = rows * len(blocks)
    count = len(weights)
    whole = lambda shape: pl.BlockSpec(shape, lambda j: (0, 0))
    shapes = [(all_rows, half)] * count + [(all_rows, width)] * bool(small)
    return pl.pallas_call(
        (lambda *refs: project_kernel(len(blocks), count, other, *refs))
        if small
        else (lambda *refs: project_again_kernel(count, other, *refs)),
        grid=(1,),
        in_specs=[whole((rows, width)) for _ in blocks]
        + [whole(array.shape) for array in small]
        + [pl.BlockSpec(memory_space=pltpu.VMEM) for _ in weights]
        + after_specs(after),
        out_specs=[whole(shape) for shape in shapes],
        out_shape=[jax.ShapeDtypeStruct(shape, jnp.bfloat16) for shape in shapes],
        compiler_params=pltpu.CompilerParams(vmem_limit_bytes=VMEM_BYTES * 20),
        cost_estimate=NO_COST,
        name="projected",
    )(*blocks, *small, *weights, *after)


def staged(weights, after, part=None):
    width, columns = weights.shape[-2:]
    pieces = 4 if width % 64 == 0 else 1
    rows = width // pieces
    anywhere = pl.BlockSpec(memory_space=pl.ANY)

    def kernel(weight_ref, after_ref, out_ref, sems):
        source_ref = weight_ref if part is None else weight_ref.at[part]
        copies = [
            pltpu.make_async_copy(
                source_ref.at[pl.ds(k * rows, rows)], out_ref.at[pl.ds(k * rows, rows)], sems.at[k]
            )
            for k in range(pieces)
        ]
        for copy in copies:
            copy.start()
        for copy in copies:
            copy.wait()

    return pl.pallas_call(
        kernel,
        grid=(1,),
        in_specs=[anywhere] + after_specs([after]),
        out_specs=pl.BlockSpec(memory_space=pltpu.VMEM),
        out_shape=pltpu.VMEM((width, columns), weights.dtype),
        scratch_shapes=[pltpu.SemaphoreType.DMA((pieces,))],
        compiler_params=pltpu.CompilerParams(vmem_limit_bytes=VMEM_BYTES),
        cost_estimate=pl.CostEstimate(
            flops=0, bytes_accessed=2 * width * columns, transcendentals=0
        ),
        name="staged",
    )(weights, after)


def mark_kernel(*refs):
    refs[-1][...] = jnp.zeros(refs[-1].shape, jnp.float32)


def mark(after, cost):
    return pl.pallas_call(
        mark_kernel,
        grid=(1,),
        in_specs=after_specs(after),
        out_specs=pl.BlockSpec((8, 128), lambda j: (0, 0)),
        out_shape=jax.ShapeDtypeStruct((8, 128), jnp.float32),
        compiler_params=pltpu.CompilerParams(vmem_limit_bytes=VMEM_BYTES),
        cost_estimate=cost,
        name="mark",
    )(*after)


def head_normal(values, gain_ref):
    spread = jnp.mean(values * values, axis=-1, keepdims=True) + 1e-06
    return (values * lax.rsqrt(spread) * gain_ref[...]).astype(jnp.bfloat16)


def heads_kernel(count, head_size, *refs):
    own_refs, arrived_refs = refs[:count], refs[count : 2 * count]
    q_gain_ref, k_gain_ref = refs[2 * count : 2 * count + 2]
    out_refs = refs[-1:] if count == 2 else refs[-2:]
    half = own_refs[0].shape[1]

    def total(part, here):
        return own_refs[part][:, here].astype(jnp.float32) + arrived_refs[part][:, here].astype(
            jnp.float32
        )

    for low in range(0, half, head_size):
        here = slice(low, low + head_size)
        if count == 3:
            out_refs[1][:, here] = head_normal(total(0, here), q_gain_ref)
        out_refs[0][:, here] = head_normal(total(count - 2, here), k_gain_ref)
        out_refs[0][:, half + low : half + low + head_size] = total(count - 1, here).astype(
            jnp.bfloat16
        )


def split_heads(own, arrived, q_gain, k_gain, after=()):
    count = len(own)
    rows, half = own[0].shape
    head_size = q_gain.shape[0]
    widths = [2 * half] if count == 2 else [2 * half, half]
    whole = lambda *shape: pl.BlockSpec(shape, lambda j: (0, 0))
    return pl.pallas_call(
        lambda *refs: heads_kernel(count, head_size, *refs),
        grid=(1,),
        in_specs=[whole(rows, half)] * (2 * count)
        + [whole(1, head_size)] * 2
        + after_specs(after),
        out_specs=[whole(rows, width) for width in widths],
        out_shape=[jax.ShapeDtypeStruct((rows, width), jnp.bfloat16) for width in widths],
        compiler_params=pltpu.CompilerParams(vmem_limit_bytes=VMEM_BYTES * 5),
        cost_estimate=NO_COST,
        name="split_heads",
    )(*own, *arrived, q_gain[None, :], k_gain[None, :], *after)


def head_scores(query, key, head_size):
    product = lax.dot_general(
        query, key, (((1,), (1,)), ((), ())), preferred_element_type=jnp.float32
    )
    return product * (1.0 / math.sqrt(head_size))


def weighted(scores, values, top):
    total, summed = 0.0, 0.0
    for part, value in zip(scores, values):
        weights = jnp.exp(part - top)
        total = total + jnp.sum(weights, axis=-1, keepdims=True)
        summed = summed + jnp.dot(
            weights.astype(jnp.bfloat16), value, preferred_element_type=jnp.float32
        )
    return total, summed


def highest(scores, top=None):
    for part in scores:
        part_top = jnp.max(part, axis=-1, keepdims=True)
        top = part_top if top is None else jnp.maximum(top, part_top)
    return top


def attend_kernel(head_size, count, query_ref, *refs):
    kv_refs, (top_ref, total_ref, summed_ref) = refs[:count], refs[-3:]
    half = query_ref.shape[1]
    places = [slice(low, low + head_size) for low in range(0, half, head_size)]
    scores = [
        [head_scores(query_ref[:, here], ref[:, here], head_size) for ref in kv_refs]
        for here in places
    ]
    tops = [highest(parts) for parts in scores]
    for here, parts, top in zip(places, scores, tops):
        values = [ref[:, half + here.start : half + here.stop] for ref in kv_refs]
        total, summed = weighted(parts, values, top)
        top_ref[:, here] = jnp.broadcast_to(top, summed.shape)
        total_ref[:, here] = jnp.broadcast_to(total, summed.shape)
        summed_ref[:, here] = summed


def attend(queries, kv_parts, head_size, after):
    whole = lambda array: pl.BlockSpec(array.shape, lambda j: (0, 0))
    state = jax.ShapeDtypeStruct(queries.shape, jnp.float32)
    return pl.pallas_call(
        lambda *refs: attend_kernel(head_size, len(kv_parts), *refs),
        grid=(1,),
        in_specs=[whole(array) for array in [queries, *kv_parts]] + after_specs(after),
        out_specs=[whole(queries)] * 3,
        out_shape=[state] * 3,
        compiler_params=pltpu.CompilerParams(vmem_limit_bytes=VMEM_BYTES * 12),
        cost_estimate=NO_COST,
        name="attend",
    )(queries, *kv_parts, *after)


def finish_kernel(head_size, count, query_ref, top_ref, total_ref, summed_ref, *refs):
    kv_refs, out_ref = refs[:count], refs[-1]
    half = query_ref.shape[1]
    places = [slice(low, low + head_size) for low in range(0, half, head_size)]
    tops = [top_ref[:, here] for here in places]
    totals = [total_ref[:, here] for here in places]
    sums = [summed_ref[:, here] for here in places]
    if kv_refs:
        keys = [kv_refs[0][:, here] for here in places]
        values = [kv_refs[0][:, half + here.start : half + here.stop] for here in places]
        scores = [
            head_scores(query_ref[:, here], key, head_size) for here, key in zip(places, keys)
        ]
        new_tops = [jnp.maximum(top, highest([part])) for top, part in zip(tops, scores)]
        decays = [jnp.exp(top - new_top) for top, new_top in zip(tops, new_tops)]
        weights = [jnp.exp(part - new_top[:, :1]) for part, new_top in zip(scores, new_tops)]
        products = [
            jnp.dot(part.astype(jnp.bfloat16), value, preferred_element_type=jnp.float32)
            for part, value in zip(weights, values)
        ]
        totals = [
            total * decay + jnp.sum(part, axis=-1, keepdims=True)
            for total, decay, part in zip(totals, decays, weights)
        ]
        sums = [part * decay + more for part, decay, more in zip(sums, decays, products)]
    for here, total, part in zip(places, totals, sums):
        out_ref[:, here] = (part / total).astype(jnp.bfloat16)


def finished(queries, state, parts, head_size, first, count, after=()):
    whole = lambda array: pl.BlockSpec(array.shape, lambda j: (0, 0))
    some = pl.BlockSpec((count, queries.shape[1]), lambda j: (first // count, 0))
    return pl.pallas_call(
        lambda *refs: finish_kernel(head_size, len(parts), *refs),
        grid=(1,),
        in_specs=[some] * 4 + [whole(array) for array in parts] + after_specs(after),
        out_specs=pl.BlockSpec((count, queries.shape[1]), lambda j: (0, 0)),
        out_shape=jax.ShapeDtypeStruct((count, queries.shape[1]), jnp.bfloat16),
        compiler_params=pltpu.CompilerParams(vmem_limit_bytes=VMEM_BYTES * 12),
        cost_estimate=NO_COST,
        name="finished",
    )(queries, *state, *parts, *after)


def column_tiles(columns):
    size = columns // 3 if columns % 384 == 0 else columns
    return [slice(low, low + size) for low in range(0, columns, size)]


def out_kernel(count, own_ref, arrived_ref, weight_ref, *refs):
    out_refs = refs[-count:]
    half = own_ref.shape[1]
    position = lax.axis_index("tensor")
    rows = [pl.ds(pl.multiple_of(at * half, 16), half) for at in (position, 1 - position)]
    for here in column_tiles(weight_ref.shape[1]):
        total = jnp.dot(
            own_ref[...], weight_ref[rows[0], here], preferred_element_type=jnp.float32
        ) + jnp.dot(arrived_ref[...], weight_ref[rows[1], here], preferred_element_type=jnp.float32)
        row_blocks(total, here, out_refs)


def row_blocks(values, columns, out_refs):
    rows = out_refs[0].shape[0]
    for k, out_ref in enumerate(out_refs):
        out_ref[:, columns] = values[k * rows : (k + 1) * rows].astype(jnp.bfloat16)


def out_projected(own, arrived, weight, rows, after):
    all_rows, half = own.shape
    width = weight.shape[1]
    whole = pl.BlockSpec((all_rows, half), lambda j: (0, 0))
    return pl.pallas_call(
        lambda *refs: out_kernel(all_rows // rows, *refs),
        grid=(1,),
        in_specs=[whole, whole, pl.BlockSpec(memory_space=pltpu.VMEM)] + after_specs(after),
        out_specs=[pl.BlockSpec((rows, width), lambda j: (0, 0))] * (all_rows // rows),
        out_shape=[jax.ShapeDtypeStruct((rows, width), jnp.bfloat16)] * (all_rows // rows),
        compiler_params=pltpu.CompilerParams(vmem_limit_bytes=VMEM_BYTES * 8),
        cost_estimate=NO_COST,
        name="out_projected",
    )(own, arrived, weight, *after)


def up_kernel(first, count, *refs):
    block_refs, weight_ref, (out_ref, joined_ref) = refs[:count], refs[count], refs[-2:]
    rows = block_refs[0].shape[0]
    for k, block_ref in enumerate(block_refs):
        joined_ref[k * rows : (k + 1) * rows, :] = block_ref[...]
    for here in column_tiles(out_ref.shape[1]):
        out_ref[:, here] = jnp.dot(
            joined_ref[...],
            weight_ref[:, first + here.start : first + here.stop],
            preferred_element_type=jnp.float32,
        ).astype(jnp.bfloat16)


def up_projected(blocks, weight, part, parts, after=()):
    rows, width = blocks[0].shape
    all_rows = rows * len(blocks)
    columns = weight.shape[1] // parts
    return pl.pallas_call(
        lambda *refs: up_kernel(part * columns, len(blocks), *refs),
        grid=(1,),
        in_specs=[pl.BlockSpec((rows, width), lambda j: (0, 0)) for _ in blocks]
        + [pl.BlockSpec(memory_space=pltpu.VMEM)]
        + after_specs(after),
        out_specs=pl.BlockSpec((all_rows, columns), lambda j: (0, 0)),
        out_shape=jax.ShapeDtypeStruct((all_rows, columns), jnp.bfloat16),
        scratch_shapes=[pltpu.VMEM((all_rows, width), jnp.bfloat16)],
        compiler_params=pltpu.CompilerParams(vmem_limit_bytes=VMEM_BYTES * 8),
        cost_estimate=pl.CostEstimate(
            flops=2 * all_rows * width * columns, bytes_accessed=0, transcendentals=0
        ),
        name="up_projected",
    )(*blocks, weight, *after)


def down_kernel(first, count, more, own_ref, arrived_ref, weight_ref, *refs):
    *out_refs, activ_ref = refs
    depth = own_ref.shape[1]
    for here in column_tiles(depth):
        hidden = own_ref[:, here].astype(jnp.float32) + arrived_ref[:, here].astype(jnp.float32)
        activ_ref[:, here] = jax.nn.gelu(hidden, approximate=True).astype(jnp.bfloat16)
    for here in column_tiles(weight_ref.shape[1]):
        total = jnp.dot(
            activ_ref[...],
            weight_ref[first : first + depth, here],
            preferred_element_type=jnp.float32,
        )
        if more:
            total = total + out_refs[0][:, here]
        if count:
            row_blocks(total, here, out_refs[-count:])
        else:
            out_refs[0][:, here] = total


def down_projected(own, arrived, weight, first, before, count):
    all_rows, depth = own.shape
    width = weight.shape[1]
    whole = lambda *shape: pl.BlockSpec(shape, lambda j: (0, 0))
    shape, kind = (all_rows // max(count, 1), width), jnp.bfloat16 if count else jnp.float32
    return pl.pallas_call(
        lambda *refs: down_kernel(first, count, len(before), *refs),
        grid=(1,),
        in_specs=[whole(all_rows, depth)] * 2
        + [pl.BlockSpec(memory_space=pltpu.VMEM)]
        + [whole(all_rows, width)] * len(before),
        out_specs=[whole(*shape)] * max(count, 1),
        out_shape=[jax.ShapeDtypeStruct(shape, kind)] * max(count, 1),
        scratch_shapes=[pltpu.VMEM((all_rows, depth), jnp.bfloat16)],
        compiler_params=pltpu.CompilerParams(vmem_limit_bytes=VMEM_BYTES * 12),
        cost_estimate=NO_COST,
        name="down_projected",
    )(own, arrived, weight, *before)


def add_kernel(first_ref, second_ref, out_ref):
    total = first_ref[...].astype(jnp.float32) + second_ref[...].astype(jnp.float32)
    out_ref[...] = total.astype(jnp.bfloat16)


def rounded_sum(first, second):
    return pl.pallas_call(
        add_kernel,
        out_shape=jax.ShapeDtypeStruct(first.shape, first.dtype),
        compiler_params=pltpu.CompilerParams(vmem_limit_bytes=VMEM_BYTES * 2),
        cost_estimate=NO_COST,
        name="rounded_sum",
    )(first, second)


def row_groups(blocks, axis):
    groups = len(blocks) // lax.axis_size(axis)
    pieces = [blocks[k : k + groups] for k in range(0, len(blocks), groups)]
    if groups != 2 or len(pieces) != 4:
        return [to_all([piece[k] for piece in pieces], axis) for k in range(groups)]
    own, first, second, far = pieces
    low, high = permuted(far[0], axis, 1), permuted(far[1], axis, 2)
    first_low, second_high = permuted(first[0], axis, 1), permuted(second[1], axis, 2)
    second_low = permuted(rounded_sum(second[0], low), axis, 2)
    first_high = permuted(rounded_sum(first[1], high), axis, 1)
    return [[own[0], first_low, second_low], [own[1], first_high, second_high]]


def mix_kernel(counts, *refs):
    token_ref, gate_ref = refs[sum(counts)], refs[sum(counts) + 1]
    mixed_ref, sums_ref = refs[-2:]
    rows = refs[0].shape[0]
    lane = lax.broadcasted_iota(jnp.int32, (rows, sums_ref.shape[1]), 1)
    at = 0
    for group, count in enumerate(counts):
        here = slice(group * rows, (group + 1) * rows)
        total = refs[at][...].astype(jnp.float32)
        for block_ref in refs[at + 1 : at + count]:
            total = total + block_ref[...].astype(jnp.float32)
        at += count
        mixed = token_ref[here, :].astype(jnp.float32) + gate_ref[...] * total
        mixed_ref[here, :] = mixed
        sums_ref[here, :] = jnp.where(
            lane < sums_ref.shape[1] // 2,
            jnp.sum(mixed, axis=-1, keepdims=True),
            jnp.sum(mixed * mixed, axis=-1, keepdims=True),
        )


def mixed_rows(groups, tokens, gate_row, after):
    rows, width = tokens.shape
    whole = lambda *shape: pl.BlockSpec(shape, lambda j: (0, 0))
    blocks = [block for group in groups for block in group]
    return pl.pallas_call(
        lambda *refs: mix_kernel([len(group) for group in groups], *refs),
        grid=(1,),
        in_specs=[whole(*block.shape) for block in blocks]
        + [whole(rows, width), whole(1, width)]
        + after_specs(after),
        out_specs=[whole(rows, width), whole(rows, 128)],
        out_shape=[
            jax.ShapeDtypeStruct((rows, width), jnp.float32),
            jax.ShapeDtypeStruct((rows, 128), jnp.float32),
        ],
        compiler_params=pltpu.CompilerParams(vmem_limit_bytes=VMEM_BYTES * 4),
        cost_estimate=NO_COST,
        name="mixed_rows",
    )(*blocks, tokens, gate_row, *after)


def norm_kernel(features, mixed_ref, own_ref, arrived_ref, shift_ref, scale_ref, out_ref):
    total = own_ref[...] + arrived_ref[...]
    average = total[:, :1] / features
    variance = total[:, total.shape[1] // 2 :][:, :1] / features - average * average
    values = (mixed_ref[...] - average) * lax.rsqrt(variance + 1e-06)
    out_ref[...] = (values * (1.0 + scale_ref[...]) + shift_ref[...]).astype(jnp.bfloat16)


def normed_rows(mixed, sums, shift_row, scale_row, features):
    return pl.pallas_call(
        lambda *refs: norm_kernel(features, *refs),
        out_shape=jax.ShapeDtypeStruct(mixed.shape, jnp.bfloat16),
        compiler_params=pltpu.CompilerParams(vmem_limit_bytes=VMEM_BYTES * 2),
        cost_estimate=NO_COST,
        name="normed_rows",
    )(mixed, sums, permuted(sums, "tensor", 1), shift_row, scale_row)


def on_pair(
    tokens, cond, mod_weight, qkv_weight, q_gain, k_gain, out_weight, up_weight, down_weight
):
    stages = [
        (axis, 1 << bit)
        for axis in ("tensor", "blk")
        for bit in range(lax.axis_size(axis).bit_length() - 1)
    ]
    rows, width = tokens.shape
    features = width * lax.axis_size("tensor")
    head_size = q_gain.shape[0]
    half = qkv_weight.shape[2] // 2
    blocks_z = lax.axis_size("blk")

    activated = jax.nn.silu(cond.astype(jnp.float32)).astype(jnp.bfloat16)
    pieces = jnp.dot(activated[None, :], mod_weight, preferred_element_type=jnp.float32)
    weights = pltpu.with_memory_space_constraint(jnp.moveaxis(qkv_weight, 1, 0), pltpu.HBM)
    start = copied(tokens, pieces, NO_COST)
    remote = [permuted(start, "blk", k) for k in range(2, blocks_z, 2)]
    normal = standardized(tokens, features, [])
    parts = []
    for stage in stages:
        after = []
        if stage[0] == "blk":
            take = [1] if stage[1] == 1 else [2]
            parts += [staged(weights, pieces, part) for part in take]
            after = parts + (remote if stage[1] == 2 else [normal])
        pieces = doubled_once(pieces, *stage, after)
    own = packed(normal, pieces)
    parts = [staged(weights, own, 0)] + parts
    chunks = [from_all(own, "ulysses")]
    if remote:
        far = stacked(remote + [permuted(block, "blk", 1) for block in remote], NO_COST)
        far = standardized(far, features, [])
        chunks.append(from_all(far, "ulysses"))
    own_mod = assembled(chunks[0], "ulysses", *pieces.shape, width)
    row = lambda k: own_mod[k : k + 1]
    out_weight, up_weight, down_weight = [
        pltpu.with_memory_space_constraint(weight, pltpu.HBM)
        for weight in (out_weight, up_weight, down_weight)
    ]

    def project(blocks, use, after):
        *partial, normed = projected(blocks, [row(0), row(1)], use, half, True, after)
        arrived = [permuted(part, "tensor", 1) for part in partial]
        return projected([normed], [], use, half, False), arrived

    own, arrived = project(chunks[0], parts, [far] * bool(remote))
    own_kv, queries = split_heads(own, arrived, q_gain, k_gain)
    kv_parts = [own_kv]
    if blocks_z > 1:
        arrived = permuted(own_kv, "blk", 1)
        kv_parts.append(copied(arrived, arrived, LONG))
    out_weight = staged(out_weight, own_kv)
    up_weight = staged(up_weight, out_weight)
    last = []
    first_blocks, last_blocks = halves(chunks[-1])
    if remote:
        own, arrived = project(first_blocks, parts[1:], [own_kv])
        kv_parts += split_heads(own, arrived, q_gain, k_gain)
    state = attend(queries, kv_parts, head_size, [out_weight, up_weight])
    if remote and last_blocks:
        tie = mark([*chunks[-1][1:], state[0]], SHORT)
        own, arrived = project(last_blocks, parts[1:], [state[0], tie])
        last = split_heads(own, arrived, q_gain, k_gain)
    all_rows = queries.shape[0]
    last_rows = rows if all_rows > rows else 0
    partial, arrived = [], []
    if last_rows:
        context = finished(queries, state, last, head_size, all_rows - rows, rows)
        arrived.append((context, permuted(context, "tensor", 1)))
    after = [own for own, _ in arrived]
    context = finished(queries, state, last, head_size, 0, all_rows - last_rows, after)
    other = permuted(context, "tensor", 1)
    arrived.append((context, other))
    for own, other in arrived:
        after = [] if own is context else [context]
        partial = list(out_projected(own, other, out_weight, rows // 2, after)) + partial
    summed = row_groups(partial, "ulysses")
    mixed, sums = mixed_rows(summed, tokens, row(2), [])
    normed_two = normed_rows(mixed, sums, row(3), row(4), features)
    blocks = from_all(normed_two, "ulysses")
    down_weight = staged(down_weight, normed_two)
    order = halves(list(range(len(blocks))))
    outs = {}
    for part, places in enumerate(order):
        if not places:
            continue
        here = [blocks[k] for k in places]
        here = [stacked(here, LONG)] if part else here
        pieces = 2
        after = [outs[order[0][0]]] if part else [down_weight]
        ups = [up_projected(here, up_weight, k, pieces, after) for k in range(pieces)]
        arrived = [permuted(piece, "tensor", 1) for piece in ups]
        before = []
        for k, (own, other) in enumerate(zip(ups, arrived)):
            count = len(places) if k == pieces - 1 else 0
            before = down_projected(own, other, down_weight, k * own.shape[1], before, count)
        outs.update(zip(places, before))
    feedforward = added(to_all([outs[k] for k in range(len(blocks))], "ulysses"))
    return mixed + own_mod[5] * feedforward


def halves(items):
    order = items[:1] + items[:0:-1]
    middle = (len(order) + 1) // 2
    return order[:middle], order[middle:]


def solution(mesh):
    sizes = [mesh.shape[axis] for axis in ("ulysses", "blk")]
    pairs = mesh.shape["tensor"] == 2 and all(size & (size - 1) == 0 for size in sizes)
    return jax.shard_map(
        on_pair if pairs else on_device,
        mesh=mesh,
        in_specs=(
            P(("ulysses", "blk"), "tensor"),
            P(),
            P(None, ("ulysses", "blk", "tensor")),
            P("tensor", None, "ulysses"),
            P(),
            P(),
            P("ulysses", "tensor"),
            P("tensor", "ulysses"),
            P("ulysses", "tensor"),
        ),
        out_specs=P(("ulysses", "blk"), "tensor"),
        check_vma=False,
    )
```

```python
import math

import jax
import jax.numpy as jnp
from jax import lax
from jax.experimental import pallas as pl
from jax.experimental.pallas import tpu as pltpu
from jax.sharding import PartitionSpec as P


def joined(array, axis, combine):
    everything = jax.tree.map(
        lambda part, kind: lax.all_gather(part.astype(kind), axis),
        array,
        jax.tree.map(lambda a: jnp.bfloat16 if a.dtype == jnp.float32 else a.dtype, array),
    )

    def take(k):
        return jax.tree.map(lambda part, own: part[k].astype(own.dtype), everything, array)

    return lax.fori_loop(
        1, lax.axis_size(axis), lambda k, so_far: combine(so_far, take(k)), take(0)
    )


def moments_norm(values, shift_row, scale_row, features):
    sums = lax.psum((jnp.sum(values, axis=-1), jnp.sum(values * values, axis=-1)), "tensor")
    average = sums[0][:, None] / features
    variance = sums[1][:, None] / features - average * average
    normal_rows = (values - average) * lax.rsqrt(variance + 1e-06)
    return (normal_rows * (1.0 + scale_row) + shift_row).astype(jnp.bfloat16)


def spread_rows(values):
    return lax.all_gather(values, "ulysses", axis=0, tiled=True)


def head_norm(values, gains):
    return values * lax.rsqrt(jnp.mean(values * values, axis=-1, keepdims=True) + 1e-06) * gains


def make_absorb(queries, score_scale, running, kv_block):
    keys_part, values_part = kv_block
    top_score, total_weight, summed = running
    scores = (
        jnp.einsum("qhd,khd->qhk", queries, keys_part, preferred_element_type=jnp.float32)
        * score_scale
    )
    new_top = jnp.max(scores, axis=-1)
    decay = jnp.exp(top_score - new_top)
    weights = jnp.exp(scores - new_top[..., None])
    total_weight = total_weight * decay + jnp.sum(weights, axis=-1)
    summed = summed * decay[..., None] + jnp.einsum(
        "qhk,khd->qhd",
        weights.astype(jnp.bfloat16),
        values_part,
        preferred_element_type=jnp.float32,
    )
    return (new_top, total_weight, summed)


def empty_state(row_count, heads_local, head_size):
    return (
        jnp.full((row_count, heads_local), -jnp.inf, jnp.float32),
        jnp.zeros((row_count, heads_local), jnp.float32),
        jnp.zeros((row_count, heads_local, head_size), jnp.float32),
    )


def combine_parts(first_part, second_part):
    top_score = jnp.maximum(first_part[0], second_part[0])
    first_decay = jnp.exp(first_part[0] - top_score)
    second_decay = jnp.exp(second_part[0] - top_score)
    total_weight = first_part[1] * first_decay + second_part[1] * second_decay
    summed = first_part[2] * first_decay[..., None] + second_part[2] * second_decay[..., None]
    return (top_score, total_weight, summed)


def on_device(
    tokens, cond, mod_weight, qkv_weight, q_gain, k_gain, out_weight, up_weight, down_weight
):
    tensor_size = lax.axis_size("tensor")
    tensor_pos = lax.axis_index("tensor")
    width = tokens.shape[1]
    features = width * tensor_size
    activated = jax.nn.silu(cond.astype(jnp.float32)).astype(jnp.bfloat16)
    local_mod = jnp.dot(activated[None, :], mod_weight, preferred_element_type=jnp.float32)[0]
    full_mod = lax.all_gather(local_mod, ("ulysses", "blk", "tensor"), axis=0, tiled=True).reshape(
        6, features
    )
    own_mod = lax.dynamic_slice_in_dim(full_mod, tensor_pos * width, width, 1)
    resid = tokens.astype(jnp.float32)
    normed = moments_norm(resid, own_mod[0], own_mod[1], features)
    gathered = spread_rows(normed)
    group_rows = gathered.shape[0]
    attn_rows = group_rows // tensor_size
    inner_local = qkv_weight.shape[2]
    head_size = q_gain.shape[0]
    heads_local = inner_local // head_size
    flat_qkv = qkv_weight.reshape(width, 3 * inner_local)
    projected = (
        lax.psum_scatter(
            jnp.dot(gathered, flat_qkv, preferred_element_type=jnp.float32).astype(jnp.bfloat16),
            "tensor",
            scatter_dimension=0,
            tiled=True,
        )
        .astype(jnp.float32)
        .reshape(attn_rows, 3, heads_local, head_size)
    )
    queries = head_norm(projected[:, 0], q_gain).astype(jnp.bfloat16)
    keys_local = head_norm(projected[:, 1], k_gain).astype(jnp.bfloat16)
    values_local = projected[:, 2].astype(jnp.bfloat16)
    score_scale = 1.0 / math.sqrt(head_size)
    all_queries = lax.all_gather(queries, "tensor", axis=0, tiled=True)
    state = make_absorb(
        all_queries,
        score_scale,
        empty_state(group_rows, heads_local, head_size),
        (
            lax.all_gather(keys_local, "blk", axis=0, tiled=True),
            lax.all_gather(values_local, "blk", axis=0, tiled=True),
        ),
    )
    merged = joined(state, "tensor", combine_parts)
    context = (
        (merged[2] / merged[1][..., None]).astype(jnp.bfloat16).reshape(group_rows, inner_local)
    )
    attended = lax.psum_scatter(
        jnp.dot(context, out_weight, preferred_element_type=jnp.float32).astype(jnp.bfloat16),
        "ulysses",
        scatter_dimension=0,
        tiled=True,
    ).astype(jnp.float32)
    mixed = resid + own_mod[2] * attended
    normed_two = moments_norm(mixed, own_mod[3], own_mod[4], features)
    gathered_two = spread_rows(normed_two)
    hidden = lax.psum_scatter(
        jnp.dot(gathered_two, up_weight, preferred_element_type=jnp.float32).astype(jnp.bfloat16),
        "tensor",
        scatter_dimension=0,
        tiled=True,
    ).astype(jnp.float32)
    activ = jax.nn.gelu(hidden, approximate=True).astype(jnp.bfloat16)
    activ_rows = lax.all_gather(activ, "tensor", axis=0, tiled=True)
    feedforward = lax.psum_scatter(
        jnp.dot(activ_rows, down_weight, preferred_element_type=jnp.float32).astype(jnp.bfloat16),
        "ulysses",
        scatter_dimension=0,
        tiled=True,
    ).astype(jnp.float32)
    return mixed + own_mod[5] * feedforward


VMEM_BYTES = 1024 * 1024
COPY_AT = 1
SHORT = pl.CostEstimate(flops=10**10, bytes_accessed=0, transcendentals=0)
LONG = pl.CostEstimate(flops=10**10, bytes_accessed=0, transcendentals=0)
NO_COST = pl.CostEstimate(flops=0, bytes_accessed=0, transcendentals=0)


def permuted(values, axis, distance):
    size = lax.axis_size(axis)
    return lax.ppermute(values, axis, [(i, i ^ distance) for i in range(size)])


def from_all(values, axis):
    return [values] + [permuted(values, axis, k) for k in range(1, lax.axis_size(axis))]


def to_all(blocks, axis):
    return [blocks[0]] + [permuted(blocks[k], axis, k) for k in range(1, len(blocks))]


def after_specs(after):
    shapes = [(1,) * (dep.ndim - 2) + (min(16, dep.shape[-2]), 128) for dep in after]
    return [pl.BlockSpec(shape, lambda j, n=len(shape): (0,) * n) for shape in shapes]


def merge_kernel(axis, distance, own_ref, other_ref, *refs):
    out_ref = refs[-1]
    rows = own_ref.shape[0]
    upper = (lax.axis_index(axis) & distance) != 0
    out_ref[:rows, :] = jnp.where(upper, other_ref[...], own_ref[...])
    out_ref[rows:, :] = jnp.where(upper, own_ref[...], other_ref[...])


def doubled_once(piece, axis, distance, after):
    other = permuted(piece, axis, distance)
    rows, length = piece.shape
    block = pl.BlockSpec((rows, length), lambda j: (0, 0))
    return pl.pallas_call(
        lambda *refs: merge_kernel(axis, distance, *refs),
        grid=(1,),
        in_specs=[block, block] + after_specs(after),
        out_specs=pl.BlockSpec((2 * rows, length), lambda j: (0, 0)),
        out_shape=jax.ShapeDtypeStruct((2 * rows, length), piece.dtype),
        compiler_params=pltpu.CompilerParams(vmem_limit_bytes=VMEM_BYTES),
        cost_estimate=NO_COST,
        name="merged",
    )(piece, other, *after)


def lane_tiles(rows, count, length):
    return -(-(-(-length // 128)) // (rows // count))


def pack_kernel(values_ref, pieces_ref, out_ref):
    rows, width = values_ref.shape
    count, length = pieces_ref.shape
    per = rows // count
    out_ref[:, :width] = values_ref[...]
    for tile in range((out_ref.shape[1] - width) // 128):
        lines = []
        for row in range(count):
            for low in range(tile * per * 128, (tile + 1) * per * 128, 128):
                size = max(0, min(128, length - low))
                line = jnp.zeros((1, 128 - size), jnp.float32)
                if size:
                    part = pieces_ref[row : row + 1, low : low + size]
                    line = jnp.concatenate([part, line], axis=1) if size < 128 else part
                lines.append(line)
        columns = slice(width + tile * 128, width + (tile + 1) * 128)
        out_ref[:, columns] = jnp.concatenate(lines, axis=0).astype(jnp.bfloat16)


def packed(values, pieces):
    rows, width = values.shape
    columns = width + 128 * lane_tiles(rows, *pieces.shape)
    return pl.pallas_call(
        pack_kernel,
        out_shape=jax.ShapeDtypeStruct((rows, columns), jnp.bfloat16),
        compiler_params=pltpu.CompilerParams(vmem_limit_bytes=VMEM_BYTES * 2),
        cost_estimate=NO_COST,
        name="packed",
    )(values, pieces)


def assemble_kernel(axis, count, length, *refs):
    *tile_refs, out_ref, pieces_ref = refs
    position = lax.axis_index(axis)
    tiles = [ref[...].astype(jnp.float32) for ref in tile_refs]
    bit = 1
    while bit < len(tiles):
        flip = (position & bit) != 0
        tiles = [jnp.where(flip, tiles[i ^ bit], tiles[i]) for i in range(len(tiles))]
        bit *= 2
    per = tiles[0].shape[0] // count
    for block, tile in enumerate(tiles):
        for row in range(count):
            for low in range(0, length, 128):
                line = row * per + low // 128 % per
                columns = low // 128 // per * 128
                size = min(128, length - low)
                pieces_ref[block * count + row : block * count + row + 1, low : low + size] = tile[
                    line : line + 1, columns : columns + size
                ]
    width = out_ref.shape[1]
    vectors = out_ref.shape[0]
    halves = len(tiles) * count * length // (vectors * width)
    for half in range(halves):

        @pl.when(lax.axis_index("tensor") == half)
        def _(half=half):
            for vector in range(vectors):
                at = (vector * halves + half) * width
                end = at + width
                parts = []
                while at < end:
                    row, low = divmod(at, length)
                    high = min(length, low + end - at)
                    parts.append(pieces_ref[row : row + 1, low:high])
                    at += high - low
                out_ref[vector : vector + 1, :] = jnp.concatenate(parts, axis=1)


def assembled(blocks, axis, count, length, width):
    rows, columns = blocks[0].shape
    extra = columns - width
    return pl.pallas_call(
        lambda *refs: assemble_kernel(axis, count, length, *refs),
        grid=(1,),
        in_specs=[pl.BlockSpec((rows, extra), lambda j: (0, width // extra)) for _ in blocks],
        out_specs=pl.BlockSpec((6, width), lambda j: (0, 0)),
        out_shape=jax.ShapeDtypeStruct((6, width), jnp.float32),
        scratch_shapes=[pltpu.VMEM((len(blocks) * count, -(-length // 128) * 128), jnp.float32)],
        compiler_params=pltpu.CompilerParams(vmem_limit_bytes=VMEM_BYTES),
        cost_estimate=NO_COST,
        name="assembled",
    )(*blocks)


def moments(values, shape):
    average = jnp.mean(values, axis=-1, keepdims=True)
    away = values - average
    lane = lax.broadcasted_iota(jnp.int32, shape, 1)
    return jnp.where(lane < shape[1] // 2, average, jnp.sum(away * away, axis=-1, keepdims=True))


def combined(own, arrived, features):
    middle = own.shape[1] // 2
    first, second = own[:, :1], arrived[:, :1]
    squares = own[:, middle:][:, :1] + arrived[:, middle:][:, :1]
    apart = first - second
    return (first + second) * 0.5, squares / features + apart * apart * 0.25


def row_sums_kernel(values_ref, out_ref, copy_ref):
    out_ref[...] = moments(values_ref[...].astype(jnp.float32), out_ref.shape)
    copy_ref[...] = values_ref[...]


def row_sums(values):
    return pl.pallas_call(
        row_sums_kernel,
        out_shape=[
            jax.ShapeDtypeStruct((values.shape[0], 128), jnp.float32),
            jax.ShapeDtypeStruct(values.shape, values.dtype),
        ],
        compiler_params=pltpu.CompilerParams(vmem_limit_bytes=VMEM_BYTES * 2),
        cost_estimate=NO_COST,
        name="row_sums",
    )(values)


def standardize_kernel(features, values_ref, own_ref, arrived_ref, *refs):
    average, variance = combined(own_ref[...], arrived_ref[...], features)
    values = values_ref[...].astype(jnp.float32)
    refs[-1][...] = ((values - average) * lax.rsqrt(variance + 1e-06)).astype(jnp.bfloat16)


def standardized(values, features, after):
    own, values = row_sums(values)
    whole = lambda array: pl.BlockSpec(array.shape, lambda j: (0, 0))
    return pl.pallas_call(
        lambda *refs: standardize_kernel(features, *refs),
        grid=(1,),
        in_specs=[whole(values), whole(own), whole(own)] + after_specs(after),
        out_specs=whole(values),
        out_shape=jax.ShapeDtypeStruct(values.shape, jnp.bfloat16),
        compiler_params=pltpu.CompilerParams(vmem_limit_bytes=VMEM_BYTES * 2),
        cost_estimate=NO_COST,
        name="standardized",
    )(values, own, permuted(own, "tensor", 1), *after)


def stack_kernel(*refs):
    *block_refs, out_ref = refs
    rows = block_refs[0].shape[0]
    for k, block_ref in enumerate(block_refs):
        out_ref[k * rows : (k + 1) * rows, :] = block_ref[...]


def stacked(blocks, cost):
    rows, width = blocks[0].shape
    return pl.pallas_call(
        stack_kernel,
        out_shape=jax.ShapeDtypeStruct((rows * len(blocks), width), blocks[0].dtype),
        compiler_params=pltpu.CompilerParams(vmem_limit_bytes=VMEM_BYTES * 2),
        cost_estimate=cost,
        name="stacked",
    )(*blocks)


def copied_kernel(values_ref, after_ref, out_ref):
    out_ref[...] = values_ref[...]


def copied(values, after, cost):
    whole = pl.BlockSpec(values.shape, lambda j: (0, 0))
    return pl.pallas_call(
        copied_kernel,
        grid=(1,),
        in_specs=[whole] + after_specs([after]),
        out_specs=whole,
        out_shape=jax.ShapeDtypeStruct(values.shape, values.dtype),
        compiler_params=pltpu.CompilerParams(vmem_limit_bytes=VMEM_BYTES * 2),
        cost_estimate=cost,
        name="copied",
    )(values, after)


def added(blocks):
    total = blocks[0].astype(jnp.float32)
    for block in blocks[1:]:
        total = total + block.astype(jnp.float32)
    return total


def project_kernel(count, parts, other, *refs):
    block_refs = refs[:count]
    shift_ref, scale_ref = refs[count : count + 2]
    weight_refs = refs[count + 2 : count + 2 + parts]
    normed_ref = refs[-1]
    rows = block_refs[0].shape[0]
    for k, block_ref in enumerate(block_refs):
        values = block_ref[...].astype(jnp.float32)
        values = values * (1.0 + scale_ref[...]) + shift_ref[...]
        normed_ref[k * rows : (k + 1) * rows, :] = values.astype(jnp.bfloat16)
    project_parts(normed_ref, weight_refs, refs[-1 - parts : -1], other)


def project_parts(normed_ref, weight_refs, out_refs, other):
    half = out_refs[0].shape[1]
    position = lax.axis_index("tensor")
    low = pl.multiple_of((1 - position if other else position) * half, 128)
    for weight_ref, out_ref in zip(weight_refs, out_refs):
        out_ref[...] = jnp.dot(
            normed_ref[...], weight_ref[:, pl.ds(low, half)], preferred_element_type=jnp.float32
        ).astype(jnp.bfloat16)


def project_again_kernel(parts, other, normed_ref, *refs):
    project_parts(normed_ref, refs[:parts], refs[-parts:], other)


def projected(blocks, small, weights, half, other, after=()):
    rows, width = blocks[0].shape[0], weights[0].shape[0]
    all_rows = rows * len(blocks)
    count = len(weights)
    whole = lambda shape: pl.BlockSpec(shape, lambda j: (0, 0))
    shapes = [(all_rows, half)] * count + [(all_rows, width)] * bool(small)
    return pl.pallas_call(
        (lambda *refs: project_kernel(len(blocks), count, other, *refs))
        if small
        else (lambda *refs: project_again_kernel(count, other, *refs)),
        grid=(1,),
        in_specs=[whole((rows, width)) for _ in blocks]
        + [whole(array.shape) for array in small]
        + [pl.BlockSpec(memory_space=pltpu.VMEM) for _ in weights]
        + after_specs(after),
        out_specs=[whole(shape) for shape in shapes],
        out_shape=[jax.ShapeDtypeStruct(shape, jnp.bfloat16) for shape in shapes],
        compiler_params=pltpu.CompilerParams(vmem_limit_bytes=VMEM_BYTES * 20),
        cost_estimate=NO_COST,
        name="projected",
    )(*blocks, *small, *weights, *after)


def staged(weights, after, part=None):
    width, columns = weights.shape[-2:]
    pieces = 4 if width % 64 == 0 else 1
    rows = width // pieces
    anywhere = pl.BlockSpec(memory_space=pl.ANY)

    def kernel(weight_ref, after_ref, out_ref, sems):
        source_ref = weight_ref if part is None else weight_ref.at[part]
        copies = [
            pltpu.make_async_copy(
                source_ref.at[pl.ds(k * rows, rows)], out_ref.at[pl.ds(k * rows, rows)], sems.at[k]
            )
            for k in range(pieces)
        ]
        for copy in copies:
            copy.start()
        for copy in copies:
            copy.wait()

    return pl.pallas_call(
        kernel,
        grid=(1,),
        in_specs=[anywhere] + after_specs([after]),
        out_specs=pl.BlockSpec(memory_space=pltpu.VMEM),
        out_shape=pltpu.VMEM((width, columns), weights.dtype),
        scratch_shapes=[pltpu.SemaphoreType.DMA((pieces,))],
        compiler_params=pltpu.CompilerParams(vmem_limit_bytes=VMEM_BYTES),
        cost_estimate=pl.CostEstimate(
            flops=0, bytes_accessed=2 * width * columns, transcendentals=0
        ),
        name="staged",
    )(weights, after)


def mark_kernel(*refs):
    refs[-1][...] = jnp.zeros(refs[-1].shape, jnp.float32)


def mark(after, cost):
    return pl.pallas_call(
        mark_kernel,
        grid=(1,),
        in_specs=after_specs(after),
        out_specs=pl.BlockSpec((8, 128), lambda j: (0, 0)),
        out_shape=jax.ShapeDtypeStruct((8, 128), jnp.float32),
        compiler_params=pltpu.CompilerParams(vmem_limit_bytes=VMEM_BYTES),
        cost_estimate=cost,
        name="mark",
    )(*after)


def head_normal(values, gain_ref):
    spread = jnp.mean(values * values, axis=-1, keepdims=True) + 1e-06
    return (values * lax.rsqrt(spread) * gain_ref[...]).astype(jnp.bfloat16)


def heads_kernel(count, head_size, *refs):
    own_refs, arrived_refs = refs[:count], refs[count : 2 * count]
    q_gain_ref, k_gain_ref = refs[2 * count : 2 * count + 2]
    out_refs = refs[-1:] if count == 2 else refs[-2:]
    half = own_refs[0].shape[1]

    def total(part, here):
        return own_refs[part][:, here].astype(jnp.float32) + arrived_refs[part][:, here].astype(
            jnp.float32
        )

    for low in range(0, half, head_size):
        here = slice(low, low + head_size)
        if count == 3:
            out_refs[1][:, here] = head_normal(total(0, here), q_gain_ref)
        out_refs[0][:, here] = head_normal(total(count - 2, here), k_gain_ref)
        out_refs[0][:, half + low : half + low + head_size] = total(count - 1, here).astype(
            jnp.bfloat16
        )


def split_heads(own, arrived, q_gain, k_gain, after=()):
    count = len(own)
    rows, half = own[0].shape
    head_size = q_gain.shape[0]
    widths = [2 * half] if count == 2 else [2 * half, half]
    whole = lambda *shape: pl.BlockSpec(shape, lambda j: (0, 0))
    return pl.pallas_call(
        lambda *refs: heads_kernel(count, head_size, *refs),
        grid=(1,),
        in_specs=[whole(rows, half)] * (2 * count)
        + [whole(1, head_size)] * 2
        + after_specs(after),
        out_specs=[whole(rows, width) for width in widths],
        out_shape=[jax.ShapeDtypeStruct((rows, width), jnp.bfloat16) for width in widths],
        compiler_params=pltpu.CompilerParams(vmem_limit_bytes=VMEM_BYTES * 5),
        cost_estimate=NO_COST,
        name="split_heads",
    )(*own, *arrived, q_gain[None, :], k_gain[None, :], *after)


def head_scores(query, key, head_size):
    product = lax.dot_general(
        query, key, (((1,), (1,)), ((), ())), preferred_element_type=jnp.float32
    )
    return product * (1.0 / math.sqrt(head_size))


def weighted(scores, values, top):
    total, summed = 0.0, 0.0
    for part, value in zip(scores, values):
        weights = jnp.exp(part - top)
        total = total + jnp.sum(weights, axis=-1, keepdims=True)
        summed = summed + jnp.dot(
            weights.astype(jnp.bfloat16), value, preferred_element_type=jnp.float32
        )
    return total, summed


def highest(scores, top=None):
    for part in scores:
        part_top = jnp.max(part, axis=-1, keepdims=True)
        top = part_top if top is None else jnp.maximum(top, part_top)
    return top


def attend_kernel(head_size, count, query_ref, *refs):
    kv_refs, (top_ref, total_ref, summed_ref) = refs[:count], refs[-3:]
    half = query_ref.shape[1]
    places = [slice(low, low + head_size) for low in range(0, half, head_size)]
    scores = [
        [head_scores(query_ref[:, here], ref[:, here], head_size) for ref in kv_refs]
        for here in places
    ]
    tops = [highest(parts) for parts in scores]
    for here, parts, top in zip(places, scores, tops):
        values = [ref[:, half + here.start : half + here.stop] for ref in kv_refs]
        total, summed = weighted(parts, values, top)
        top_ref[:, here] = jnp.broadcast_to(top, summed.shape)
        total_ref[:, here] = jnp.broadcast_to(total, summed.shape)
        summed_ref[:, here] = summed


def attend(queries, kv_parts, head_size, after):
    whole = lambda array: pl.BlockSpec(array.shape, lambda j: (0, 0))
    state = jax.ShapeDtypeStruct(queries.shape, jnp.float32)
    return pl.pallas_call(
        lambda *refs: attend_kernel(head_size, len(kv_parts), *refs),
        grid=(1,),
        in_specs=[whole(array) for array in [queries, *kv_parts]] + after_specs(after),
        out_specs=[whole(queries)] * 3,
        out_shape=[state] * 3,
        compiler_params=pltpu.CompilerParams(vmem_limit_bytes=VMEM_BYTES * 12),
        cost_estimate=NO_COST,
        name="attend",
    )(queries, *kv_parts, *after)


def finish_kernel(head_size, count, query_ref, top_ref, total_ref, summed_ref, *refs):
    kv_refs, out_ref = refs[:count], refs[-1]
    half = query_ref.shape[1]
    places = [slice(low, low + head_size) for low in range(0, half, head_size)]
    tops = [top_ref[:, here] for here in places]
    totals = [total_ref[:, here] for here in places]
    sums = [summed_ref[:, here] for here in places]
    if kv_refs:
        keys = [kv_refs[0][:, here] for here in places]
        values = [kv_refs[0][:, half + here.start : half + here.stop] for here in places]
        scores = [
            head_scores(query_ref[:, here], key, head_size) for here, key in zip(places, keys)
        ]
        new_tops = [jnp.maximum(top, highest([part])) for top, part in zip(tops, scores)]
        decays = [jnp.exp(top - new_top) for top, new_top in zip(tops, new_tops)]
        weights = [jnp.exp(part - new_top[:, :1]) for part, new_top in zip(scores, new_tops)]
        products = [
            jnp.dot(part.astype(jnp.bfloat16), value, preferred_element_type=jnp.float32)
            for part, value in zip(weights, values)
        ]
        totals = [
            total * decay + jnp.sum(part, axis=-1, keepdims=True)
            for total, decay, part in zip(totals, decays, weights)
        ]
        sums = [part * decay + more for part, decay, more in zip(sums, decays, products)]
    for here, total, part in zip(places, totals, sums):
        out_ref[:, here] = (part / total).astype(jnp.bfloat16)


def finished(queries, state, parts, head_size, first, count, after=()):
    whole = lambda array: pl.BlockSpec(array.shape, lambda j: (0, 0))
    some = pl.BlockSpec((count, queries.shape[1]), lambda j: (first // count, 0))
    return pl.pallas_call(
        lambda *refs: finish_kernel(head_size, len(parts), *refs),
        grid=(1,),
        in_specs=[some] * 4 + [whole(array) for array in parts] + after_specs(after),
        out_specs=pl.BlockSpec((count, queries.shape[1]), lambda j: (0, 0)),
        out_shape=jax.ShapeDtypeStruct((count, queries.shape[1]), jnp.bfloat16),
        compiler_params=pltpu.CompilerParams(vmem_limit_bytes=VMEM_BYTES * 12),
        cost_estimate=NO_COST,
        name="finished",
    )(queries, *state, *parts, *after)


def column_tiles(columns):
    size = columns // 3 if columns % 384 == 0 else columns
    return [slice(low, low + size) for low in range(0, columns, size)]


def out_kernel(count, own_ref, arrived_ref, weight_ref, *refs):
    out_refs = refs[-count:]
    half = own_ref.shape[1]
    position = lax.axis_index("tensor")
    rows = [pl.ds(pl.multiple_of(at * half, 16), half) for at in (position, 1 - position)]
    for here in column_tiles(weight_ref.shape[1]):
        total = jnp.dot(
            own_ref[...], weight_ref[rows[0], here], preferred_element_type=jnp.float32
        ) + jnp.dot(arrived_ref[...], weight_ref[rows[1], here], preferred_element_type=jnp.float32)
        row_blocks(total, here, out_refs)


def row_blocks(values, columns, out_refs):
    rows = out_refs[0].shape[0]
    for k, out_ref in enumerate(out_refs):
        out_ref[:, columns] = values[k * rows : (k + 1) * rows].astype(jnp.bfloat16)


def out_projected(own, arrived, weight, rows, after):
    all_rows, half = own.shape
    width = weight.shape[1]
    whole = pl.BlockSpec((all_rows, half), lambda j: (0, 0))
    return pl.pallas_call(
        lambda *refs: out_kernel(all_rows // rows, *refs),
        grid=(1,),
        in_specs=[whole, whole, pl.BlockSpec(memory_space=pltpu.VMEM)] + after_specs(after),
        out_specs=[pl.BlockSpec((rows, width), lambda j: (0, 0))] * (all_rows // rows),
        out_shape=[jax.ShapeDtypeStruct((rows, width), jnp.bfloat16)] * (all_rows // rows),
        compiler_params=pltpu.CompilerParams(vmem_limit_bytes=VMEM_BYTES * 8),
        cost_estimate=NO_COST,
        name="out_projected",
    )(own, arrived, weight, *after)


def up_kernel(first, count, *refs):
    block_refs, weight_ref, (out_ref, joined_ref) = refs[:count], refs[count], refs[-2:]
    rows = block_refs[0].shape[0]
    for k, block_ref in enumerate(block_refs):
        joined_ref[k * rows : (k + 1) * rows, :] = block_ref[...]
    for here in column_tiles(out_ref.shape[1]):
        out_ref[:, here] = jnp.dot(
            joined_ref[...],
            weight_ref[:, first + here.start : first + here.stop],
            preferred_element_type=jnp.float32,
        ).astype(jnp.bfloat16)


def up_projected(blocks, weight, part, parts, after=()):
    rows, width = blocks[0].shape
    all_rows = rows * len(blocks)
    columns = weight.shape[1] // parts
    return pl.pallas_call(
        lambda *refs: up_kernel(part * columns, len(blocks), *refs),
        grid=(1,),
        in_specs=[pl.BlockSpec((rows, width), lambda j: (0, 0)) for _ in blocks]
        + [pl.BlockSpec(memory_space=pltpu.VMEM)]
        + after_specs(after),
        out_specs=pl.BlockSpec((all_rows, columns), lambda j: (0, 0)),
        out_shape=jax.ShapeDtypeStruct((all_rows, columns), jnp.bfloat16),
        scratch_shapes=[pltpu.VMEM((all_rows, width), jnp.bfloat16)],
        compiler_params=pltpu.CompilerParams(vmem_limit_bytes=VMEM_BYTES * 8),
        cost_estimate=pl.CostEstimate(
            flops=2 * all_rows * width * columns, bytes_accessed=0, transcendentals=0
        ),
        name="up_projected",
    )(*blocks, weight, *after)


def down_kernel(first, count, more, own_ref, arrived_ref, weight_ref, *refs):
    *out_refs, activ_ref = refs
    depth = own_ref.shape[1]
    for here in column_tiles(depth):
        hidden = own_ref[:, here].astype(jnp.float32) + arrived_ref[:, here].astype(jnp.float32)
        activ_ref[:, here] = jax.nn.gelu(hidden, approximate=True).astype(jnp.bfloat16)
    for here in column_tiles(weight_ref.shape[1]):
        total = jnp.dot(
            activ_ref[...],
            weight_ref[first : first + depth, here],
            preferred_element_type=jnp.float32,
        )
        if more:
            total = total + out_refs[0][:, here]
        if count:
            row_blocks(total, here, out_refs[-count:])
        else:
            out_refs[0][:, here] = total


def down_projected(own, arrived, weight, first, before, count):
    all_rows, depth = own.shape
    width = weight.shape[1]
    whole = lambda *shape: pl.BlockSpec(shape, lambda j: (0, 0))
    shape, kind = (all_rows // max(count, 1), width), jnp.bfloat16 if count else jnp.float32
    return pl.pallas_call(
        lambda *refs: down_kernel(first, count, len(before), *refs),
        grid=(1,),
        in_specs=[whole(all_rows, depth)] * 2
        + [pl.BlockSpec(memory_space=pltpu.VMEM)]
        + [whole(all_rows, width)] * len(before),
        out_specs=[whole(*shape)] * max(count, 1),
        out_shape=[jax.ShapeDtypeStruct(shape, kind)] * max(count, 1),
        scratch_shapes=[pltpu.VMEM((all_rows, depth), jnp.bfloat16)],
        compiler_params=pltpu.CompilerParams(vmem_limit_bytes=VMEM_BYTES * 12),
        cost_estimate=NO_COST,
        name="down_projected",
    )(own, arrived, weight, *before)


def add_kernel(first_ref, second_ref, out_ref):
    total = first_ref[...].astype(jnp.float32) + second_ref[...].astype(jnp.float32)
    out_ref[...] = total.astype(jnp.bfloat16)


def rounded_sum(first, second):
    return pl.pallas_call(
        add_kernel,
        out_shape=jax.ShapeDtypeStruct(first.shape, first.dtype),
        compiler_params=pltpu.CompilerParams(vmem_limit_bytes=VMEM_BYTES * 2),
        cost_estimate=NO_COST,
        name="rounded_sum",
    )(first, second)


def row_groups(blocks, axis):
    groups = len(blocks) // lax.axis_size(axis)
    pieces = [blocks[k : k + groups] for k in range(0, len(blocks), groups)]
    if groups != 2 or len(pieces) != 4:
        return [to_all([piece[k] for piece in pieces], axis) for k in range(groups)]
    own, first, second, far = pieces
    low, high = permuted(far[0], axis, 1), permuted(far[1], axis, 2)
    first_low, second_high = permuted(first[0], axis, 1), permuted(second[1], axis, 2)
    second_low = permuted(rounded_sum(second[0], low), axis, 2)
    first_high = permuted(rounded_sum(first[1], high), axis, 1)
    return [[own[0], first_low, second_low], [own[1], first_high, second_high]]


def mix_kernel(counts, *refs):
    token_ref, gate_ref = refs[sum(counts)], refs[sum(counts) + 1]
    mixed_ref, sums_ref = refs[-2:]
    rows = refs[0].shape[0]
    at = 0
    for group, count in enumerate(counts):
        here = slice(group * rows, (group + 1) * rows)
        total = refs[at][...].astype(jnp.float32)
        for block_ref in refs[at + 1 : at + count]:
            total = total + block_ref[...].astype(jnp.float32)
        at += count
        mixed = token_ref[here, :].astype(jnp.float32) + gate_ref[...] * total
        mixed_ref[here, :] = mixed
        sums_ref[here, :] = moments(mixed, (rows, sums_ref.shape[1]))


def mixed_rows(groups, tokens, gate_row, after):
    rows, width = tokens.shape
    whole = lambda *shape: pl.BlockSpec(shape, lambda j: (0, 0))
    blocks = [block for group in groups for block in group]
    return pl.pallas_call(
        lambda *refs: mix_kernel([len(group) for group in groups], *refs),
        grid=(1,),
        in_specs=[whole(*block.shape) for block in blocks]
        + [whole(rows, width), whole(1, width)]
        + after_specs(after),
        out_specs=[whole(rows, width), whole(rows, 128)],
        out_shape=[
            jax.ShapeDtypeStruct((rows, width), jnp.float32),
            jax.ShapeDtypeStruct((rows, 128), jnp.float32),
        ],
        compiler_params=pltpu.CompilerParams(vmem_limit_bytes=VMEM_BYTES * 4),
        cost_estimate=NO_COST,
        name="mixed_rows",
    )(*blocks, tokens, gate_row, *after)


def norm_kernel(features, mixed_ref, own_ref, arrived_ref, shift_ref, scale_ref, out_ref):
    average, variance = combined(own_ref[...], arrived_ref[...], features)
    values = (mixed_ref[...] - average) * lax.rsqrt(variance + 1e-06)
    out_ref[...] = (values * (1.0 + scale_ref[...]) + shift_ref[...]).astype(jnp.bfloat16)


def normed_rows(mixed, sums, shift_row, scale_row, features):
    return pl.pallas_call(
        lambda *refs: norm_kernel(features, *refs),
        out_shape=jax.ShapeDtypeStruct(mixed.shape, jnp.bfloat16),
        compiler_params=pltpu.CompilerParams(vmem_limit_bytes=VMEM_BYTES * 2),
        cost_estimate=NO_COST,
        name="normed_rows",
    )(mixed, sums, permuted(sums, "tensor", 1), shift_row, scale_row)


def on_pair(
    tokens, cond, mod_weight, qkv_weight, q_gain, k_gain, out_weight, up_weight, down_weight
):
    stages = [
        (axis, 1 << bit)
        for axis in ("tensor", "blk")
        for bit in range(lax.axis_size(axis).bit_length() - 1)
    ]
    rows, width = tokens.shape
    features = width * lax.axis_size("tensor")
    head_size = q_gain.shape[0]
    half = qkv_weight.shape[2] // 2
    blocks_z = lax.axis_size("blk")

    activated = jax.nn.silu(cond.astype(jnp.float32)).astype(jnp.bfloat16)
    pieces = jnp.dot(activated[None, :], mod_weight, preferred_element_type=jnp.float32)
    weights = pltpu.with_memory_space_constraint(jnp.moveaxis(qkv_weight, 1, 0), pltpu.HBM)
    start = copied(tokens, pieces, NO_COST)
    remote = [permuted(start, "blk", k) for k in range(2, blocks_z, 2)]
    normal = standardized(tokens, features, [])
    parts = []
    for stage in stages:
        after = []
        if stage[0] == "blk":
            take = [1] if stage[1] == 1 else [2]
            parts += [staged(weights, pieces, part) for part in take]
            after = parts + (remote if stage[1] == 2 else [normal])
        pieces = doubled_once(pieces, *stage, after)
    own = packed(normal, pieces)
    parts = [staged(weights, own, 0)] + parts
    chunks = [from_all(own, "ulysses")]
    if remote:
        far = stacked(remote + [permuted(block, "blk", 1) for block in remote], NO_COST)
        far = standardized(far, features, [])
        chunks.append(from_all(far, "ulysses"))
    own_mod = assembled(chunks[0], "ulysses", *pieces.shape, width)
    row = lambda k: own_mod[k : k + 1]
    out_weight, up_weight, down_weight = [
        pltpu.with_memory_space_constraint(weight, pltpu.HBM)
        for weight in (out_weight, up_weight, down_weight)
    ]

    def project(blocks, use, after):
        *partial, normed = projected(blocks, [row(0), row(1)], use, half, True, after)
        arrived = [permuted(part, "tensor", 1) for part in partial]
        return projected([normed], [], use, half, False), arrived

    own, arrived = project(chunks[0], parts, [far] * bool(remote))
    own_kv, queries = split_heads(own, arrived, q_gain, k_gain)
    kv_parts = [own_kv]
    if blocks_z > 1:
        arrived = permuted(own_kv, "blk", 1)
        kv_parts.append(copied(arrived, arrived, LONG))
    out_weight = staged(out_weight, own_kv)
    up_weight = staged(up_weight, out_weight)
    last = []
    first_blocks, last_blocks = halves(chunks[-1])
    if remote:
        own, arrived = project(first_blocks, parts[1:], [own_kv])
        kv_parts += split_heads(own, arrived, q_gain, k_gain)
    state = attend(queries, kv_parts, head_size, [out_weight, up_weight])
    if remote and last_blocks:
        tie = mark([*chunks[-1][1:], state[0]], SHORT)
        own, arrived = project(last_blocks, parts[1:], [state[0], tie])
        last = split_heads(own, arrived, q_gain, k_gain)
    all_rows = queries.shape[0]
    last_rows = rows if all_rows > rows else 0
    partial, arrived = [], []
    if last_rows:
        context = finished(queries, state, last, head_size, all_rows - rows, rows)
        arrived.append((context, permuted(context, "tensor", 1)))
    after = [own for own, _ in arrived]
    context = finished(queries, state, last, head_size, 0, all_rows - last_rows, after)
    other = permuted(context, "tensor", 1)
    arrived.append((context, other))
    for own, other in arrived:
        after = [] if own is context else [context]
        partial = list(out_projected(own, other, out_weight, rows // 2, after)) + partial
    summed = row_groups(partial, "ulysses")
    mixed, sums = mixed_rows(summed, tokens, row(2), [])
    normed_two = normed_rows(mixed, sums, row(3), row(4), features)
    blocks = from_all(normed_two, "ulysses")
    down_weight = staged(down_weight, normed_two)
    order = halves(list(range(len(blocks))))
    outs = {}
    for part, places in enumerate(order):
        if not places:
            continue
        here = [blocks[k] for k in places]
        here = [stacked(here, LONG)] if part else here
        pieces = 2
        after = [outs[order[0][0]]] if part else [down_weight]
        ups = [up_projected(here, up_weight, k, pieces, after) for k in range(pieces)]
        arrived = [permuted(piece, "tensor", 1) for piece in ups]
        before = []
        for k, (own, other) in enumerate(zip(ups, arrived)):
            count = len(places) if k == pieces - 1 else 0
            before = down_projected(own, other, down_weight, k * own.shape[1], before, count)
        outs.update(zip(places, before))
    feedforward = added(to_all([outs[k] for k in range(len(blocks))], "ulysses"))
    return mixed + own_mod[5] * feedforward


def halves(items):
    order = items[:1] + items[:0:-1]
    middle = (len(order) + 1) // 2
    return order[:middle], order[middle:]


def solution(mesh):
    sizes = [mesh.shape[axis] for axis in ("ulysses", "blk")]
    pairs = mesh.shape["tensor"] == 2 and all(size & (size - 1) == 0 for size in sizes)
    return jax.shard_map(
        on_pair if pairs else on_device,
        mesh=mesh,
        in_specs=(
            P(("ulysses", "blk"), "tensor"),
            P(),
            P(None, ("ulysses", "blk", "tensor")),
            P("tensor", None, "ulysses"),
            P(),
            P(),
            P("ulysses", "tensor"),
            P("tensor", "ulysses"),
            P("ulysses", "tensor"),
        ),
        out_specs=P(("ulysses", "blk"), "tensor"),
        check_vma=False,
    )
```

```python
import math

import jax
import jax.numpy as jnp
from jax import lax
from jax.experimental import pallas as pl
from jax.experimental.pallas import tpu as pltpu
from jax.sharding import PartitionSpec as P


def joined(array, axis, combine):
    everything = jax.tree.map(
        lambda part, kind: lax.all_gather(part.astype(kind), axis),
        array,
        jax.tree.map(lambda a: jnp.bfloat16 if a.dtype == jnp.float32 else a.dtype, array),
    )

    def take(k):
        return jax.tree.map(lambda part, own: part[k].astype(own.dtype), everything, array)

    return lax.fori_loop(
        1, lax.axis_size(axis), lambda k, so_far: combine(so_far, take(k)), take(0)
    )


def moments_norm(values, shift_row, scale_row, features):
    sums = lax.psum((jnp.sum(values, axis=-1), jnp.sum(values * values, axis=-1)), "tensor")
    average = sums[0][:, None] / features
    variance = sums[1][:, None] / features - average * average
    normal_rows = (values - average) * lax.rsqrt(variance + 1e-06)
    return (normal_rows * (1.0 + scale_row) + shift_row).astype(jnp.bfloat16)


def spread_rows(values):
    return lax.all_gather(values, "ulysses", axis=0, tiled=True)


def head_norm(values, gains):
    return values * lax.rsqrt(jnp.mean(values * values, axis=-1, keepdims=True) + 1e-06) * gains


def make_absorb(queries, score_scale, running, kv_block):
    keys_part, values_part = kv_block
    top_score, total_weight, summed = running
    scores = (
        jnp.einsum("qhd,khd->qhk", queries, keys_part, preferred_element_type=jnp.float32)
        * score_scale
    )
    new_top = jnp.max(scores, axis=-1)
    decay = jnp.exp(top_score - new_top)
    weights = jnp.exp(scores - new_top[..., None])
    total_weight = total_weight * decay + jnp.sum(weights, axis=-1)
    summed = summed * decay[..., None] + jnp.einsum(
        "qhk,khd->qhd",
        weights.astype(jnp.bfloat16),
        values_part,
        preferred_element_type=jnp.float32,
    )
    return (new_top, total_weight, summed)


def empty_state(row_count, heads_local, head_size):
    return (
        jnp.full((row_count, heads_local), -jnp.inf, jnp.float32),
        jnp.zeros((row_count, heads_local), jnp.float32),
        jnp.zeros((row_count, heads_local, head_size), jnp.float32),
    )


def combine_parts(first_part, second_part):
    top_score = jnp.maximum(first_part[0], second_part[0])
    first_decay = jnp.exp(first_part[0] - top_score)
    second_decay = jnp.exp(second_part[0] - top_score)
    total_weight = first_part[1] * first_decay + second_part[1] * second_decay
    summed = first_part[2] * first_decay[..., None] + second_part[2] * second_decay[..., None]
    return (top_score, total_weight, summed)


def on_device(
    tokens, cond, mod_weight, qkv_weight, q_gain, k_gain, out_weight, up_weight, down_weight
):
    tensor_size = lax.axis_size("tensor")
    tensor_pos = lax.axis_index("tensor")
    width = tokens.shape[1]
    features = width * tensor_size
    activated = jax.nn.silu(cond.astype(jnp.float32)).astype(jnp.bfloat16)
    local_mod = jnp.dot(activated[None, :], mod_weight, preferred_element_type=jnp.float32)[0]
    full_mod = lax.all_gather(local_mod, ("ulysses", "blk", "tensor"), axis=0, tiled=True).reshape(
        6, features
    )
    own_mod = lax.dynamic_slice_in_dim(full_mod, tensor_pos * width, width, 1)
    resid = tokens.astype(jnp.float32)
    normed = moments_norm(resid, own_mod[0], own_mod[1], features)
    gathered = spread_rows(normed)
    group_rows = gathered.shape[0]
    attn_rows = group_rows // tensor_size
    inner_local = qkv_weight.shape[2]
    head_size = q_gain.shape[0]
    heads_local = inner_local // head_size
    flat_qkv = qkv_weight.reshape(width, 3 * inner_local)
    projected = (
        lax.psum_scatter(
            jnp.dot(gathered, flat_qkv, preferred_element_type=jnp.float32).astype(jnp.bfloat16),
            "tensor",
            scatter_dimension=0,
            tiled=True,
        )
        .astype(jnp.float32)
        .reshape(attn_rows, 3, heads_local, head_size)
    )
    queries = head_norm(projected[:, 0], q_gain).astype(jnp.bfloat16)
    keys_local = head_norm(projected[:, 1], k_gain).astype(jnp.bfloat16)
    values_local = projected[:, 2].astype(jnp.bfloat16)
    score_scale = 1.0 / math.sqrt(head_size)
    all_queries = lax.all_gather(queries, "tensor", axis=0, tiled=True)
    state = make_absorb(
        all_queries,
        score_scale,
        empty_state(group_rows, heads_local, head_size),
        (
            lax.all_gather(keys_local, "blk", axis=0, tiled=True),
            lax.all_gather(values_local, "blk", axis=0, tiled=True),
        ),
    )
    merged = joined(state, "tensor", combine_parts)
    context = (
        (merged[2] / merged[1][..., None]).astype(jnp.bfloat16).reshape(group_rows, inner_local)
    )
    attended = lax.psum_scatter(
        jnp.dot(context, out_weight, preferred_element_type=jnp.float32).astype(jnp.bfloat16),
        "ulysses",
        scatter_dimension=0,
        tiled=True,
    ).astype(jnp.float32)
    mixed = resid + own_mod[2] * attended
    normed_two = moments_norm(mixed, own_mod[3], own_mod[4], features)
    gathered_two = spread_rows(normed_two)
    hidden = lax.psum_scatter(
        jnp.dot(gathered_two, up_weight, preferred_element_type=jnp.float32).astype(jnp.bfloat16),
        "tensor",
        scatter_dimension=0,
        tiled=True,
    ).astype(jnp.float32)
    activ = jax.nn.gelu(hidden, approximate=True).astype(jnp.bfloat16)
    activ_rows = lax.all_gather(activ, "tensor", axis=0, tiled=True)
    feedforward = lax.psum_scatter(
        jnp.dot(activ_rows, down_weight, preferred_element_type=jnp.float32).astype(jnp.bfloat16),
        "ulysses",
        scatter_dimension=0,
        tiled=True,
    ).astype(jnp.float32)
    return mixed + own_mod[5] * feedforward


VMEM_BYTES = 1024 * 1024
COPY_AT = 1
SHORT = pl.CostEstimate(flops=10**10, bytes_accessed=0, transcendentals=0)
LONG = pl.CostEstimate(flops=10**10, bytes_accessed=0, transcendentals=0)
NO_COST = pl.CostEstimate(flops=0, bytes_accessed=0, transcendentals=0)


def permuted(values, axis, distance):
    size = lax.axis_size(axis)
    return lax.ppermute(values, axis, [(i, i ^ distance) for i in range(size)])


def from_all(values, axis):
    return [values] + [permuted(values, axis, k) for k in range(1, lax.axis_size(axis))]


def to_all(blocks, axis):
    return [blocks[0]] + [permuted(blocks[k], axis, k) for k in range(1, len(blocks))]


def after_specs(after):
    shapes = [(1,) * (dep.ndim - 2) + (min(16, dep.shape[-2]), 128) for dep in after]
    return [pl.BlockSpec(shape, lambda j, n=len(shape): (0,) * n) for shape in shapes]


def merge_kernel(axis, distance, own_ref, other_ref, *refs):
    out_ref = refs[-1]
    rows = own_ref.shape[0]
    upper = (lax.axis_index(axis) & distance) != 0
    out_ref[:rows, :] = jnp.where(upper, other_ref[...], own_ref[...])
    out_ref[rows:, :] = jnp.where(upper, own_ref[...], other_ref[...])


def doubled_once(piece, axis, distance, after):
    other = permuted(piece, axis, distance)
    rows, length = piece.shape
    block = pl.BlockSpec((rows, length), lambda j: (0, 0))
    return pl.pallas_call(
        lambda *refs: merge_kernel(axis, distance, *refs),
        grid=(1,),
        in_specs=[block, block] + after_specs(after),
        out_specs=pl.BlockSpec((2 * rows, length), lambda j: (0, 0)),
        out_shape=jax.ShapeDtypeStruct((2 * rows, length), piece.dtype),
        compiler_params=pltpu.CompilerParams(vmem_limit_bytes=VMEM_BYTES),
        cost_estimate=NO_COST,
        name="merged",
    )(piece, other, *after)


def lane_tiles(rows, count, length):
    return -(-(-(-length // 128)) // (rows // count))


def pack_kernel(values_ref, pieces_ref, out_ref):
    rows, width = values_ref.shape
    count, length = pieces_ref.shape
    per = rows // count
    out_ref[:, :width] = values_ref[...]
    for tile in range((out_ref.shape[1] - width) // 128):
        lines = []
        for row in range(count):
            for low in range(tile * per * 128, (tile + 1) * per * 128, 128):
                size = max(0, min(128, length - low))
                line = jnp.zeros((1, 128 - size), jnp.float32)
                if size:
                    part = pieces_ref[row : row + 1, low : low + size]
                    line = jnp.concatenate([part, line], axis=1) if size < 128 else part
                lines.append(line)
        columns = slice(width + tile * 128, width + (tile + 1) * 128)
        out_ref[:, columns] = jnp.concatenate(lines, axis=0).astype(jnp.bfloat16)


def packed(values, pieces):
    rows, width = values.shape
    columns = width + 128 * lane_tiles(rows, *pieces.shape)
    return pl.pallas_call(
        pack_kernel,
        out_shape=jax.ShapeDtypeStruct((rows, columns), jnp.bfloat16),
        compiler_params=pltpu.CompilerParams(vmem_limit_bytes=VMEM_BYTES * 2),
        cost_estimate=NO_COST,
        name="packed",
    )(values, pieces)


def assemble_kernel(axis, count, length, *refs):
    *tile_refs, out_ref, pieces_ref = refs
    position = lax.axis_index(axis)
    tiles = [ref[...].astype(jnp.float32) for ref in tile_refs]
    bit = 1
    while bit < len(tiles):
        flip = (position & bit) != 0
        tiles = [jnp.where(flip, tiles[i ^ bit], tiles[i]) for i in range(len(tiles))]
        bit *= 2
    per = tiles[0].shape[0] // count
    for block, tile in enumerate(tiles):
        for row in range(count):
            for low in range(0, length, 128):
                line = row * per + low // 128 % per
                columns = low // 128 // per * 128
                size = min(128, length - low)
                pieces_ref[block * count + row : block * count + row + 1, low : low + size] = tile[
                    line : line + 1, columns : columns + size
                ]
    width = out_ref.shape[1]
    vectors = out_ref.shape[0]
    halves = len(tiles) * count * length // (vectors * width)
    for half in range(halves):

        @pl.when(lax.axis_index("tensor") == half)
        def _(half=half):
            for vector in range(vectors):
                at = (vector * halves + half) * width
                end = at + width
                parts = []
                while at < end:
                    row, low = divmod(at, length)
                    high = min(length, low + end - at)
                    parts.append(pieces_ref[row : row + 1, low:high])
                    at += high - low
                out_ref[vector : vector + 1, :] = jnp.concatenate(parts, axis=1)


def assembled(blocks, axis, count, length, width):
    rows, columns = blocks[0].shape
    extra = columns - width
    return pl.pallas_call(
        lambda *refs: assemble_kernel(axis, count, length, *refs),
        grid=(1,),
        in_specs=[pl.BlockSpec((rows, extra), lambda j: (0, width // extra)) for _ in blocks],
        out_specs=pl.BlockSpec((6, width), lambda j: (0, 0)),
        out_shape=jax.ShapeDtypeStruct((6, width), jnp.float32),
        scratch_shapes=[pltpu.VMEM((len(blocks) * count, -(-length // 128) * 128), jnp.float32)],
        compiler_params=pltpu.CompilerParams(vmem_limit_bytes=VMEM_BYTES),
        cost_estimate=NO_COST,
        name="assembled",
    )(*blocks)


def moments(values, shape):
    average = jnp.mean(values, axis=-1, keepdims=True)
    away = values - average
    lane = lax.broadcasted_iota(jnp.int32, shape, 1)
    return jnp.where(lane < shape[1] // 2, average, jnp.sum(away * away, axis=-1, keepdims=True))


def combined(own, arrived, features):
    middle = own.shape[1] // 2
    first, second = own[:, :1], arrived[:, :1]
    squares = own[:, middle:][:, :1] + arrived[:, middle:][:, :1]
    apart = first - second
    return (first + second) * 0.5, squares / features + apart * apart * 0.25


def row_sums_kernel(values_ref, out_ref, copy_ref):
    out_ref[...] = moments(values_ref[...].astype(jnp.float32), out_ref.shape)
    copy_ref[...] = values_ref[...]


def row_sums(values):
    return pl.pallas_call(
        row_sums_kernel,
        out_shape=[
            jax.ShapeDtypeStruct((values.shape[0], 128), jnp.float32),
            jax.ShapeDtypeStruct(values.shape, values.dtype),
        ],
        compiler_params=pltpu.CompilerParams(vmem_limit_bytes=VMEM_BYTES * 2),
        cost_estimate=NO_COST,
        name="row_sums",
    )(values)


def standardize_kernel(features, values_ref, own_ref, arrived_ref, *refs):
    average, variance = combined(own_ref[...], arrived_ref[...], features)
    values = values_ref[...].astype(jnp.float32)
    refs[-1][...] = ((values - average) * lax.rsqrt(variance + 1e-06)).astype(jnp.bfloat16)


def standardized(values, features, after):
    own, values = row_sums(values)
    whole = lambda array: pl.BlockSpec(array.shape, lambda j: (0, 0))
    return pl.pallas_call(
        lambda *refs: standardize_kernel(features, *refs),
        grid=(1,),
        in_specs=[whole(values), whole(own), whole(own)] + after_specs(after),
        out_specs=whole(values),
        out_shape=jax.ShapeDtypeStruct(values.shape, jnp.bfloat16),
        compiler_params=pltpu.CompilerParams(vmem_limit_bytes=VMEM_BYTES * 2),
        cost_estimate=NO_COST,
        name="standardized",
    )(values, own, permuted(own, "tensor", 1), *after)


def stack_kernel(*refs):
    *block_refs, out_ref = refs
    rows = block_refs[0].shape[0]
    for k, block_ref in enumerate(block_refs):
        out_ref[k * rows : (k + 1) * rows, :] = block_ref[...]


def stacked(blocks, cost):
    rows, width = blocks[0].shape
    return pl.pallas_call(
        stack_kernel,
        out_shape=jax.ShapeDtypeStruct((rows * len(blocks), width), blocks[0].dtype),
        compiler_params=pltpu.CompilerParams(vmem_limit_bytes=VMEM_BYTES * 2),
        cost_estimate=cost,
        name="stacked",
    )(*blocks)


def copied_kernel(values_ref, after_ref, out_ref):
    out_ref[...] = values_ref[...]


def copied(values, after, cost):
    whole = pl.BlockSpec(values.shape, lambda j: (0, 0))
    return pl.pallas_call(
        copied_kernel,
        grid=(1,),
        in_specs=[whole] + after_specs([after]),
        out_specs=whole,
        out_shape=jax.ShapeDtypeStruct(values.shape, values.dtype),
        compiler_params=pltpu.CompilerParams(vmem_limit_bytes=VMEM_BYTES * 2),
        cost_estimate=cost,
        name="copied",
    )(values, after)


def added(blocks):
    total = blocks[0].astype(jnp.float32)
    for block in blocks[1:]:
        total = total + block.astype(jnp.float32)
    return total


def project_kernel(count, parts, other, *refs):
    block_refs = refs[:count]
    shift_ref, scale_ref = refs[count : count + 2]
    weight_refs = refs[count + 2 : count + 2 + parts]
    normed_ref = refs[-1]
    rows = block_refs[0].shape[0]
    for k, block_ref in enumerate(block_refs):
        values = block_ref[...].astype(jnp.float32)
        values = values * (1.0 + scale_ref[...]) + shift_ref[...]
        normed_ref[k * rows : (k + 1) * rows, :] = values.astype(jnp.bfloat16)
    project_parts(normed_ref, weight_refs, refs[-1 - parts : -1], other)


def project_parts(normed_ref, weight_refs, out_refs, other):
    half = out_refs[0].shape[1]
    position = lax.axis_index("tensor")
    low = pl.multiple_of((1 - position if other else position) * half, 128)
    for weight_ref, out_ref in zip(weight_refs, out_refs):
        out_ref[...] = jnp.dot(
            normed_ref[...], weight_ref[:, pl.ds(low, half)], preferred_element_type=jnp.float32
        ).astype(jnp.bfloat16)


def project_again_kernel(parts, other, normed_ref, *refs):
    project_parts(normed_ref, refs[:parts], refs[-parts:], other)


def projected(blocks, small, weights, half, other, after=()):
    rows, width = blocks[0].shape[0], weights[0].shape[0]
    all_rows = rows * len(blocks)
    count = len(weights)
    whole = lambda shape: pl.BlockSpec(shape, lambda j: (0, 0))
    shapes = [(all_rows, half)] * count + [(all_rows, width)] * bool(small)
    return pl.pallas_call(
        (lambda *refs: project_kernel(len(blocks), count, other, *refs))
        if small
        else (lambda *refs: project_again_kernel(count, other, *refs)),
        grid=(1,),
        in_specs=[whole((rows, width)) for _ in blocks]
        + [whole(array.shape) for array in small]
        + [pl.BlockSpec(memory_space=pltpu.VMEM) for _ in weights]
        + after_specs(after),
        out_specs=[whole(shape) for shape in shapes],
        out_shape=[jax.ShapeDtypeStruct(shape, jnp.bfloat16) for shape in shapes],
        compiler_params=pltpu.CompilerParams(vmem_limit_bytes=VMEM_BYTES * 20),
        cost_estimate=NO_COST,
        name="projected",
    )(*blocks, *small, *weights, *after)


def staged(weights, after, part=None):
    width, columns = weights.shape[-2:]
    pieces = 4 if width % 64 == 0 else 1
    rows = width // pieces
    anywhere = pl.BlockSpec(memory_space=pl.ANY)

    def kernel(weight_ref, after_ref, out_ref, sems):
        source_ref = weight_ref if part is None else weight_ref.at[part]
        copies = [
            pltpu.make_async_copy(
                source_ref.at[pl.ds(k * rows, rows)], out_ref.at[pl.ds(k * rows, rows)], sems.at[k]
            )
            for k in range(pieces)
        ]
        for copy in copies:
            copy.start()
        for copy in copies:
            copy.wait()

    return pl.pallas_call(
        kernel,
        grid=(1,),
        in_specs=[anywhere] + after_specs([after]),
        out_specs=pl.BlockSpec(memory_space=pltpu.VMEM),
        out_shape=pltpu.VMEM((width, columns), weights.dtype),
        scratch_shapes=[pltpu.SemaphoreType.DMA((pieces,))],
        compiler_params=pltpu.CompilerParams(vmem_limit_bytes=VMEM_BYTES),
        cost_estimate=pl.CostEstimate(
            flops=0, bytes_accessed=2 * width * columns, transcendentals=0
        ),
        name="staged",
    )(weights, after)


def mark_kernel(*refs):
    refs[-1][...] = jnp.zeros(refs[-1].shape, jnp.float32)


def mark(after, cost):
    return pl.pallas_call(
        mark_kernel,
        grid=(1,),
        in_specs=after_specs(after),
        out_specs=pl.BlockSpec((8, 128), lambda j: (0, 0)),
        out_shape=jax.ShapeDtypeStruct((8, 128), jnp.float32),
        compiler_params=pltpu.CompilerParams(vmem_limit_bytes=VMEM_BYTES),
        cost_estimate=cost,
        name="mark",
    )(*after)


def head_normal(values, gain_ref):
    spread = jnp.mean(values * values, axis=-1, keepdims=True) + 1e-06
    return (values * lax.rsqrt(spread) * gain_ref[...]).astype(jnp.bfloat16)


def heads_kernel(count, head_size, *refs):
    own_refs, arrived_refs = refs[:count], refs[count : 2 * count]
    q_gain_ref, k_gain_ref = refs[2 * count : 2 * count + 2]
    out_refs = refs[-1:] if count == 2 else refs[-2:]
    half = own_refs[0].shape[1]

    def total(part, here):
        return own_refs[part][:, here].astype(jnp.float32) + arrived_refs[part][:, here].astype(
            jnp.float32
        )

    for low in range(0, half, head_size):
        here = slice(low, low + head_size)
        if count == 3:
            out_refs[1][:, here] = head_normal(total(0, here), q_gain_ref)
        out_refs[0][:, here] = head_normal(total(count - 2, here), k_gain_ref)
        out_refs[0][:, half + low : half + low + head_size] = total(count - 1, here).astype(
            jnp.bfloat16
        )


def split_heads(own, arrived, q_gain, k_gain, after=()):
    count = len(own)
    rows, half = own[0].shape
    head_size = q_gain.shape[0]
    widths = [2 * half] if count == 2 else [2 * half, half]
    whole = lambda *shape: pl.BlockSpec(shape, lambda j: (0, 0))
    return pl.pallas_call(
        lambda *refs: heads_kernel(count, head_size, *refs),
        grid=(1,),
        in_specs=[whole(rows, half)] * (2 * count)
        + [whole(1, head_size)] * 2
        + after_specs(after),
        out_specs=[whole(rows, width) for width in widths],
        out_shape=[jax.ShapeDtypeStruct((rows, width), jnp.bfloat16) for width in widths],
        compiler_params=pltpu.CompilerParams(vmem_limit_bytes=VMEM_BYTES * 5),
        cost_estimate=NO_COST,
        name="split_heads",
    )(*own, *arrived, q_gain[None, :], k_gain[None, :], *after)


def head_scores(query, key, head_size):
    product = lax.dot_general(
        query, key, (((1,), (1,)), ((), ())), preferred_element_type=jnp.float32
    )
    return product * (1.0 / math.sqrt(head_size))


def weighted(scores, values, top):
    total, summed = 0.0, 0.0
    for part, value in zip(scores, values):
        weights = jnp.exp(part - top)
        total = total + jnp.sum(weights, axis=-1, keepdims=True)
        summed = summed + jnp.dot(
            weights.astype(jnp.bfloat16), value, preferred_element_type=jnp.float32
        )
    return total, summed


def highest(scores, top=None):
    for part in scores:
        part_top = jnp.max(part, axis=-1, keepdims=True)
        top = part_top if top is None else jnp.maximum(top, part_top)
    return top


def attend_kernel(head_size, count, query_ref, *refs):
    kv_refs, (top_ref, total_ref, summed_ref) = refs[:count], refs[-3:]
    half = query_ref.shape[1]
    places = [slice(low, low + head_size) for low in range(0, half, head_size)]
    scores = [
        [head_scores(query_ref[:, here], ref[:, here], head_size) for ref in kv_refs]
        for here in places
    ]
    tops = [highest(parts) for parts in scores]
    for here, parts, top in zip(places, scores, tops):
        values = [ref[:, half + here.start : half + here.stop] for ref in kv_refs]
        total, summed = weighted(parts, values, top)
        top_ref[:, here] = jnp.broadcast_to(top, summed.shape)
        total_ref[:, here] = jnp.broadcast_to(total, summed.shape)
        summed_ref[:, here] = summed


def attend(queries, kv_parts, head_size, after):
    whole = lambda array: pl.BlockSpec(array.shape, lambda j: (0, 0))
    state = jax.ShapeDtypeStruct(queries.shape, jnp.float32)
    return pl.pallas_call(
        lambda *refs: attend_kernel(head_size, len(kv_parts), *refs),
        grid=(1,),
        in_specs=[whole(array) for array in [queries, *kv_parts]] + after_specs(after),
        out_specs=[whole(queries)] * 3,
        out_shape=[state] * 3,
        compiler_params=pltpu.CompilerParams(vmem_limit_bytes=VMEM_BYTES * 12),
        cost_estimate=NO_COST,
        name="attend",
    )(queries, *kv_parts, *after)


def finish_kernel(head_size, count, query_ref, top_ref, total_ref, summed_ref, *refs):
    kv_refs, out_ref = refs[:count], refs[-1]
    half = query_ref.shape[1]
    places = [slice(low, low + head_size) for low in range(0, half, head_size)]
    tops = [top_ref[:, here] for here in places]
    totals = [total_ref[:, here] for here in places]
    sums = [summed_ref[:, here] for here in places]
    if kv_refs:
        keys = [kv_refs[0][:, here] for here in places]
        values = [kv_refs[0][:, half + here.start : half + here.stop] for here in places]
        scores = [
            head_scores(query_ref[:, here], key, head_size) for here, key in zip(places, keys)
        ]
        new_tops = [jnp.maximum(top, highest([part])) for top, part in zip(tops, scores)]
        decays = [jnp.exp(top - new_top) for top, new_top in zip(tops, new_tops)]
        weights = [jnp.exp(part - new_top[:, :1]) for part, new_top in zip(scores, new_tops)]
        products = [
            jnp.dot(part.astype(jnp.bfloat16), value, preferred_element_type=jnp.float32)
            for part, value in zip(weights, values)
        ]
        totals = [
            total * decay + jnp.sum(part, axis=-1, keepdims=True)
            for total, decay, part in zip(totals, decays, weights)
        ]
        sums = [part * decay + more for part, decay, more in zip(sums, decays, products)]
    for here, total, part in zip(places, totals, sums):
        out_ref[:, here] = (part / total).astype(jnp.bfloat16)


def finished(queries, state, parts, head_size, first, count, after=()):
    whole = lambda array: pl.BlockSpec(array.shape, lambda j: (0, 0))
    some = pl.BlockSpec((count, queries.shape[1]), lambda j: (first // count, 0))
    return pl.pallas_call(
        lambda *refs: finish_kernel(head_size, len(parts), *refs),
        grid=(1,),
        in_specs=[some] * 4 + [whole(array) for array in parts] + after_specs(after),
        out_specs=pl.BlockSpec((count, queries.shape[1]), lambda j: (0, 0)),
        out_shape=jax.ShapeDtypeStruct((count, queries.shape[1]), jnp.bfloat16),
        compiler_params=pltpu.CompilerParams(vmem_limit_bytes=VMEM_BYTES * 12),
        cost_estimate=NO_COST,
        name="finished",
    )(queries, *state, *parts, *after)


def column_tiles(columns):
    size = columns // 3 if columns % 384 == 0 else columns
    return [slice(low, low + size) for low in range(0, columns, size)]


def out_kernel(count, own_ref, arrived_ref, weight_ref, *refs):
    out_refs = refs[-count:]
    half = own_ref.shape[1]
    position = lax.axis_index("tensor")
    rows = [pl.ds(pl.multiple_of(at * half, 16), half) for at in (position, 1 - position)]
    for here in column_tiles(weight_ref.shape[1]):
        total = jnp.dot(
            own_ref[...], weight_ref[rows[0], here], preferred_element_type=jnp.float32
        ) + jnp.dot(arrived_ref[...], weight_ref[rows[1], here], preferred_element_type=jnp.float32)
        row_blocks(total, here, out_refs)


def row_blocks(values, columns, out_refs):
    rows = out_refs[0].shape[0]
    for k, out_ref in enumerate(out_refs):
        out_ref[:, columns] = values[k * rows : (k + 1) * rows].astype(jnp.bfloat16)


def out_projected(own, arrived, weight, rows, after):
    all_rows, half = own.shape
    width = weight.shape[1]
    whole = pl.BlockSpec((all_rows, half), lambda j: (0, 0))
    return pl.pallas_call(
        lambda *refs: out_kernel(all_rows // rows, *refs),
        grid=(1,),
        in_specs=[whole, whole, pl.BlockSpec(memory_space=pltpu.VMEM)] + after_specs(after),
        out_specs=[pl.BlockSpec((rows, width), lambda j: (0, 0))] * (all_rows // rows),
        out_shape=[jax.ShapeDtypeStruct((rows, width), jnp.bfloat16)] * (all_rows // rows),
        compiler_params=pltpu.CompilerParams(vmem_limit_bytes=VMEM_BYTES * 8),
        cost_estimate=NO_COST,
        name="out_projected",
    )(own, arrived, weight, *after)


def up_kernel(first, count, *refs):
    block_refs, weight_ref, (out_ref, joined_ref) = refs[:count], refs[count], refs[-2:]
    rows = block_refs[0].shape[0]
    for k, block_ref in enumerate(block_refs):
        joined_ref[k * rows : (k + 1) * rows, :] = block_ref[...]
    for here in column_tiles(out_ref.shape[1]):
        out_ref[:, here] = jnp.dot(
            joined_ref[...],
            weight_ref[:, first + here.start : first + here.stop],
            preferred_element_type=jnp.float32,
        ).astype(jnp.bfloat16)


def up_projected(blocks, weight, part, parts, after=()):
    rows, width = blocks[0].shape
    all_rows = rows * len(blocks)
    columns = weight.shape[1] // parts
    return pl.pallas_call(
        lambda *refs: up_kernel(part * columns, len(blocks), *refs),
        grid=(1,),
        in_specs=[pl.BlockSpec((rows, width), lambda j: (0, 0)) for _ in blocks]
        + [pl.BlockSpec(memory_space=pltpu.VMEM)]
        + after_specs(after),
        out_specs=pl.BlockSpec((all_rows, columns), lambda j: (0, 0)),
        out_shape=jax.ShapeDtypeStruct((all_rows, columns), jnp.bfloat16),
        scratch_shapes=[pltpu.VMEM((all_rows, width), jnp.bfloat16)],
        compiler_params=pltpu.CompilerParams(vmem_limit_bytes=VMEM_BYTES * 8),
        cost_estimate=pl.CostEstimate(
            flops=2 * all_rows * width * columns, bytes_accessed=0, transcendentals=0
        ),
        name="up_projected",
    )(*blocks, weight, *after)


def down_kernel(first, count, more, own_ref, arrived_ref, weight_ref, *refs):
    *out_refs, activ_ref = refs
    depth = own_ref.shape[1]
    for here in column_tiles(depth):
        hidden = own_ref[:, here].astype(jnp.float32) + arrived_ref[:, here].astype(jnp.float32)
        activ_ref[:, here] = jax.nn.gelu(hidden, approximate=True).astype(jnp.bfloat16)
    for here in column_tiles(weight_ref.shape[1]):
        total = jnp.dot(
            activ_ref[...],
            weight_ref[first : first + depth, here],
            preferred_element_type=jnp.float32,
        )
        if more:
            total = total + out_refs[0][:, here]
        if count:
            row_blocks(total, here, out_refs[-count:])
        else:
            out_refs[0][:, here] = total


def down_projected(own, arrived, weight, first, before, count):
    all_rows, depth = own.shape
    width = weight.shape[1]
    whole = lambda *shape: pl.BlockSpec(shape, lambda j: (0, 0))
    shape, kind = (all_rows // max(count, 1), width), jnp.bfloat16 if count else jnp.float32
    return pl.pallas_call(
        lambda *refs: down_kernel(first, count, len(before), *refs),
        grid=(1,),
        in_specs=[whole(all_rows, depth)] * 2
        + [pl.BlockSpec(memory_space=pltpu.VMEM)]
        + [whole(all_rows, width)] * len(before),
        out_specs=[whole(*shape)] * max(count, 1),
        out_shape=[jax.ShapeDtypeStruct(shape, kind)] * max(count, 1),
        scratch_shapes=[pltpu.VMEM((all_rows, depth), jnp.bfloat16)],
        compiler_params=pltpu.CompilerParams(vmem_limit_bytes=VMEM_BYTES * 12),
        cost_estimate=NO_COST,
        name="down_projected",
    )(own, arrived, weight, *before)


def add_kernel(first_ref, second_ref, out_ref):
    total = first_ref[...].astype(jnp.float32) + second_ref[...].astype(jnp.float32)
    out_ref[...] = total.astype(jnp.bfloat16)


def rounded_sum(first, second):
    return pl.pallas_call(
        add_kernel,
        out_shape=jax.ShapeDtypeStruct(first.shape, first.dtype),
        compiler_params=pltpu.CompilerParams(vmem_limit_bytes=VMEM_BYTES * 2),
        cost_estimate=NO_COST,
        name="rounded_sum",
    )(first, second)


def row_groups(blocks, axis):
    groups = len(blocks) // lax.axis_size(axis)
    pieces = [blocks[k : k + groups] for k in range(0, len(blocks), groups)]
    if groups != 2 or len(pieces) != 4:
        return [to_all([piece[k] for piece in pieces], axis) for k in range(groups)]
    own, first, second, far = pieces
    low, high = permuted(far[0], axis, 1), permuted(far[1], axis, 2)
    first_low, second_high = permuted(first[0], axis, 1), permuted(second[1], axis, 2)
    second_low = permuted(rounded_sum(second[0], low), axis, 2)
    first_high = permuted(rounded_sum(first[1], high), axis, 1)
    return [[own[0], first_low, second_low], [own[1], first_high, second_high]]


def mix_kernel(counts, *refs):
    token_ref, gate_ref = refs[sum(counts)], refs[sum(counts) + 1]
    mixed_ref, sums_ref = refs[-2:]
    rows = refs[0].shape[0]
    at = 0
    for group, count in enumerate(counts):
        here = slice(group * rows, (group + 1) * rows)
        total = refs[at][...].astype(jnp.float32)
        for block_ref in refs[at + 1 : at + count]:
            total = total + block_ref[...].astype(jnp.float32)
        at += count
        mixed = token_ref[here, :].astype(jnp.float32) + gate_ref[...] * total
        mixed_ref[here, :] = mixed
        sums_ref[here, :] = moments(mixed, (rows, sums_ref.shape[1]))


def mixed_rows(groups, tokens, gate_row, after):
    rows, width = tokens.shape
    whole = lambda *shape: pl.BlockSpec(shape, lambda j: (0, 0))
    blocks = [block for group in groups for block in group]
    return pl.pallas_call(
        lambda *refs: mix_kernel([len(group) for group in groups], *refs),
        grid=(1,),
        in_specs=[whole(*block.shape) for block in blocks]
        + [whole(rows, width), whole(1, width)]
        + after_specs(after),
        out_specs=[whole(rows, width), whole(rows, 128)],
        out_shape=[
            jax.ShapeDtypeStruct((rows, width), jnp.float32),
            jax.ShapeDtypeStruct((rows, 128), jnp.float32),
        ],
        compiler_params=pltpu.CompilerParams(vmem_limit_bytes=VMEM_BYTES * 4),
        cost_estimate=NO_COST,
        name="mixed_rows",
    )(*blocks, tokens, gate_row, *after)


def norm_kernel(features, mixed_ref, own_ref, arrived_ref, shift_ref, scale_ref, out_ref):
    average, variance = combined(own_ref[...], arrived_ref[...], features)
    values = (mixed_ref[...] - average) * lax.rsqrt(variance + 1e-06)
    out_ref[...] = (values * (1.0 + scale_ref[...]) + shift_ref[...]).astype(jnp.bfloat16)


def normed_rows(mixed, sums, shift_row, scale_row, features):
    return pl.pallas_call(
        lambda *refs: norm_kernel(features, *refs),
        out_shape=jax.ShapeDtypeStruct(mixed.shape, jnp.bfloat16),
        compiler_params=pltpu.CompilerParams(vmem_limit_bytes=VMEM_BYTES * 2),
        cost_estimate=NO_COST,
        name="normed_rows",
    )(mixed, sums, permuted(sums, "tensor", 1), shift_row, scale_row)


def on_pair(
    tokens, cond, mod_weight, qkv_weight, q_gain, k_gain, out_weight, up_weight, down_weight
):
    stages = [
        (axis, 1 << bit)
        for axis in ("tensor", "blk")
        for bit in range(lax.axis_size(axis).bit_length() - 1)
    ]
    rows, width = tokens.shape
    features = width * lax.axis_size("tensor")
    head_size = q_gain.shape[0]
    half = qkv_weight.shape[2] // 2
    blocks_z = lax.axis_size("blk")

    activated = jax.nn.silu(cond.astype(jnp.float32)).astype(jnp.bfloat16)
    pieces = jnp.dot(activated[None, :], mod_weight, preferred_element_type=jnp.float32)
    weights = pltpu.with_memory_space_constraint(jnp.moveaxis(qkv_weight, 1, 0), pltpu.HBM)
    start = copied(tokens, pieces, NO_COST)
    remote = [permuted(start, "blk", k) for k in range(2, blocks_z, 2)]
    normal = standardized(tokens, features, [])
    parts = []
    for stage in stages:
        after = []
        if stage[0] == "blk":
            take = [1] if stage[1] == 1 else [2]
            parts += [staged(weights, pieces, part) for part in take]
            after = parts + (remote if stage[1] == 2 else [normal])
        pieces = doubled_once(pieces, *stage, after)
    own = packed(normal, pieces)
    parts = [staged(weights, own, 0)] + parts
    chunks = [from_all(own, "ulysses")]
    if remote:
        far = stacked(remote + [permuted(block, "blk", 1) for block in remote], NO_COST)
        far = standardized(far, features, [])
        chunks.append(from_all(far, "ulysses"))
    own_mod = assembled(chunks[0], "ulysses", *pieces.shape, width)
    row = lambda k: own_mod[k : k + 1]
    out_weight, up_weight, down_weight = [
        pltpu.with_memory_space_constraint(weight, pltpu.HBM)
        for weight in (out_weight, up_weight, down_weight)
    ]

    def project(blocks, use, after):
        *partial, normed = projected(blocks, [row(0), row(1)], use, half, True, after)
        arrived = [permuted(part, "tensor", 1) for part in partial]
        return projected([normed], [], use, half, False), arrived

    own, arrived = project(chunks[0], parts, [far] * bool(remote))
    own_kv, queries = split_heads(own, arrived, q_gain, k_gain)
    kv_parts = [own_kv]
    if blocks_z > 1:
        arrived = permuted(own_kv, "blk", 1)
        kv_parts.append(copied(arrived, arrived, LONG))
    out_weight = staged(out_weight, own_kv)
    up_weight = staged(up_weight, out_weight)
    last = []
    first_blocks, last_blocks = halves(chunks[-1])
    if remote:
        own, arrived = project(first_blocks, parts[1:], [own_kv])
        kv_parts += split_heads(own, arrived, q_gain, k_gain)
    state = attend(queries, kv_parts, head_size, [out_weight, up_weight])
    if remote and last_blocks:
        tie = mark([*chunks[-1][1:], state[0]], SHORT)
        own, arrived = project(last_blocks, parts[1:], [state[0], tie])
        last = split_heads(own, arrived, q_gain, k_gain)
    all_rows = queries.shape[0]
    last_rows = rows if all_rows > rows else 0
    partial, arrived = [], []
    if last_rows:
        context = finished(queries, state, last, head_size, all_rows - rows, rows)
        other = permuted(context, "tensor", 1)
        arrived.append((context, copied(other, other, LONG)))
    after = [own for own, _ in arrived]
    context = finished(queries, state, last, head_size, 0, all_rows - last_rows, after)
    other = permuted(context, "tensor", 1)
    arrived.append((context, other))
    for own, other in arrived:
        after = [] if own is context else [context]
        partial = list(out_projected(own, other, out_weight, rows // 2, after)) + partial
    summed = row_groups(partial, "ulysses")
    mixed, sums = mixed_rows(summed, tokens, row(2), [])
    normed_two = normed_rows(mixed, sums, row(3), row(4), features)
    blocks = from_all(normed_two, "ulysses")
    down_weight = staged(down_weight, normed_two)
    order = halves(list(range(len(blocks))))
    outs = {}
    for part, places in enumerate(order):
        if not places:
            continue
        here = [blocks[k] for k in places]
        here = [stacked(here, LONG)] if part else here
        pieces = 2
        after = [outs[order[0][0]]] if part else [down_weight]
        ups = [up_projected(here, up_weight, k, pieces, after) for k in range(pieces)]
        arrived = [permuted(piece, "tensor", 1) for piece in ups]
        before = []
        for k, (own, other) in enumerate(zip(ups, arrived)):
            count = len(places) if k == pieces - 1 else 0
            before = down_projected(own, other, down_weight, k * own.shape[1], before, count)
        outs.update(zip(places, before))
    feedforward = added(to_all([outs[k] for k in range(len(blocks))], "ulysses"))
    return mixed + own_mod[5] * feedforward


def halves(items):
    order = items[:1] + items[:0:-1]
    middle = (len(order) + 1) // 2
    return order[:middle], order[middle:]


def solution(mesh):
    sizes = [mesh.shape[axis] for axis in ("ulysses", "blk")]
    pairs = mesh.shape["tensor"] == 2 and all(size & (size - 1) == 0 for size in sizes)
    return jax.shard_map(
        on_pair if pairs else on_device,
        mesh=mesh,
        in_specs=(
            P(("ulysses", "blk"), "tensor"),
            P(),
            P(None, ("ulysses", "blk", "tensor")),
            P("tensor", None, "ulysses"),
            P(),
            P(),
            P("ulysses", "tensor"),
            P("tensor", "ulysses"),
            P("ulysses", "tensor"),
        ),
        out_specs=P(("ulysses", "blk"), "tensor"),
        check_vma=False,
    )
```
